256 devices in a mesh: query: 32 (over y, x, core), feat: 8 (over z).
Axes of the slice: x: 4, y: 4, z: 8, core: 2. Of those that a mesh axis runs over, the one named last changes fastest.
Arguments:
- scores: float32 [262144], P(('query', 'feat')), may hold values from -6 to 6
- labels: int32 [262144], P('query'), may hold values from 0 to 4
- leaves: int32 [262144], P(('query', 'feat')), may hold values from 0 to 1023
- bins: int32 [262144, 256], P(('query', 'feat')), may hold values from 0 to 255
- lengths: int32 [32, 32], P('query'), may hold values from 1 to 1024, 8192 in all within a row
- owner: int32 [256], replicated, may hold values from 0 to 255, each once
Outputs:
- lambdas: float32 [2, 262144], P(None, ('query', 'feat'))
- leaf_values: float32 [1024], replicated
- score_step: float32 [262144], P(('query', 'feat'))
- histograms: float32 [3, 65536], P(None, ('query', 'feat'))
The draws below stay inside these ranges and needn't reach their ends.
Inputs may be any that keep to these rules, and one draw needn't show every extreme that they name: `lengths`: each row sums to 8192. `owner`: a permutation; the p-th device of query+feat, in that order, holds the histograms of the features owner[j] for p <= j < (p + 1).
All inputs are finite; a program needn't handle non-finite values.
Results may differ from the reference program's by a relative error of at most 0.0003.
Values sent between devices are 32-bit elements; how exact they have to be, the bound alone decides.
A program may use at most 128 MiB of HBM per device.

```python
import math
import jax
import jax.numpy as jnp
import numpy as np
from jax import lax

FEATURES = 256
BINS = 256
LEAVES = 1024
MAX_LEN = 1024
TILE_ROWS = 512
DOCS_DEV = 1024
BLOCK_DOCS = 8192
QUERIES_BLOCK = 32
DOCS_ALL = 262144
WINDOW = 1536
LEAF_SPAN = 32
N_QUERY = 32


def grade_draw(key):
    return jax.random.randint(jax.random.fold_in(key, 101), (DOCS_ALL,), 0, 5, dtype=jnp.int32)


def draw_labels(key, part):
    return grade_draw(key).astype(jnp.int32)


def draw_leaves(key, part):
    grades = grade_draw(key)
    places = jnp.arange(DOCS_ALL, dtype=jnp.int32)
    jitter = jax.random.randint(jax.random.fold_in(key, 102), (DOCS_ALL,), 0, 16, dtype=jnp.int32)
    nearby = (places // BLOCK_DOCS * LEAF_SPAN + grades * 8 + jitter) % LEAVES
    anywhere = jax.random.randint(jax.random.fold_in(key, 103), (DOCS_ALL,), 0, LEAVES, dtype=jnp.int32)
    picked = jax.random.randint(jax.random.fold_in(key, 104), (DOCS_ALL,), 0, 10, dtype=jnp.int32) < 9
    chosen = jnp.where(picked, nearby, anywhere)
    chosen = chosen.at[0].set(0).at[DOCS_ALL - 1].set(LEAVES - 1)
    return chosen.astype(jnp.int32)


def plant(entries, rng, low, high):
    spot = [jax.random.randint(jax.random.fold_in(rng, axis), (), 0, length) for axis, length in enumerate(entries.shape)]
    widest = entries.shape.index(max(entries.shape))
    neighbour = spot[:widest] + [(spot[widest] + 1) % entries.shape[widest]] + spot[widest + 1:]
    return entries.at[tuple(spot)].set(low).at[tuple(neighbour)].set(high)


def level_of(rng, extent, cuts, smallest, top_value):
    def one(axis_at, shards_of):
        draws = jax.random.uniform(jax.random.fold_in(jax.random.fold_in(rng, 6), axis_at), (shards_of,), jnp.float32, smallest / len(cuts), top_value / len(cuts))
        return jnp.repeat(jnp.exp(draws), extent[axis_at] // shards_of).reshape((-1,) + (1,) * (len(extent) - axis_at - 1))

    loudness = one(*cuts[0])
    for cut in cuts[1:]:
        loudness = loudness * one(*cut)
    return loudness


def profile(count, total, bound, slope):
    loads = [(1 << 20) // math.isqrt(grade ** slope) + 1 for grade in range(2, count + 1)]
    spare, holding = total - bound - (count - 1), [1] * (count - 1)
    while spare > 0:
        movable = [i for i in range(count - 1) if holding[i] < bound]
        mass, budget = sum([loads[i] for i in movable]), spare
        for i in movable:
            more = min(bound - holding[i], max(1, budget * loads[i] // mass), spare)
            holding[i] = holding[i] + more
            spare = spare - more
    return np.array([bound] + holding)


def uneven(stream_key, amount, total, limit, slope):
    if amount == 2:
        one = jax.random.randint(stream_key, (), max(1, total - limit), min(limit, total - 1) + 1)
        return jnp.stack([one, total - one])
    sizes = jnp.asarray(profile(amount, total, limit, slope), jnp.int32)
    twos = (amount - 1) // 2
    donor, receiver = sizes[1:1 + 2 * twos:2], sizes[2:2 + 2 * twos:2]
    slack = jnp.minimum(donor - 1, limit - receiver)
    passed = jax.random.randint(jax.random.fold_in(stream_key, 1), (twos,), 0, 1 << 20) % (slack + 1)
    sizes = sizes.at[1:1 + 2 * twos:2].set(donor - passed).at[2:2 + 2 * twos:2].set(receiver + passed)
    return sizes[jax.random.permutation(jax.random.fold_in(stream_key, 2), amount)]


def gaussian(stream_key, dims, scale, reach, cuts=(), held_as=jnp.bfloat16):
    result = scale * jax.random.normal(stream_key, dims, jnp.float32)
    if cuts:
        result = result * level_of(stream_key, dims, cuts, -0.22, 0.18)
    return jnp.clip(result, -reach, reach).astype(held_as)


def setup_inputs(seed: int = 0) -> dict:
    streams_of = jax.random.split(jax.random.key(seed), 7)
    return {
        "scores": gaussian(streams_of[0], (DOCS_ALL,), 1.0, 6.0, ((0, 256),), jnp.float32),
        "labels": draw_labels(jax.random.fold_in(streams_of[6], 71), 0),
        "leaves": draw_leaves(jax.random.fold_in(streams_of[6], 71), 0),
        "bins": plant(jax.random.randint(streams_of[3], (DOCS_ALL, FEATURES), 0, BINS), jax.random.fold_in(streams_of[3], 1), 0, BINS - 1).astype(jnp.int32),
        "lengths": jax.vmap(lambda own: uneven(own, QUERIES_BLOCK, BLOCK_DOCS, MAX_LEN, 2))(jax.random.split(streams_of[4], N_QUERY)).reshape((N_QUERY, QUERIES_BLOCK)).astype(jnp.int32),
        "owner": jax.random.permutation(streams_of[5], FEATURES).astype(jnp.int32),
    }


lasso_penalty = 1.0
ridge_penalty = 1.0
shrinkage = 0.1


def query_of(lengths_row, count):
    bounds = jnp.cumsum(lengths_row)
    places = jnp.arange(count, dtype=jnp.int32)
    return jnp.searchsorted(bounds, places, side="right").astype(jnp.int32)


def place_in_query(sorted_ids):
    places = jnp.arange(sorted_ids.shape[0], dtype=jnp.int32)
    first = jnp.concatenate([jnp.ones((1,), dtype=jnp.bool_), sorted_ids[1:] != sorted_ids[:-1]])
    starts = lax.cummax(jnp.where(first, places, 0), axis=0)
    return places - starts


def query_stats(values, grades, query_ids, count):
    order = jnp.lexsort((-values, query_ids))
    ranked = place_in_query(query_ids[order])
    standing = jnp.zeros(values.shape, jnp.int32).at[order].set(ranked)
    discount = 1.0 / jnp.log2(2.0 + standing.astype(jnp.float32))
    ideal_order = jnp.lexsort((-grades, query_ids))
    ideal_ids = query_ids[ideal_order]
    ideal_place = place_in_query(ideal_ids)
    worth = jnp.exp2(grades[ideal_order].astype(jnp.float32)) - 1.0
    terms = worth / jnp.log2(2.0 + ideal_place.astype(jnp.float32))
    slots = jnp.where(ideal_ids >= 0, ideal_ids, count)
    ideal = jax.ops.segment_sum(terms, slots, num_segments=count + 1)
    usable = ideal > 0.5
    inverse = jnp.where(usable, 1.0 / jnp.where(usable, ideal, 1.0), 0.0)
    return discount, inverse[jnp.where(query_ids >= 0, query_ids, count)]


def pair_block(row_part, col_part, forward):
    row_score, row_grade, row_query, row_discount, row_inverse, row_place = row_part
    col_score, col_grade, col_query, col_discount, col_place = col_part
    keep = (row_query[:, None] == col_query[None, :]) & (row_query[:, None] >= 0)
    if forward:
        keep = keep & (col_place[None, :] > row_place[:, None])
    else:
        keep = keep & (col_place[None, :] != row_place[:, None])
    row_worth = jnp.exp2(row_grade.astype(jnp.float32))
    col_worth = jnp.exp2(col_grade.astype(jnp.float32))
    signs = jnp.sign(row_grade[:, None] - col_grade[None, :]).astype(jnp.float32)
    change = jnp.abs(row_worth[:, None] - col_worth[None, :]) * jnp.abs(row_discount[:, None] - col_discount[None, :]) * row_inverse[:, None]
    chance = jax.nn.sigmoid(-signs * (row_score[:, None] - col_score[None, :]))
    push = jnp.where(keep, change * chance, 0.0) * signs
    bend = jnp.where(keep, change * chance * (1.0 - chance), 0.0)
    return -jnp.sum(push, axis=1), jnp.sum(bend, axis=1), jnp.sum(push, axis=0), jnp.sum(bend, axis=0)


def add_into(total, piece, start):
    current = lax.dynamic_slice_in_dim(total, start, piece.shape[0])
    return lax.dynamic_update_slice_in_dim(total, current + piece, start, 0)


def leaf_newton(sums):
    total_grad = sums[0]
    total_curv = sums[1]
    return -jnp.sign(total_grad) * jnp.maximum(jnp.abs(total_grad) - lasso_penalty, 0.0) / (total_curv + ridge_penalty)


def histogram_of(gradient, curvature, bins, slot):
    cells = (slot[None, :] * BINS + bins).reshape(-1)
    weights = jnp.stack([gradient, curvature, jnp.ones_like(gradient)])
    spread = jnp.repeat(weights, FEATURES, axis=1)

    def one_stat(column):
        return jax.ops.segment_sum(column, cells, num_segments=FEATURES * BINS)

    return jax.vmap(one_stat)(spread)


def reference(scores, labels, leaves, bins, lengths, owner):
    def block_query(lengths_row):
        return query_of(lengths_row, BLOCK_DOCS)

    local_ids = jax.vmap(block_query)(lengths)
    query_ids = (local_ids + (jnp.arange(N_QUERY, dtype=jnp.int32) * QUERIES_BLOCK)[:, None]).reshape(-1)
    total_queries = N_QUERY * QUERIES_BLOCK
    discount, inverse = query_stats(scores, labels, query_ids, total_queries)
    padded = (jnp.pad(scores, (0, WINDOW)), jnp.pad(labels, (0, WINDOW)),
              jnp.pad(query_ids, (0, WINDOW), constant_values=-1), jnp.pad(discount, (0, WINDOW)),
              jnp.pad(inverse, (0, WINDOW)), jnp.arange(DOCS_ALL + WINDOW, dtype=jnp.int32))

    def visit(carry, tile_index):
        acc_grad, acc_curv = carry
        start = tile_index * TILE_ROWS
        row_part = tuple(lax.dynamic_slice_in_dim(item, start, TILE_ROWS) for item in padded)
        col_part = tuple(lax.dynamic_slice_in_dim(padded[which], start, WINDOW) for which in (0, 1, 2, 3, 5))
        row_grad, row_curv, col_grad, col_curv = pair_block(row_part, col_part, True)
        acc_grad = add_into(add_into(acc_grad, col_grad, start), row_grad, start)
        acc_curv = add_into(add_into(acc_curv, col_curv, start), row_curv, start)
        return (acc_grad, acc_curv), None

    empty = jnp.zeros((DOCS_ALL + WINDOW,), jnp.float32)
    (acc_grad, acc_curv), unused = lax.scan(visit, (empty, empty), jnp.arange(DOCS_ALL // TILE_ROWS, dtype=jnp.int32))
    gradient = acc_grad[:DOCS_ALL]
    curvature = acc_curv[:DOCS_ALL]
    lambdas = jnp.stack([gradient, curvature])
    leaf_sums = jnp.stack([jax.ops.segment_sum(gradient, leaves, num_segments=LEAVES),
                           jax.ops.segment_sum(curvature, leaves, num_segments=LEAVES)])
    leaf_values = leaf_newton(leaf_sums)
    score_step = shrinkage * leaf_values[leaves]
    slot = jnp.zeros((FEATURES,), jnp.int32).at[owner].set(jnp.arange(FEATURES, dtype=jnp.int32))

    def add_block(hist, block_index):
        start = block_index * DOCS_DEV
        block_bins = lax.dynamic_slice_in_dim(bins, start, DOCS_DEV, 0)
        part_grad = lax.dynamic_slice_in_dim(gradient, start, DOCS_DEV)
        part_curv = lax.dynamic_slice_in_dim(curvature, start, DOCS_DEV)
        return hist + histogram_of(part_grad, part_curv, block_bins, slot), None

    histograms, unused = lax.scan(add_block, jnp.zeros((3, FEATURES * BINS), jnp.float32),
                                  jnp.arange(DOCS_ALL // DOCS_DEV, dtype=jnp.int32))
    return lambdas, leaf_values, score_step, histograms
```

```python
import jax
import jax.numpy as jnp
from jax import lax
from jax.experimental import pallas as pl
from jax.experimental.pallas import tpu as pltpu
from jax.sharding import PartitionSpec as P

BINS = 256
LEAVES = 1024
FEATURES = 256
OWN = 1024
WIN = 3 * OWN
BLOCK = 8192
QUERIES = 32
TILE = 128
TILES = WIN // TILE
OWN_TILES = OWN // TILE
STEP = 64
PEERS = 32
RING = 8
GROUP = 8
HI = 8
LO = 32

lasso_penalty = 1.0
ridge_penalty = 1.0
shrinkage = 0.1

F32 = jnp.float32
BF16 = jnp.bfloat16
MESH_ID = pl.DeviceIdType.MESH
VMEM = pl.BlockSpec(memory_space=pltpu.VMEM)
SMEM = pl.BlockSpec(memory_space=pltpu.SMEM)


def nt_dot(left, right):
    return lax.dot_general(left, right, (((1,), (1,)), ((), ())), preferred_element_type=F32)


def iota(shape, axis):
    return lax.broadcasted_iota(jnp.int32, shape, axis)


def prepare_kernel(
    scores, labels, lengths, owner, bins, rows, table, bins_t, from_left, from_right, send_sem, recv_sem
):
    feat = lax.axis_index("feat")
    query = lax.axis_index("query")
    left = lax.rem(feat + RING - 1, RING)
    right = lax.rem(feat + 1, RING)

    barrier = pltpu.get_barrier_semaphore()
    for peer in (left, right):
        pl.semaphore_signal(barrier, inc=1, device_id=(query, peer), device_id_type=MESH_ID)
    pl.semaphore_wait(barrier, 2)
    to_right = pltpu.make_async_remote_copy(
        src_ref=scores, dst_ref=from_left, send_sem=send_sem.at[0], recv_sem=recv_sem.at[0],
        device_id=(query, right), device_id_type=MESH_ID)
    to_left = pltpu.make_async_remote_copy(
        src_ref=scores, dst_ref=from_right, send_sem=send_sem.at[1], recv_sem=recv_sem.at[1],
        device_id=(query, left), device_id_type=MESH_ID)
    to_right.start()
    to_left.start()

    pick_t = (iota((FEATURES, FEATURES), 0) == owner[...]).astype(F32)
    pick = pick_t.T.astype(BF16)
    bins_t[...] = nt_dot(pick, bins[...].astype(F32).astype(BF16))

    base = (feat * OWN - OWN).astype(F32)
    length_row = jnp.broadcast_to(lengths[...].astype(F32), (QUERIES, QUERIES))
    other, one = iota((QUERIES, QUERIES), 1), iota((QUERIES, QUERIES), 0)
    starts = jnp.sum(jnp.where(other < one, length_row, 0.0), axis=1, keepdims=True)
    ends = jnp.sum(jnp.where(other <= one, length_row, 0.0), axis=1, keepdims=True)
    place = iota((1, WIN), 1).astype(F32) + base
    inside = (place >= starts) & (place < ends)
    passed = jnp.sum(jnp.where(place >= ends, 1.0, 0.0), axis=0, keepdims=True)
    ids = jnp.where(place < 0.0, -1.0, passed)

    def label_part(block):
        return labels[:, pl.ds(pl.multiple_of(block * OWN, OWN), OWN)]

    grades = jnp.concatenate([label_part(left), label_part(feat), label_part(right)], axis=1)
    worth = lax.shift_left(jnp.ones_like(grades), grades).astype(F32)

    at_least = (jnp.broadcast_to(grades, (8, WIN)) > iota((8, WIN), 0)).astype(F32).astype(BF16)
    counts = nt_dot(inside.astype(F32).astype(BF16), at_least)
    spot = iota((1, OWN), 1).astype(F32)
    gain = 1.0 / jnp.log2(2.0 + spot)
    parts = jnp.zeros((QUERIES, OWN), F32)
    for level in range(4):
        parts = parts + jnp.where(spot < counts[:, level:level + 1], gain * float(2 ** level), 0.0)
    ideal = jnp.sum(parts, axis=1, keepdims=True)
    usable = ideal > 0.5
    inverse = jnp.where(usable, 1.0 / jnp.where(usable, ideal, 1.0), 0.0)
    own_inverse = jnp.sum(jnp.where(inside, inverse, 0.0), axis=0, keepdims=True)

    def bound_at(spots, values):
        hit = (spots >= starts) & (spots < ends)
        return jnp.sum(jnp.where(hit, values, 0.0), axis=0, keepdims=True)

    zeros = jnp.zeros((1, TILE), F32)
    first = bound_at(zeros + (base + OWN), starts)
    last = bound_at(zeros + (base + 2 * OWN - 1.0), ends)
    tile_first = base + iota((1, TILE), 1).astype(F32) * TILE
    low = bound_at(jnp.maximum(tile_first, first), starts)
    high = bound_at(jnp.minimum(tile_first + (TILE - 1.0), last - 1.0), ends)
    line = iota((8, TILE), 0)
    bounds = jnp.where(line == 0, low, jnp.where(line == 1, high, jnp.where(line == 2, first, last)))
    table[...] = (bounds - base).astype(jnp.int32)

    rows[1:2, :] = ids
    rows[2:3, :] = worth
    rows[3:4, :] = own_inverse
    rows[4:8, :] = jnp.zeros((4, WIN), F32)
    to_right.wait()
    to_left.wait()
    rows[0:1, 0:OWN] = from_left[...]
    rows[0:1, OWN:2 * OWN] = scores[...]
    rows[0:1, 2 * OWN:WIN] = from_right[...]


def pair_kernel(table, rows, out, score_col, id_col, worth_col, up_col, discount_col, discount_row):
    def spread(column):
        return jnp.broadcast_to(column, (TILE, TILE))

    for tile in range(TILES):
        at = slice(tile * TILE, (tile + 1) * TILE)
        flipped = rows[:, at].T
        score_col[at, :] = spread(flipped[:, 0:1])
        id_col[at, :] = spread(flipped[:, 1:2])
        worth_col[at, :] = spread(flipped[:, 2:3])
        up_col[at, :] = spread(jnp.exp(-flipped[:, 0:1]))
    discount_row[...] = jnp.zeros_like(discount_row)

    active = table[2, 0] // TILE
    stop = (table[3, 0] + TILE - 1) // TILE

    def rank_tile(tile, carry):
        begin = pl.multiple_of(tile * TILE, TILE)
        score = jnp.broadcast_to(rows[0:1, pl.ds(begin, TILE)], (8, TILE))
        ident = jnp.broadcast_to(rows[1:2, pl.ds(begin, TILE)], (8, TILE))

        def count(start, steps, ahead, total):
            for sub in range(steps):
                spot = pl.multiple_of(start + sub * 8, 8)
                other = score_col[pl.ds(spot, 8), :]
                same = id_col[pl.ds(spot, 8), :] == ident
                if ahead is None:
                    earlier = iota((8, TILE), 0) + sub * 8 < iota((8, TILE), 1)
                    beats = (other > score) | ((other == score) & earlier)
                elif ahead:
                    beats = other >= score
                else:
                    beats = other > score
                total = total + jnp.where(same & beats, 1.0, 0.0)
            return total

        total = count(begin, TILE // 8, None, jnp.zeros((8, TILE), F32))
        total = lax.fori_loop(
            table[0, tile] // STEP, begin // STEP,
            lambda i, t: count(i * STEP, STEP // 8, True, t), total)
        total = lax.fori_loop(
            (begin + TILE) // STEP, (table[1, tile] + STEP - 1) // STEP,
            lambda i, t: count(i * STEP, STEP // 8, False, t), total)
        rank = jnp.sum(total, axis=0, keepdims=True)
        discount_row[0:1, pl.ds(begin, TILE)] = 1.0 / jnp.log2(2.0 + rank)
        return carry

    lax.fori_loop(active, stop, rank_tile, 0)

    for tile in range(TILES):
        at = slice(tile * TILE, (tile + 1) * TILE)
        flipped = discount_row[:, at].T
        discount_col[at, :] = spread(flipped[:, 0:1])

    def own_tile(index, carry):
        tile = index + OWN_TILES
        begin = pl.multiple_of(tile * TILE, TILE)

        def own(ref, line):
            return jnp.broadcast_to(ref[line:line + 1, pl.ds(begin, TILE)], (8, TILE))

        up = jnp.exp(own(rows, 0))
        ident = own(rows, 1)
        worth = own(rows, 2)
        discount = own(discount_row, 0)

        def meet(block, sums):
            grad, curv = sums
            for sub in range(STEP // 8):
                at = pl.ds(pl.multiple_of(block * STEP + sub * 8, 8), 8)
                odds = up * up_col[at, :]
                win = pltpu.reciprocal(1.0 + odds, approx=True)
                lose = odds * win
                gap = jnp.where(id_col[at, :] == ident, jnp.abs(discount - discount_col[at, :]), 0.0)
                rise = worth - worth_col[at, :]
                change = rise * gap
                grad = grad + change * jnp.where(rise > 0.0, win, lose)
                curv = curv + jnp.abs(change) * (win * lose)
            return grad, curv

        empty = jnp.zeros((8, TILE), F32)
        grad, curv = lax.fori_loop(
            table[0, tile] // STEP, (table[1, tile] + STEP - 1) // STEP, meet, (empty, empty))
        inverse = rows[3:4, pl.ds(begin, TILE)]
        spot = pl.ds(pl.multiple_of(index * TILE, TILE), TILE)
        out[0:1, spot] = -inverse * jnp.sum(grad, axis=0, keepdims=True)
        out[1:2, spot] = inverse * jnp.sum(curv, axis=0, keepdims=True)
        return carry

    lax.fori_loop(0, OWN_TILES, own_tile, 0)


def in_pieces(value, pieces):
    found = []
    for unused in range(pieces):
        piece = value.astype(BF16)
        found.append(piece)
        value = value - piece.astype(F32)
    return found


def histogram_kernel(
    lambdas, leaves, bins_t, leaf_out, step_out, hist_out,
    left_side, right_side, weights, sent, got, leaf_got, leaf_ring, chunk, chunk_got,
    send_sem, recv_sem, leaf_send, leaf_recv, ring_send, ring_recv, chunk_send, chunk_recv
):
    query = lax.axis_index("query")
    feat = lax.axis_index("feat")

    def plane_peer(offset):
        return lax.rem(query + offset, PEERS)

    def ring_peer(offset):
        return lax.rem(feat + offset, RING)

    barrier = pltpu.get_barrier_semaphore()

    @pl.loop(1, PEERS)
    def _(offset):
        pl.semaphore_signal(barrier, inc=1, device_id=(plane_peer(offset), feat), device_id_type=MESH_ID)

    @pl.loop(1, RING)
    def _(offset):
        pl.semaphore_signal(barrier, inc=1, device_id=(query, ring_peer(offset)), device_id_type=MESH_ID)

    grad, curv = lambdas[0:1, :], lambdas[1:2, :]
    leaf = leaves[...]
    leaf_row = lax.shift_right_logical(leaf, 7)
    leaf_lane = jnp.bitwise_and(leaf, 127)
    in_row = iota((8, OWN), 0) == leaf_row
    lane_hot = (iota((TILE, OWN), 0) == leaf_lane).astype(F32).astype(BF16)
    spread = []
    for value in (grad, curv):
        for piece in in_pieces(value, 3):
            spread.append(jnp.where(in_row, piece.astype(F32), 0.0).astype(BF16))
    leaf_sums = nt_dot(jnp.concatenate(spread, axis=0), lane_hot)
    leaf_got[query, 0:8, :] = leaf_sums[0:8] + leaf_sums[8:16] + leaf_sums[16:24]
    leaf_got[query, 8:16, :] = leaf_sums[24:32] + leaf_sums[32:40] + leaf_sums[40:48]

    grad_parts, curv_parts = in_pieces(grad, 2), in_pieces(curv, 2)
    stats = grad_parts + curv_parts + [jnp.ones((1, OWN), BF16)]
    for which, value in enumerate(stats):
        weights[which] = jnp.broadcast_to(value, (16, OWN))

    pl.semaphore_wait(barrier, PEERS - 1 + RING - 1)

    def leaf_copy(offset):
        return pltpu.make_async_remote_copy(
            src_ref=leaf_got.at[query], dst_ref=leaf_got.at[query],
            send_sem=leaf_send.at[offset], recv_sem=leaf_recv.at[query],
            device_id=(plane_peer(offset), feat), device_id_type=MESH_ID)

    def leaf_arrival(peer):
        return pltpu.make_async_remote_copy(
            src_ref=leaf_got.at[query], dst_ref=leaf_got.at[peer],
            send_sem=leaf_send.at[0], recv_sem=leaf_recv.at[peer],
            device_id=(peer, feat), device_id_type=MESH_ID)

    @pl.loop(1, PEERS)
    def _(offset):
        leaf_copy(offset).start()

    low_levels = iota((LO, OWN), 0).astype(F32).astype(BF16)
    high_levels = jnp.bitwise_and(iota((16, OWN), 0), 7).astype(F32).astype(BF16)
    upper = iota((16, OWN), 0) < 8
    zero = jnp.zeros((), BF16)
    unit = jnp.ones((), BF16)

    def hist_copy(offset):
        peer = plane_peer(offset)
        return pltpu.make_async_remote_copy(
            src_ref=sent.at[peer], dst_ref=got.at[query],
            send_sem=send_sem.at[offset], recv_sem=recv_sem.at[query],
            device_id=(peer, feat), device_id_type=MESH_ID)

    def hist_arrival(peer):
        return pltpu.make_async_remote_copy(
            src_ref=sent.at[peer], dst_ref=got.at[peer],
            send_sem=send_sem.at[0], recv_sem=recv_sem.at[peer],
            device_id=(peer, feat), device_id_type=MESH_ID)

    def one_group(group):
        block = bins_t[pl.ds(pl.multiple_of(group * GROUP, GROUP), GROUP), :]
        high = jnp.floor(block * (1.0 / LO))
        low = block - high * LO
        for k in range(GROUP):
            spread_low = jnp.broadcast_to(low[k:k + 1].astype(BF16), (LO, OWN))
            right_side[k * LO:(k + 1) * LO, :] = jnp.where(spread_low == low_levels, unit, zero)
        for pair in range(GROUP // 2):
            k = 2 * pair
            both = jnp.where(
                upper, jnp.broadcast_to(high[k:k + 1], (16, OWN)),
                jnp.broadcast_to(high[k + 1:k + 2], (16, OWN))).astype(BF16)
            hot = both == high_levels
            for which in range(5):
                left_side[which * 64 + pair * 16:which * 64 + (pair + 1) * 16, :] = jnp.where(
                    hot, weights[which], zero)
        full = nt_dot(left_side[...], right_side[...])
        lane = iota((HI, TILE), 1)
        for stat, whichs in enumerate(((0, 1), (2, 3), (4,))):
            for half in range(2):
                lanes = slice(half * TILE, (half + 1) * TILE)
                total = None
                for which in whichs:
                    picked = None
                    for j in range(4):
                        k = half * 4 + j
                        piece = full[which * 64 + k * HI:which * 64 + (k + 1) * HI, lanes]
                        picked = piece if j == 0 else jnp.where(lane >= j * LO, piece, picked)
                    total = picked if total is None else total + picked
                sent[group, stat * HI:(stat + 1) * HI, lanes] = total

    @pl.loop(1, PEERS // 2)
    def _(offset):
        one_group(plane_peer(offset))
        hist_copy(offset).start()

    @pl.loop(1, PEERS)
    def _(offset):
        leaf_arrival(plane_peer(offset)).wait_recv()

    def add_leaf(peer, total):
        return total + leaf_got[peer]

    leaf_ring[feat] = lax.fori_loop(0, PEERS, add_leaf, jnp.zeros((16, TILE), F32))

    def ring_copy(offset):
        return pltpu.make_async_remote_copy(
            src_ref=leaf_ring.at[feat], dst_ref=leaf_ring.at[feat],
            send_sem=ring_send.at[offset], recv_sem=ring_recv.at[feat],
            device_id=(query, ring_peer(offset)), device_id_type=MESH_ID)

    def ring_arrival(peer):
        return pltpu.make_async_remote_copy(
            src_ref=leaf_ring.at[feat], dst_ref=leaf_ring.at[peer],
            send_sem=ring_send.at[0], recv_sem=ring_recv.at[peer],
            device_id=(query, peer), device_id_type=MESH_ID)

    @pl.loop(1, RING)
    def _(offset):
        ring_copy(offset).start()

    @pl.loop(PEERS // 2, PEERS)
    def _(offset):
        one_group(plane_peer(offset))
        hist_copy(offset).start()

    one_group(query)

    @pl.loop(1, RING)
    def _(offset):
        ring_arrival(ring_peer(offset)).wait_recv()

    totals = leaf_ring[0]
    for peer in range(1, RING):
        totals = totals + leaf_ring[peer]
    total_grad, total_curv = totals[0:8], totals[8:16]
    shrunk = jnp.maximum(jnp.abs(total_grad) - lasso_penalty, 0.0) / (total_curv + ridge_penalty)
    values = jnp.where(total_grad > 0.0, -shrunk, shrunk)
    leaf_out[...] = values
    found = jnp.zeros((8, OWN), F32)
    for piece in in_pieces(values, 3):
        found = found + jnp.dot(piece, lane_hot, preferred_element_type=F32)
    step_out[...] = shrinkage * jnp.sum(jnp.where(in_row, found, 0.0), axis=0, keepdims=True)

    def add_hist(offset, total):
        peer = plane_peer(offset)
        hist_arrival(peer).wait_recv()
        return total + got[peer]

    summed = lax.fori_loop(1, PEERS, add_hist, sent[query])

    lane_block = lax.shift_right_logical(iota((GROUP, TILE), 1), 5)
    holder = iota((GROUP, TILE), 0)
    for stat in range(3):
        for half in range(2):
            moved = jnp.zeros((GROUP, TILE), F32)
            for r in range(4):
                row = stat * HI + half * 4 + r
                line = jnp.where(
                    holder < 4, jnp.broadcast_to(summed[row:row + 1, 0:TILE], (GROUP, TILE)),
                    jnp.broadcast_to(summed[row:row + 1, TILE:2 * TILE], (GROUP, TILE)))
                for kk in range(4):
                    shift = (r - kk) % 4 * LO
                    turned = pltpu.roll(line, shift, 1) if shift else line
                    moved = jnp.where((jnp.bitwise_and(holder, 3) == kk) & (lane_block == r), turned, moved)
            for k in range(GROUP):
                chunk[k, stat:stat + 1, half * TILE:(half + 1) * TILE] = moved[k:k + 1, :]
    for k in range(GROUP):
        chunk[k, 3:8, :] = jnp.zeros((5, BINS), F32)

    def chunk_copy(offset):
        peer = ring_peer(offset)
        return pltpu.make_async_remote_copy(
            src_ref=chunk.at[peer], dst_ref=chunk_got.at[feat],
            send_sem=chunk_send.at[offset], recv_sem=chunk_recv.at[feat],
            device_id=(query, peer), device_id_type=MESH_ID)

    def chunk_arrival(peer):
        return pltpu.make_async_remote_copy(
            src_ref=chunk.at[peer], dst_ref=chunk_got.at[peer],
            send_sem=chunk_send.at[0], recv_sem=chunk_recv.at[peer],
            device_id=(query, peer), device_id_type=MESH_ID)

    @pl.loop(1, RING)
    def _(offset):
        chunk_copy(offset).start()

    def add_chunk(offset, total):
        peer = ring_peer(offset)
        chunk_arrival(peer).wait_recv()
        return total + chunk_got[peer]

    final = lax.fori_loop(1, RING, add_chunk, chunk[feat])
    hist_out[...] = final[0:3]

    @pl.loop(1, PEERS)
    def _(offset):
        leaf_copy(offset).wait_send()
        hist_copy(offset).wait_send()

    @pl.loop(1, RING)
    def _(offset):
        ring_copy(offset).wait_send()
        chunk_copy(offset).wait_send()


def local(scores, labels, leaves, bins, lengths, owner):
    shape = jax.ShapeDtypeStruct
    dma = pltpu.SemaphoreType.DMA
    rows, table, bins_t = pl.pallas_call(
        prepare_kernel,
        out_shape=(
            shape((8, WIN), F32),
            shape((8, TILE), jnp.int32),
            shape((FEATURES, OWN), F32),
        ),
        in_specs=[VMEM] * 5,
        out_specs=(VMEM, VMEM, VMEM),
        scratch_shapes=[pltpu.VMEM((1, OWN), F32), pltpu.VMEM((1, OWN), F32), dma((2,)), dma((2,))],
        compiler_params=pltpu.CompilerParams(
            collective_id=1, has_side_effects=True, vmem_limit_bytes=32 * 2**20),
        name="prepare",
    )(scores.reshape(1, OWN), labels.reshape(1, BLOCK), lengths, owner.reshape(1, FEATURES), bins)
    column = pltpu.VMEM((WIN, TILE), F32)
    lambdas = pl.pallas_call(
        pair_kernel,
        out_shape=shape((2, OWN), F32),
        in_specs=[SMEM, VMEM],
        out_specs=VMEM,
        scratch_shapes=[column] * 5 + [pltpu.VMEM((8, WIN), F32)],
        compiler_params=pltpu.CompilerParams(vmem_limit_bytes=32 * 2**20),
        name="pairs",
    )(table, rows)
    leaf_values, score_step, histograms = pl.pallas_call(
        histogram_kernel,
        out_shape=(
            shape((8, TILE), F32),
            shape((1, OWN), F32),
            shape((3, BINS), F32),
        ),
        in_specs=[VMEM] * 3,
        out_specs=(VMEM, VMEM, VMEM),
        scratch_shapes=[
            pltpu.VMEM((5 * GROUP * HI, OWN), BF16),
            pltpu.VMEM((GROUP * LO, OWN), BF16),
            pltpu.VMEM((5, 16, OWN), BF16),
            pltpu.VMEM((PEERS, 3 * HI, GROUP * LO), F32),
            pltpu.VMEM((PEERS, 3 * HI, GROUP * LO), F32),
            pltpu.VMEM((PEERS, 16, TILE), F32),
            pltpu.VMEM((RING, 16, TILE), F32),
            pltpu.VMEM((RING, 8, BINS), F32),
            pltpu.VMEM((RING, 8, BINS), F32),
            dma((PEERS,)), dma((PEERS,)), dma((PEERS,)), dma((PEERS,)),
            dma((RING,)), dma((RING,)), dma((RING,)), dma((RING,)),
        ],
        compiler_params=pltpu.CompilerParams(
            collective_id=2, has_side_effects=True, vmem_limit_bytes=32 * 2**20),
        name="histograms",
    )(lambdas, leaves.reshape(1, OWN), bins_t)
    return lambdas, leaf_values.reshape(LEAVES), score_step.reshape(OWN), histograms


def solution(mesh):
    in_specs = (
        P(("query", "feat")),
        P("query"),
        P(("query", "feat")),
        P(("query", "feat"), None),
        P("query", None),
        P(),
    )
    out_specs = (P(None, ("query", "feat")), P(), P(("query", "feat")), P(None, ("query", "feat")))
    return jax.shard_map(local, mesh=mesh, in_specs=in_specs, out_specs=out_specs, check_vma=False)
```

```python
import jax
import jax.numpy as jnp
from jax import lax
from jax.experimental import pallas as pl
from jax.experimental.pallas import tpu as pltpu
from jax.sharding import PartitionSpec as P

BINS = 256
LEAVES = 1024
FEATURES = 256
OWN = 1024
WIN = 3 * OWN
BLOCK = 8192
QUERIES = 32
TILE = 128
TILES = WIN // TILE
OWN_TILES = OWN // TILE
STEP = 64
PAIR = 2 * TILE
CHIPS = 16
SIDE = 4
RING = 8
GROUP = 8
EARLY = 5
HI = 8
LO = 32

lasso_penalty = 1.0
ridge_penalty = 1.0
shrinkage = 0.1

F32 = jnp.float32
BF16 = jnp.bfloat16
MESH_ID = pl.DeviceIdType.MESH
VMEM = pl.BlockSpec(memory_space=pltpu.VMEM)
HBM = pl.BlockSpec(memory_space=pltpu.HBM)
SMEM = pl.BlockSpec(memory_space=pltpu.SMEM)


def nt_dot(left, right):
    return lax.dot_general(left, right, (((1,), (1,)), ((), ())), preferred_element_type=F32)


def iota(shape, axis):
    return lax.broadcasted_iota(jnp.int32, shape, axis)


def prepare_kernel(labels, lengths, owner, bins, rows, table, bins_t, id_col, worth_col):
    feat = lax.axis_index("feat")
    left = lax.rem(feat + RING - 1, RING)
    right = lax.rem(feat + 1, RING)

    pick_t = (iota((FEATURES, FEATURES), 0) == owner[...]).astype(F32)
    pick = pick_t.T.astype(BF16)
    bins_t[...] = nt_dot(pick, bins[...].astype(F32).astype(BF16))

    base = (feat * OWN - OWN).astype(F32)
    length_row = jnp.broadcast_to(lengths[...].astype(F32), (QUERIES, QUERIES))
    other, one = iota((QUERIES, QUERIES), 1), iota((QUERIES, QUERIES), 0)
    starts = jnp.sum(jnp.where(other < one, length_row, 0.0), axis=1, keepdims=True)
    ends = jnp.sum(jnp.where(other <= one, length_row, 0.0), axis=1, keepdims=True)
    place = iota((1, WIN), 1).astype(F32) + base
    inside = (place >= starts) & (place < ends)
    passed = jnp.sum(jnp.where(place >= ends, 1.0, 0.0), axis=0, keepdims=True)
    ids = jnp.where(place < 0.0, -1.0, passed)

    def label_part(block):
        return labels[:, pl.ds(pl.multiple_of(block * OWN, OWN), OWN)]

    grades = jnp.concatenate([label_part(left), label_part(feat), label_part(right)], axis=1)
    worth = lax.shift_left(jnp.ones_like(grades), grades).astype(F32)

    at_least = (jnp.broadcast_to(grades, (8, WIN)) > iota((8, WIN), 0)).astype(F32).astype(BF16)
    counts = nt_dot(inside.astype(F32).astype(BF16), at_least)
    spot = iota((1, OWN), 1).astype(F32)
    gain = 1.0 / jnp.log2(2.0 + spot)
    parts = jnp.zeros((QUERIES, OWN), F32)
    for level in range(4):
        parts = parts + jnp.where(spot < counts[:, level:level + 1], gain * float(2 ** level), 0.0)
    ideal = jnp.sum(parts, axis=1, keepdims=True)
    usable = ideal > 0.5
    inverse = jnp.where(usable, 1.0 / jnp.where(usable, ideal, 1.0), 0.0)
    own_inverse = jnp.sum(jnp.where(inside, inverse, 0.0), axis=0, keepdims=True)

    def bound_at(spots, values):
        hit = (spots >= starts) & (spots < ends)
        return jnp.sum(jnp.where(hit, values, 0.0), axis=0, keepdims=True)

    zeros = jnp.zeros((1, TILE), F32)
    first = bound_at(zeros + (base + OWN), starts)
    last = bound_at(zeros + (base + 2 * OWN - 1.0), ends)
    tile_first = base + iota((1, TILE), 1).astype(F32) * TILE
    low = bound_at(jnp.maximum(tile_first, first), starts)
    high = bound_at(jnp.minimum(tile_first + (TILE - 1.0), last - 1.0), ends)
    line = iota((8, TILE), 0)
    bounds = jnp.where(line == 0, low, jnp.where(line == 1, high, jnp.where(line == 2, first, last)))
    table[...] = (bounds - base).astype(jnp.int32)

    rows[...] = jnp.concatenate([ids, worth, own_inverse, own_inverse] * 2, axis=0)
    pair_lines = jnp.concatenate([ids, worth] * 4, axis=0)
    for tile in range(TILES):
        at = slice(tile * TILE, (tile + 1) * TILE)
        flipped = pair_lines[:, at].T
        id_col[at, :] = jnp.broadcast_to(flipped[:, 0:1], (TILE, TILE))
        worth_col[at, :] = jnp.broadcast_to(flipped[:, 1:2], (TILE, TILE))


def pair_kernel(
    table, from_left, scores, from_right, rows, id_col, worth_col, out, out_again,
    lines, score_col, up_col, discount_col, counts, discount_row, grads, curvs
):
    def spread(column):
        return jnp.broadcast_to(column, (TILE, TILE))

    window = jnp.concatenate([from_left[...], scores[...], from_right[...]], axis=1)
    lines[...] = jnp.concatenate([window, jnp.exp(-window), jnp.exp(window), window] * 2, axis=0)
    for tile in range(TILES):
        at = slice(tile * TILE, (tile + 1) * TILE)
        flipped = lines[:, at].T
        score_col[at, :] = spread(flipped[:, 0:1])
        up_col[at, :] = spread(flipped[:, 1:2])
    counts[...] = jnp.zeros_like(counts)

    active = table[2, 0] // PAIR
    stop = (table[3, 0] + PAIR - 1) // PAIR

    def rank_pair(pair, carry):
        begin = pl.multiple_of(pair * PAIR, PAIR)
        score = jnp.broadcast_to(lines[0:1, pl.ds(begin, PAIR)], (8, PAIR))
        ident = jnp.broadcast_to(rows[0:1, pl.ds(begin, PAIR)], (8, PAIR))

        def count(start, steps, beats, total):
            for sub in range(steps):
                spot = pl.multiple_of(start + sub * 8, 8)
                other = score_col[pl.ds(spot, 8), :]
                other_id = id_col[pl.ds(spot, 8), :]
                parts = []
                for half in range(2):
                    lanes = slice(half * TILE, (half + 1) * TILE)
                    hit = (other_id == ident[:, lanes]) & beats(other, score[:, lanes], half, sub)
                    parts.append(total[half] + jnp.where(hit, 1.0, 0.0))
                total = tuple(parts)
            return total

        def ahead(other, own, half, sub):
            return other >= own

        def behind(other, own, half, sub):
            return other > own

        def around(other, own, half, sub):
            if sub * 8 < half * TILE:
                return other >= own
            if sub * 8 >= (half + 1) * TILE:
                return other > own
            earlier = iota((8, TILE), 0) + (sub * 8 - half * TILE) < iota((8, TILE), 1)
            return (other > own) | ((other == own) & earlier)

        empty = jnp.zeros((8, TILE), F32)
        total = count(begin, PAIR // 8, around, (empty, empty))
        total = lax.fori_loop(
            table[0, 2 * pair] // STEP, begin // STEP,
            lambda i, t: count(i * STEP, STEP // 8, ahead, t), total)
        total = lax.fori_loop(
            (begin + PAIR) // STEP, (table[1, 2 * pair + 1] + STEP - 1) // STEP,
            lambda i, t: count(i * STEP, STEP // 8, behind, t), total)
        counts[:, pl.ds(begin, PAIR)] = jnp.concatenate(total, axis=1)
        return carry

    lax.fori_loop(active, stop, rank_pair, 0)

    rank = jnp.broadcast_to(jnp.sum(counts[...], axis=0, keepdims=True), (8, WIN))
    discount = 1.0 / jnp.log2(2.0 + rank)
    discount_row[...] = discount
    for tile in range(TILES):
        at = slice(tile * TILE, (tile + 1) * TILE)
        discount_col[at, :] = spread(discount[:, at].T[:, 0:1])

    def own_pair(index, carry):
        pair = index + OWN // PAIR
        begin = pl.multiple_of(pair * PAIR, PAIR)

        def own(ref, line):
            return jnp.broadcast_to(ref[line:line + 1, pl.ds(begin, PAIR)], (8, PAIR))

        up = -own(lines, 2)
        ident = own(rows, 0)
        worth = own(rows, 1)
        discount = discount_row[:, pl.ds(begin, PAIR)]

        def meet(block, sums):
            for sub in range(STEP // 8):
                at = pl.ds(pl.multiple_of(block * STEP + sub * 8, 8), 8)
                other_up, other_id = up_col[at, :], id_col[at, :]
                other_discount, other_worth = discount_col[at, :], worth_col[at, :]
                parts = []
                for half in range(2):
                    lanes = slice(half * TILE, (half + 1) * TILE)
                    odds = up[:, lanes] * other_up
                    win = pltpu.reciprocal(1.0 - odds, approx=True)
                    lose = odds * win
                    gap = jnp.where(other_id == ident[:, lanes], discount[:, lanes] - other_discount, 0.0)
                    rise = worth[:, lanes] - other_worth
                    change = jnp.abs(rise * gap)
                    parts.append(sums[half][0] + change * jnp.where(rise > 0.0, win, lose))
                    parts.append(sums[half][1] + change * (win * lose))
                sums = ((parts[0], parts[1]), (parts[2], parts[3]))
            return sums

        empty = jnp.zeros((8, TILE), F32)
        sums = lax.fori_loop(
            table[0, 2 * pair] // STEP, (table[1, 2 * pair + 1] + STEP - 1) // STEP, meet,
            ((empty, empty), (empty, empty)))
        for half in range(2):
            spot = pl.ds(pl.multiple_of(index * PAIR + half * TILE, TILE), TILE)
            grads[:, spot] = sums[half][0]
            curvs[:, spot] = sums[half][1]
        return carry

    lax.fori_loop(0, OWN // PAIR, own_pair, 0)
    inverse = -rows[2:3, OWN:2 * OWN]
    both = jnp.concatenate([
        inverse * jnp.sum(grads[...], axis=0, keepdims=True),
        inverse * jnp.sum(curvs[...], axis=0, keepdims=True)], axis=0)
    out[...] = both
    out_again[...] = both


def in_pieces(value, pieces):
    found = []
    for unused in range(pieces):
        piece = value.astype(BF16)
        found.append(piece)
        value = value - piece.astype(F32)
    return found


def histogram_kernel(
    lambdas, leaves, bins_t, leaf_out, step_out, hist_out,
    left_side, right_side, weights, pair_sent, pair_got, sent, got,
    leaf_mine, leaf_pair, leaf_got, leaf_ring, leaf_both, chunk, chunk_got,
    pair_send, pair_recv, send_sem, recv_sem, leaf_send, leaf_recv, ring_send, ring_recv,
    chunk_send, chunk_recv, one_send, one_recv
):
    query = lax.axis_index("query")
    feat = lax.axis_index("feat")
    core = lax.rem(query, 2)
    chip = lax.div(query, 2)
    other_core = 1 - core
    sibling = chip * 2 + other_core
    chip_y, chip_x = lax.div(chip, SIDE), lax.rem(chip, SIDE)

    def chip_peer(offset):
        return lax.rem(chip_y + lax.div(offset, SIDE), SIDE) * SIDE + lax.rem(chip_x + lax.rem(offset, SIDE), SIDE)

    def ring_peer(offset):
        return lax.rem(feat + offset, RING)

    def remote(source, target, send, recv, device):
        return pltpu.make_async_remote_copy(
            src_ref=source, dst_ref=target, send_sem=send, recv_sem=recv, device_id=device, device_id_type=MESH_ID)

    barrier = pltpu.get_barrier_semaphore()
    pl.semaphore_signal(barrier, inc=1, device_id=(sibling, feat), device_id_type=MESH_ID)

    @pl.loop(1, CHIPS)
    def _(offset):
        pl.semaphore_signal(barrier, inc=1, device_id=(chip_peer(offset) * 2 + core, feat), device_id_type=MESH_ID)

    @pl.loop(1, RING)
    def _(offset):
        pl.semaphore_signal(barrier, inc=1, device_id=(query, ring_peer(offset)), device_id_type=MESH_ID)

    grad, curv = lambdas[0:1, :], lambdas[1:2, :]
    leaf = leaves[...]
    leaf_row = lax.shift_right_logical(leaf, 7)
    leaf_lane = jnp.bitwise_and(leaf, 127)
    in_row = iota((8, OWN), 0) == leaf_row
    lane_hot = (iota((TILE, OWN), 0) == leaf_lane).astype(F32).astype(BF16)
    spread = []
    for value in (grad, curv):
        for piece in in_pieces(value, 3):
            spread.append(jnp.where(in_row, piece.astype(F32), 0.0).astype(BF16))
    leaf_sums = nt_dot(jnp.concatenate(spread, axis=0), lane_hot)
    leaf_mine[0] = leaf_sums[0:8] + leaf_sums[8:16] + leaf_sums[16:24]
    leaf_mine[1] = leaf_sums[24:32] + leaf_sums[32:40] + leaf_sums[40:48]
    chunk[...] = jnp.zeros_like(chunk)

    stats = in_pieces(grad, 2) + in_pieces(curv, 2) + [jnp.ones((1, OWN), BF16)]
    for which, value in enumerate(stats):
        weights[which] = jnp.broadcast_to(value, (16, OWN))

    low_levels = iota((LO, OWN), 0).astype(F32).astype(BF16)
    high_levels = jnp.bitwise_and(iota((16, OWN), 0), 7).astype(F32).astype(BF16)
    upper = iota((16, OWN), 0) < 8
    zero = jnp.zeros((), BF16)
    unit = jnp.ones((), BF16)

    def one_hots(group, slot):
        block = bins_t[pl.ds(pl.multiple_of(group * GROUP, GROUP), GROUP), :]
        high = jnp.floor(block * (1.0 / LO))
        low = block - high * LO
        for k in range(GROUP):
            spread_low = jnp.broadcast_to(low[k:k + 1].astype(BF16), (LO, OWN))
            right_side[slot, k * LO:(k + 1) * LO, :] = jnp.where(spread_low == low_levels, unit, zero)
        for pair in range(GROUP // 2):
            k = 2 * pair
            both = jnp.where(
                upper, jnp.broadcast_to(high[k:k + 1], (16, OWN)),
                jnp.broadcast_to(high[k + 1:k + 2], (16, OWN))).astype(BF16)
            hot = both == high_levels
            for which in range(5):
                left_side[slot, which * 64 + pair * 16:which * 64 + (pair + 1) * 16, :] = jnp.where(
                    hot, weights[which], zero)

    def sums(slot, target, index):
        full = nt_dot(left_side[slot], right_side[slot])
        lane = iota((HI, TILE), 1)
        for stat, whichs in enumerate(((0, 1), (2, 3), (4,))):
            for half in range(2):
                lanes = slice(half * TILE, (half + 1) * TILE)
                total = None
                for which in whichs:
                    picked = None
                    for j in range(4):
                        k = half * 4 + j
                        piece = full[which * 64 + k * HI:which * 64 + (k + 1) * HI, lanes]
                        picked = piece if j == 0 else jnp.where(lane >= j * LO, piece, picked)
                    total = picked if total is None else total + picked
                target[index, stat * HI:(stat + 1) * HI, lanes] = total

    def chip_at(turn):
        return chip_peer(lax.rem(turn + 1, CHIPS))

    def both_groups(turn):
        peer = chip_at(turn)
        one_hots(peer * 2 + other_core, 0)
        one_hots(peer * 2 + core, 1)
        sums(0, pair_sent, peer)
        sums(1, sent, peer)

    def pair_copy(turn):
        peer = chip_at(turn)
        return remote(pair_sent.at[peer], pair_got.at[peer], pair_send.at[peer], pair_recv.at[peer], (sibling, feat))

    def plane_copy(offset):
        peer = chip_peer(offset)
        return remote(sent.at[peer], got.at[chip], send_sem.at[peer], recv_sem.at[chip], (peer * 2 + core, feat))

    def plane_arrival(offset):
        peer = chip_peer(offset)
        return remote(sent.at[peer], got.at[peer], send_sem.at[peer], recv_sem.at[peer], (peer * 2 + core, feat))

    def join(turn):
        pair_copy(turn).wait_recv()
        peer = chip_at(turn)
        sent[peer] = sent[peer] + pair_got[peer]

    @pl.loop(0, EARLY)
    def _(turn):
        both_groups(turn)

    pl.semaphore_wait(barrier, 1 + CHIPS - 1 + RING - 1)

    leaf_swap = remote(leaf_mine.at[other_core], leaf_pair, one_send.at[0], one_recv.at[0], (sibling, feat))
    leaf_swap.start()

    @pl.loop(0, EARLY)
    def _(turn):
        pair_copy(turn).start()

    both_groups(EARLY)
    pair_copy(EARLY).start()
    both_groups(EARLY + 1)
    pair_copy(EARLY + 1).start()

    @pl.loop(1, EARLY + 1)
    def _(turn):
        join(turn - 1)
        plane_copy(turn).start()

    leaf_swap.wait_recv()
    leaf_got[chip] = leaf_mine[core] + leaf_pair[...]

    def leaf_copy(offset):
        peer = chip_peer(offset)
        return remote(leaf_got.at[chip], leaf_got.at[chip], leaf_send.at[peer], leaf_recv.at[chip], (peer * 2 + core, feat))

    def leaf_arrival(offset):
        peer = chip_peer(offset)
        return remote(leaf_got.at[chip], leaf_got.at[peer], leaf_send.at[peer], leaf_recv.at[peer], (peer * 2 + core, feat))

    @pl.loop(1, CHIPS)
    def _(offset):
        leaf_copy(offset).start()

    @pl.loop(EARLY + 2, CHIPS)
    def _(turn):
        both_groups(turn)
        pair_copy(turn).start()
        join(turn - 2)
        plane_copy(turn - 1).start()

    join(CHIPS - 2)
    plane_copy(CHIPS - 1).start()
    join(CHIPS - 1)

    @pl.loop(1, CHIPS)
    def _(offset):
        leaf_arrival(offset).wait_recv()

    leaf_ring[feat] = lax.fori_loop(
        0, CHIPS, lambda peer, total: total + leaf_got[peer], jnp.zeros((8, TILE), F32))

    def ring_copy(offset):
        peer = ring_peer(offset)
        return remote(leaf_ring.at[feat], leaf_ring.at[feat], ring_send.at[peer], ring_recv.at[feat], (query, peer))

    def ring_arrival(offset):
        peer = ring_peer(offset)
        return remote(leaf_ring.at[feat], leaf_ring.at[peer], ring_send.at[peer], ring_recv.at[peer], (query, peer))

    @pl.loop(1, RING)
    def _(offset):
        ring_copy(offset).start()

    def add_hist(offset, total):
        plane_arrival(offset).wait_recv()
        return total + got[chip_peer(offset)]

    summed = lax.fori_loop(1, CHIPS, add_hist, sent[chip])

    lane_block = lax.shift_right_logical(iota((GROUP, TILE), 1), 5)
    holder = iota((GROUP, TILE), 0)
    for stat in range(3):
        for half in range(2):
            moved = jnp.zeros((GROUP, TILE), F32)
            for r in range(4):
                row = stat * HI + half * 4 + r
                line = jnp.where(
                    holder < 4, jnp.broadcast_to(summed[row:row + 1, 0:TILE], (GROUP, TILE)),
                    jnp.broadcast_to(summed[row:row + 1, TILE:2 * TILE], (GROUP, TILE)))
                for kk in range(4):
                    shift = (r - kk) % 4 * LO
                    turned = pltpu.roll(line, shift, 1) if shift else line
                    moved = jnp.where((jnp.bitwise_and(holder, 3) == kk) & (lane_block == r), turned, moved)
            line = stat * 2 + half
            for k in range(GROUP):
                chunk[k, line:line + 1, :] = moved[k:k + 1, :]

    def chunk_copy(offset):
        peer = ring_peer(offset)
        return remote(chunk.at[peer], chunk_got.at[feat], chunk_send.at[peer], chunk_recv.at[feat], (query, peer))

    def chunk_arrival(offset):
        peer = ring_peer(offset)
        return remote(chunk.at[peer], chunk_got.at[peer], chunk_send.at[peer], chunk_recv.at[peer], (query, peer))

    @pl.loop(1, RING)
    def _(offset):
        chunk_copy(offset).start()

    @pl.loop(1, RING)
    def _(offset):
        ring_arrival(offset).wait_recv()

    half_total = leaf_ring[0]
    for peer in range(1, RING):
        half_total = half_total + leaf_ring[peer]
    leaf_both[core] = half_total
    leaf_back = remote(leaf_both.at[core], leaf_both.at[core], one_send.at[1], one_recv.at[1], (sibling, feat))
    leaf_back.start()

    leaf_back_here = remote(
        leaf_both.at[core], leaf_both.at[other_core], one_send.at[1], one_recv.at[1], (sibling, feat))
    leaf_back_here.wait_recv()
    total_grad, total_curv = leaf_both[0], leaf_both[1]
    shrunk = jnp.maximum(jnp.abs(total_grad) - lasso_penalty, 0.0) / (total_curv + ridge_penalty)
    values = jnp.where(total_grad > 0.0, -shrunk, shrunk)
    leaf_out[...] = values
    found = jnp.zeros((8, OWN), F32)
    for piece in in_pieces(values, 3):
        found = found + jnp.dot(piece, lane_hot, preferred_element_type=F32)
    step_out[...] = shrinkage * jnp.sum(jnp.where(in_row, found, 0.0), axis=0, keepdims=True)

    def add_chunk(offset, total):
        chunk_arrival(offset).wait_recv()
        return total + chunk_got[ring_peer(offset)]

    hist_out[...] = lax.fori_loop(1, RING, add_chunk, chunk[feat])

    leaf_swap.wait_send()
    leaf_back.wait_send()
    pair_copy(CHIPS - 1).wait_send()

    @pl.loop(1, CHIPS)
    def _(offset):
        pair_copy(offset - 1).wait_send()
        plane_copy(offset).wait_send()
        leaf_copy(offset).wait_send()

    @pl.loop(1, RING)
    def _(offset):
        ring_copy(offset).wait_send()
        chunk_copy(offset).wait_send()


def finish_kernel(leaf_in, step_in, hist_in, leaf_out, step_out, hist_out, hist, sem):
    for stat in range(3):
        for half in range(2):
            line = stat * 2 + half
            hist[stat:stat + 1, half * TILE:(half + 1) * TILE] = hist_in[line:line + 1, :]
    copies = [
        pltpu.make_async_copy(source, target, sem.at[which])
        for which, (source, target) in enumerate(((leaf_in, leaf_out), (step_in, step_out), (hist, hist_out)))]
    for copy in copies:
        copy.start()
    for copy in copies:
        copy.wait()


def local(scores, labels, leaves, bins, lengths, owner):
    shape = jax.ShapeDtypeStruct
    dma = pltpu.SemaphoreType.DMA
    column = pltpu.VMEM((WIN, TILE), F32)
    ring = [(place, (place + 1) % RING) for place in range(RING)]
    from_left = lax.ppermute(scores, "feat", ring)
    from_right = lax.ppermute(scores, "feat", [(there, here) for here, there in ring])
    rows, table, bins_t, id_col, worth_col = pl.pallas_call(
        prepare_kernel,
        out_shape=(
            shape((8, WIN), F32),
            shape((8, TILE), jnp.int32),
            shape((FEATURES, OWN), F32),
            shape((WIN, TILE), F32),
            shape((WIN, TILE), F32),
        ),
        in_specs=[VMEM] * 4,
        out_specs=(VMEM,) * 5,
        cost_estimate=pl.CostEstimate(flops=2**30, bytes_accessed=2**23, transcendentals=0),
        compiler_params=pltpu.CompilerParams(vmem_limit_bytes=32 * 2**20),
        name="prepare",
    )(labels.reshape(1, BLOCK), lengths, owner.reshape(1, FEATURES), bins)
    lambdas, lambdas_again = pl.pallas_call(
        pair_kernel,
        out_shape=(shape((2, OWN), F32), shape((2, OWN), F32)),
        in_specs=[SMEM] + [VMEM] * 6,
        out_specs=(VMEM, VMEM),
        scratch_shapes=[pltpu.VMEM((8, WIN), F32)] + [column] * 3 + [pltpu.VMEM((8, WIN), F32)] * 2 + [pltpu.VMEM((8, OWN), F32)] * 2,
        compiler_params=pltpu.CompilerParams(vmem_limit_bytes=32 * 2**20),
        name="pairs",
    )(table, from_left.reshape(1, OWN), scores.reshape(1, OWN), from_right.reshape(1, OWN), rows, id_col, worth_col)
    part = pltpu.VMEM((CHIPS, 3 * HI, GROUP * LO), F32)
    leaf_values, score_step, histograms = pl.pallas_call(
        histogram_kernel,
        out_shape=(
            shape((8, TILE), F32),
            shape((1, OWN), F32),
            shape((8, TILE), F32),
        ),
        in_specs=[VMEM] * 3,
        out_specs=(VMEM, VMEM, VMEM),
        scratch_shapes=[
            pltpu.VMEM((2, 5 * GROUP * HI, OWN), BF16),
            pltpu.VMEM((2, GROUP * LO, OWN), BF16),
            pltpu.VMEM((5, 16, OWN), BF16),
            part, part, part, part,
            pltpu.VMEM((2, 8, TILE), F32),
            pltpu.VMEM((8, TILE), F32),
            pltpu.VMEM((CHIPS, 8, TILE), F32),
            pltpu.VMEM((RING, 8, TILE), F32),
            pltpu.VMEM((2, 8, TILE), F32),
            pltpu.VMEM((RING, 8, TILE), F32),
            pltpu.VMEM((RING, 8, TILE), F32),
            dma((CHIPS,)), dma((CHIPS,)), dma((CHIPS,)), dma((CHIPS,)), dma((CHIPS,)), dma((CHIPS,)),
            dma((RING,)), dma((RING,)), dma((RING,)), dma((RING,)), dma((2,)), dma((2,)),
        ],
        compiler_params=pltpu.CompilerParams(
            collective_id=2, has_side_effects=True, vmem_limit_bytes=32 * 2**20),
        name="histograms",
    )(lambdas_again, leaves.reshape(1, OWN), bins_t)
    leaf_values, score_step, histograms = pl.pallas_call(
        finish_kernel,
        out_shape=(
            shape((8, TILE), F32),
            shape((1, OWN), F32),
            shape((3, BINS), F32),
        ),
        in_specs=[VMEM] * 3,
        out_specs=(HBM, HBM, HBM),
        scratch_shapes=[pltpu.VMEM((3, BINS), F32), dma((3,))],
        compiler_params=pltpu.CompilerParams(vmem_limit_bytes=2**21),
        name="finish",
    )(leaf_values, score_step, histograms)
    return lambdas, leaf_values.reshape(LEAVES), score_step.reshape(OWN), histograms


def solution(mesh):
    in_specs = (
        P(("query", "feat")),
        P("query"),
        P(("query", "feat")),
        P(("query", "feat"), None),
        P("query", None),
        P(),
    )
    out_specs = (P(None, ("query", "feat")), P(), P(("query", "feat")), P(None, ("query", "feat")))
    return jax.shard_map(local, mesh=mesh, in_specs=in_specs, out_specs=out_specs, check_vma=False)
```

```python
import jax
import jax.numpy as jnp
from jax import lax
from jax.experimental import pallas as pl
from jax.experimental.pallas import tpu as pltpu
from jax.sharding import PartitionSpec as P

BINS = 256
LEAVES = 1024
FEATURES = 256
OWN = 1024
WIN = 3 * OWN
BLOCK = 8192
QUERIES = 32
TILE = 128
TILES = WIN // TILE
OWN_TILES = OWN // TILE
STEP = 128
PAIR = 2 * TILE
CHIPS = 16
SIDE = 4
RING = 8
GROUP = 8
EARLY = 5
HI = 8
LO = 32

lasso_penalty = 1.0
ridge_penalty = 1.0
shrinkage = 0.1

F32 = jnp.float32
BF16 = jnp.bfloat16
MESH_ID = pl.DeviceIdType.MESH
VMEM = pl.BlockSpec(memory_space=pltpu.VMEM)
HBM = pl.BlockSpec(memory_space=pltpu.HBM)
SMEM = pl.BlockSpec(memory_space=pltpu.SMEM)


def nt_dot(left, right):
    return lax.dot_general(left, right, (((1,), (1,)), ((), ())), preferred_element_type=F32)


def spread(line):
    return jnp.broadcast_to(line, (TILE, TILE)).T


def in_hbm(array):
    return pltpu.with_memory_space_constraint(array, pltpu.HBM)


def iota(shape, axis):
    return lax.broadcasted_iota(jnp.int32, shape, axis)


def prepare_kernel(
    labels_in, lengths_in, owner_in, bins_in, rows, table, bins_t, id_col, worth_col,
    labels, lengths, owner, bins, load_sem
):
    feat = lax.axis_index("feat")
    left = lax.rem(feat + RING - 1, RING)
    right = lax.rem(feat + 1, RING)

    loads = [
        pltpu.make_async_copy(source, target, load_sem.at[which])
        for which, (source, target) in enumerate((
            (lengths_in, lengths), (labels_in, labels), (owner_in, owner), (bins_in, bins)))]
    for load in loads:
        load.start()
    for load in loads[:2]:
        load.wait()

    base = (feat * OWN - OWN).astype(F32)
    length_row = jnp.broadcast_to(lengths[...].astype(F32), (QUERIES, QUERIES))
    other, one = iota((QUERIES, QUERIES), 1), iota((QUERIES, QUERIES), 0)
    starts = jnp.sum(jnp.where(other < one, length_row, 0.0), axis=1, keepdims=True)
    ends = jnp.sum(jnp.where(other <= one, length_row, 0.0), axis=1, keepdims=True)
    place = iota((1, WIN), 1).astype(F32) + base
    inside = (place >= starts) & (place < ends)
    passed = jnp.sum(jnp.where(place >= ends, 1.0, 0.0), axis=0, keepdims=True)
    ids = jnp.where(place < 0.0, -1.0, passed)

    def label_part(block):
        return labels[:, pl.ds(pl.multiple_of(block * OWN, OWN), OWN)]

    grades = jnp.concatenate([label_part(left), label_part(feat), label_part(right)], axis=1)
    worth = lax.shift_left(jnp.ones_like(grades), grades).astype(F32)

    at_least = (jnp.broadcast_to(grades, (8, WIN)) > iota((8, WIN), 0)).astype(F32).astype(BF16)
    counts = nt_dot(inside.astype(F32).astype(BF16), at_least)
    spot = iota((1, OWN), 1).astype(F32)
    gain = 1.0 / jnp.log2(2.0 + spot)
    parts = jnp.zeros((QUERIES, OWN), F32)
    for level in range(4):
        parts = parts + jnp.where(spot < counts[:, level:level + 1], gain * float(2 ** level), 0.0)
    ideal = jnp.sum(parts, axis=1, keepdims=True)
    usable = ideal > 0.5
    inverse = jnp.where(usable, 1.0 / jnp.where(usable, ideal, 1.0), 0.0)
    own_inverse = jnp.sum(jnp.where(inside, inverse, 0.0), axis=0, keepdims=True)

    def bound_at(spots, values):
        hit = (spots >= starts) & (spots < ends)
        return jnp.sum(jnp.where(hit, values, 0.0), axis=0, keepdims=True)

    zeros = jnp.zeros((1, TILE), F32)
    first = bound_at(zeros + (base + OWN), starts)
    last = bound_at(zeros + (base + 2 * OWN - 1.0), ends)
    tile_first = base + iota((1, TILE), 1).astype(F32) * TILE
    low = bound_at(jnp.maximum(tile_first, first), starts)
    high = bound_at(jnp.minimum(tile_first + (TILE - 1.0), last - 1.0), ends)
    line = iota((8, TILE), 0)
    bounds = jnp.where(line == 0, low, jnp.where(line == 1, high, jnp.where(line == 2, first, last)))
    table[...] = (bounds - base).astype(jnp.int32)

    rows[...] = jnp.concatenate([ids, worth, own_inverse, own_inverse] * 2, axis=0)
    for tile in range(TILES):
        at = slice(tile * TILE, (tile + 1) * TILE)
        id_col[at, :] = spread(ids[:, at])
        worth_col[at, :] = spread(worth[:, at])

    for load in loads[2:]:
        load.wait()
    pick_t = (iota((FEATURES, FEATURES), 0) == owner[...]).astype(F32)
    pick = pick_t.T.astype(BF16)
    bins_t[...] = nt_dot(pick, bins[...].astype(F32).astype(BF16))


def pair_kernel(
    table, from_left, scores, from_right, rows, id_col, worth_col, out, out_again,
    lines, score_col, up_col, discount_col, counts, discount_row, grads, curvs
):
    window = jnp.concatenate([from_left[...], scores[...], from_right[...]], axis=1)
    lines[...] = jnp.concatenate([window, jnp.exp(-window), jnp.exp(window), window] * 2, axis=0)
    for tile in range(TILES):
        at = slice(tile * TILE, (tile + 1) * TILE)
        score_col[at, :] = spread(lines[0:1, at])
        up_col[at, :] = spread(lines[1:2, at])
    counts[...] = jnp.zeros_like(counts)

    active = table[2, 0] // PAIR
    stop = (table[3, 0] + PAIR - 1) // PAIR

    def rank_pair(pair, carry):
        begin = pl.multiple_of(pair * PAIR, PAIR)
        score = jnp.broadcast_to(lines[0:1, pl.ds(begin, PAIR)], (8, PAIR))
        ident = jnp.broadcast_to(rows[0:1, pl.ds(begin, PAIR)], (8, PAIR))

        def count(start, steps, beats, total):
            for sub in range(steps):
                spot = pl.multiple_of(start + sub * 8, 8)
                other = score_col[pl.ds(spot, 8), :]
                other_id = id_col[pl.ds(spot, 8), :]
                parts = []
                for half in range(2):
                    lanes = slice(half * TILE, (half + 1) * TILE)
                    hit = (other_id == ident[:, lanes]) & beats(other, score[:, lanes], half, sub)
                    parts.append(total[half] + jnp.where(hit, 1.0, 0.0))
                total = tuple(parts)
            return total

        def ahead(other, own, half, sub):
            return other >= own

        def behind(other, own, half, sub):
            return other > own

        def around(other, own, half, sub):
            if sub * 8 < half * TILE:
                return other >= own
            if sub * 8 >= (half + 1) * TILE:
                return other > own
            earlier = iota((8, TILE), 0) + (sub * 8 - half * TILE) < iota((8, TILE), 1)
            return (other > own) | ((other == own) & earlier)

        empty = jnp.zeros((8, TILE), F32)
        total = count(begin, PAIR // 8, around, (empty, empty))
        total = lax.fori_loop(
            table[0, 2 * pair] // STEP, begin // STEP,
            lambda i, t: count(i * STEP, STEP // 8, ahead, t), total)
        total = lax.fori_loop(
            (begin + PAIR) // STEP, (table[1, 2 * pair + 1] + STEP - 1) // STEP,
            lambda i, t: count(i * STEP, STEP // 8, behind, t), total)
        counts[:, pl.ds(begin, PAIR)] = jnp.concatenate(total, axis=1)
        return carry

    lax.fori_loop(active, stop, rank_pair, 0)

    rank = jnp.broadcast_to(jnp.sum(counts[...], axis=0, keepdims=True), (8, WIN))
    discount = 1.0 / jnp.log2(2.0 + rank)
    discount_row[...] = discount
    for tile in range(TILES):
        at = slice(tile * TILE, (tile + 1) * TILE)
        discount_col[at, :] = spread(discount[0:1, at])

    def own_pair(index, carry):
        pair = index + OWN // PAIR
        begin = pl.multiple_of(pair * PAIR, PAIR)

        def own(ref, line):
            return jnp.broadcast_to(ref[line:line + 1, pl.ds(begin, PAIR)], (8, PAIR))

        up = -own(lines, 2)
        ident = own(rows, 0)
        worth = own(rows, 1)
        discount = discount_row[:, pl.ds(begin, PAIR)]

        def meet(block, sums):
            for sub in range(STEP // 8):
                at = pl.ds(pl.multiple_of(block * STEP + sub * 8, 8), 8)
                other_up, other_id = up_col[at, :], id_col[at, :]
                other_discount, other_worth = discount_col[at, :], worth_col[at, :]
                parts = []
                for half in range(2):
                    lanes = slice(half * TILE, (half + 1) * TILE)
                    odds = up[:, lanes] * other_up
                    win = pltpu.reciprocal(1.0 - odds, approx=True)
                    lose = odds * win
                    gap = jnp.where(other_id == ident[:, lanes], discount[:, lanes] - other_discount, 0.0)
                    rise = worth[:, lanes] - other_worth
                    change = jnp.abs(rise * gap)
                    parts.append(sums[half][0] + change * jnp.where(rise > 0.0, win, lose))
                    parts.append(sums[half][1] + change * (win * lose))
                sums = ((parts[0], parts[1]), (parts[2], parts[3]))
            return sums

        empty = jnp.zeros((8, TILE), F32)
        sums = lax.fori_loop(
            table[0, 2 * pair] // STEP, (table[1, 2 * pair + 1] + STEP - 1) // STEP, meet,
            ((empty, empty), (empty, empty)))
        for half in range(2):
            spot = pl.ds(pl.multiple_of(index * PAIR + half * TILE, TILE), TILE)
            grads[:, spot] = sums[half][0]
            curvs[:, spot] = sums[half][1]
        return carry

    lax.fori_loop(0, OWN // PAIR, own_pair, 0)
    inverse = -rows[2:3, OWN:2 * OWN]
    both = jnp.concatenate([
        inverse * jnp.sum(grads[...], axis=0, keepdims=True),
        inverse * jnp.sum(curvs[...], axis=0, keepdims=True)], axis=0)
    out[...] = both
    out_again[...] = both


def in_pieces(value, pieces):
    found = []
    for unused in range(pieces):
        piece = value.astype(BF16)
        found.append(piece)
        value = value - piece.astype(F32)
    return found


def histogram_kernel(
    lambdas, leaves, bins_t, leaf_out, step_out, hist_out,
    left_side, right_side, weights, pair_sent, pair_got, sent, got,
    leaf_mine, leaf_pair, leaf_got, leaf_ring, leaf_both, chunk, chunk_got,
    pair_send, pair_recv, send_sem, recv_sem, leaf_send, leaf_recv, ring_send, ring_recv,
    chunk_send, chunk_recv, one_send, one_recv
):
    query = lax.axis_index("query")
    feat = lax.axis_index("feat")
    core = lax.rem(query, 2)
    chip = lax.div(query, 2)
    other_core = 1 - core
    sibling = chip * 2 + other_core
    chip_y, chip_x = lax.div(chip, SIDE), lax.rem(chip, SIDE)

    def steps_to(offset):
        turn = lax.rem(offset + CHIPS - 1, CHIPS)
        return lax.rem(lax.div(turn, SIDE) + 1, SIDE), lax.rem(lax.rem(turn, SIDE) + 1, SIDE)

    def chip_peer(offset):
        down, across = steps_to(offset)
        return lax.rem(chip_y + down, SIDE) * SIDE + lax.rem(chip_x + across, SIDE)

    def chip_source(offset):
        down, across = steps_to(offset)
        return lax.rem(chip_y + SIDE - down, SIDE) * SIDE + lax.rem(chip_x + SIDE - across, SIDE)

    def ring_peer(offset):
        return lax.rem(feat + offset, RING)

    def remote(source, target, send, recv, device):
        return pltpu.make_async_remote_copy(
            src_ref=source, dst_ref=target, send_sem=send, recv_sem=recv, device_id=device, device_id_type=MESH_ID)

    barrier = pltpu.get_barrier_semaphore()
    pl.semaphore_signal(barrier, inc=1, device_id=(sibling, feat), device_id_type=MESH_ID)

    @pl.loop(1, CHIPS)
    def _(offset):
        pl.semaphore_signal(barrier, inc=1, device_id=(chip_peer(offset) * 2 + core, feat), device_id_type=MESH_ID)

    @pl.loop(1, RING)
    def _(offset):
        pl.semaphore_signal(barrier, inc=1, device_id=(query, ring_peer(offset)), device_id_type=MESH_ID)

    grad, curv = lambdas[0:1, :], lambdas[1:2, :]
    leaf = leaves[...]
    leaf_row = lax.shift_right_logical(leaf, 7)
    leaf_lane = jnp.bitwise_and(leaf, 127)
    in_row = iota((8, OWN), 0) == leaf_row
    lane_hot = (iota((TILE, OWN), 0) == leaf_lane).astype(F32).astype(BF16)
    placed = []
    for value in (grad, curv):
        for piece in in_pieces(value, 3):
            placed.append(jnp.where(in_row, piece.astype(F32), 0.0).astype(BF16))
    leaf_sums = nt_dot(jnp.concatenate(placed, axis=0), lane_hot)
    leaf_mine[0] = leaf_sums[0:8] + leaf_sums[8:16] + leaf_sums[16:24]
    leaf_mine[1] = leaf_sums[24:32] + leaf_sums[32:40] + leaf_sums[40:48]
    chunk[...] = jnp.zeros_like(chunk)

    stats = in_pieces(grad, 2) + in_pieces(curv, 2) + [jnp.ones((1, OWN), BF16)]
    for which, value in enumerate(stats):
        weights[which] = jnp.broadcast_to(value, (16, OWN))

    low_levels = iota((LO, OWN), 0).astype(F32).astype(BF16)
    high_levels = jnp.bitwise_and(iota((16, OWN), 0), 7).astype(F32).astype(BF16)
    upper = iota((16, OWN), 0) < 8
    zero = jnp.zeros((), BF16)
    unit = jnp.ones((), BF16)

    def one_hots(group, slot):
        block = bins_t[pl.ds(pl.multiple_of(group * GROUP, GROUP), GROUP), :]
        high = jnp.floor(block * (1.0 / LO))
        low = block - high * LO
        for k in range(GROUP):
            spread_low = jnp.broadcast_to(low[k:k + 1].astype(BF16), (LO, OWN))
            right_side[slot, k * LO:(k + 1) * LO, :] = jnp.where(spread_low == low_levels, unit, zero)
        for pair in range(GROUP // 2):
            k = 2 * pair
            both = jnp.where(
                upper, jnp.broadcast_to(high[k:k + 1], (16, OWN)),
                jnp.broadcast_to(high[k + 1:k + 2], (16, OWN))).astype(BF16)
            hot = both == high_levels
            for which in range(5):
                left_side[slot, which * 64 + pair * 16:which * 64 + (pair + 1) * 16, :] = jnp.where(
                    hot, weights[which], zero)

    def sums(slot, target, index):
        full = nt_dot(left_side[slot], right_side[slot])
        lane = iota((HI, TILE), 1)
        for stat, whichs in enumerate(((0, 1), (2, 3), (4,))):
            for half in range(2):
                lanes = slice(half * TILE, (half + 1) * TILE)
                total = None
                for which in whichs:
                    picked = None
                    for j in range(4):
                        k = half * 4 + j
                        piece = full[which * 64 + k * HI:which * 64 + (k + 1) * HI, lanes]
                        picked = piece if j == 0 else jnp.where(lane >= j * LO, piece, picked)
                    total = picked if total is None else total + picked
                target[index, stat * HI:(stat + 1) * HI, lanes] = total

    def chip_at(turn):
        return chip_peer(lax.rem(turn + 1, CHIPS))

    def both_groups(turn):
        peer = chip_at(turn)
        one_hots(peer * 2 + other_core, 0)
        one_hots(peer * 2 + core, 1)
        sums(0, pair_sent, peer)
        sums(1, sent, peer)

    def pair_copy(turn):
        peer = chip_at(turn)
        return remote(pair_sent.at[peer], pair_got.at[peer], pair_send.at[peer], pair_recv.at[peer], (sibling, feat))

    def plane_copy(offset):
        peer = chip_peer(offset)
        return remote(sent.at[peer], got.at[chip], send_sem.at[peer], recv_sem.at[chip], (peer * 2 + core, feat))

    def plane_arrival(offset):
        peer = chip_source(offset)
        return remote(sent.at[peer], got.at[peer], send_sem.at[peer], recv_sem.at[peer], (peer * 2 + core, feat))

    def join(turn):
        pair_copy(turn).wait_recv()
        peer = chip_at(turn)
        sent[peer] = sent[peer] + pair_got[peer]

    @pl.loop(0, EARLY)
    def _(turn):
        both_groups(turn)

    pl.semaphore_wait(barrier, 1 + CHIPS - 1 + RING - 1)

    leaf_swap = remote(leaf_mine.at[other_core], leaf_pair, one_send.at[0], one_recv.at[0], (sibling, feat))
    leaf_swap.start()

    @pl.loop(0, EARLY)
    def _(turn):
        pair_copy(turn).start()

    both_groups(EARLY)
    pair_copy(EARLY).start()
    both_groups(EARLY + 1)
    pair_copy(EARLY + 1).start()

    @pl.loop(1, EARLY + 1)
    def _(turn):
        join(turn - 1)
        plane_copy(turn).start()

    leaf_swap.wait_recv()
    leaf_got[chip] = leaf_mine[core] + leaf_pair[...]

    def leaf_copy(offset):
        peer = chip_peer(offset)
        return remote(leaf_got.at[chip], leaf_got.at[chip], leaf_send.at[peer], leaf_recv.at[chip], (peer * 2 + core, feat))

    def leaf_arrival(offset):
        peer = chip_peer(offset)
        return remote(leaf_got.at[chip], leaf_got.at[peer], leaf_send.at[peer], leaf_recv.at[peer], (peer * 2 + core, feat))

    @pl.loop(1, CHIPS)
    def _(offset):
        leaf_copy(offset).start()

    @pl.loop(EARLY + 2, CHIPS)
    def _(turn):
        both_groups(turn)
        pair_copy(turn).start()
        join(turn - 2)
        plane_copy(turn - 1).start()

    join(CHIPS - 2)
    plane_copy(CHIPS - 1).start()
    join(CHIPS - 1)

    @pl.loop(1, CHIPS)
    def _(offset):
        leaf_arrival(offset).wait_recv()

    leaf_ring[feat] = lax.fori_loop(
        0, CHIPS, lambda peer, total: total + leaf_got[peer], jnp.zeros((8, TILE), F32))

    def ring_copy(offset):
        peer = ring_peer(offset)
        return remote(leaf_ring.at[feat], leaf_ring.at[feat], ring_send.at[peer], ring_recv.at[feat], (query, peer))

    def ring_arrival(offset):
        peer = ring_peer(offset)
        return remote(leaf_ring.at[feat], leaf_ring.at[peer], ring_send.at[peer], ring_recv.at[peer], (query, peer))

    @pl.loop(1, RING)
    def _(offset):
        ring_copy(offset).start()

    def add_hist(offset, total):
        plane_arrival(offset).wait_recv()
        return total + got[chip_source(offset)]

    summed = lax.fori_loop(1, CHIPS, add_hist, sent[chip])

    lane_block = lax.shift_right_logical(iota((GROUP, TILE), 1), 5)
    holder = iota((GROUP, TILE), 0)
    for stat in range(3):
        for half in range(2):
            moved = jnp.zeros((GROUP, TILE), F32)
            for r in range(4):
                row = stat * HI + half * 4 + r
                line = jnp.where(
                    holder < 4, jnp.broadcast_to(summed[row:row + 1, 0:TILE], (GROUP, TILE)),
                    jnp.broadcast_to(summed[row:row + 1, TILE:2 * TILE], (GROUP, TILE)))
                for kk in range(4):
                    shift = (r - kk) % 4 * LO
                    turned = pltpu.roll(line, shift, 1) if shift else line
                    moved = jnp.where((jnp.bitwise_and(holder, 3) == kk) & (lane_block == r), turned, moved)
            line = stat * 2 + half
            for k in range(GROUP):
                chunk[k, line:line + 1, :] = moved[k:k + 1, :]

    def chunk_copy(offset):
        peer = ring_peer(offset)
        return remote(chunk.at[peer], chunk_got.at[feat], chunk_send.at[peer], chunk_recv.at[feat], (query, peer))

    def chunk_arrival(offset):
        peer = ring_peer(offset)
        return remote(chunk.at[peer], chunk_got.at[peer], chunk_send.at[peer], chunk_recv.at[peer], (query, peer))

    @pl.loop(1, RING)
    def _(offset):
        chunk_copy(offset).start()

    @pl.loop(1, RING)
    def _(offset):
        ring_arrival(offset).wait_recv()

    half_total = leaf_ring[0]
    for peer in range(1, RING):
        half_total = half_total + leaf_ring[peer]
    leaf_both[core] = half_total
    leaf_back = remote(leaf_both.at[core], leaf_both.at[core], one_send.at[1], one_recv.at[1], (sibling, feat))
    leaf_back.start()

    leaf_back_here = remote(
        leaf_both.at[core], leaf_both.at[other_core], one_send.at[1], one_recv.at[1], (sibling, feat))
    leaf_back_here.wait_recv()
    total_grad, total_curv = leaf_both[0], leaf_both[1]
    shrunk = jnp.maximum(jnp.abs(total_grad) - lasso_penalty, 0.0) / (total_curv + ridge_penalty)
    values = jnp.where(total_grad > 0.0, -shrunk, shrunk)
    leaf_out[...] = values
    found = jnp.zeros((8, OWN), F32)
    for piece in in_pieces(values, 3):
        found = found + jnp.dot(piece, lane_hot, preferred_element_type=F32)
    step_out[...] = shrinkage * jnp.sum(jnp.where(in_row, found, 0.0), axis=0, keepdims=True)

    def add_chunk(offset, total):
        chunk_arrival(offset).wait_recv()
        return total + chunk_got[ring_peer(offset)]

    hist_out[...] = lax.fori_loop(1, RING, add_chunk, chunk[feat])

    leaf_swap.wait_send()
    leaf_back.wait_send()
    pair_copy(CHIPS - 1).wait_send()

    @pl.loop(1, CHIPS)
    def _(offset):
        pair_copy(offset - 1).wait_send()
        plane_copy(offset).wait_send()
        leaf_copy(offset).wait_send()

    @pl.loop(1, RING)
    def _(offset):
        ring_copy(offset).wait_send()
        chunk_copy(offset).wait_send()


def finish_kernel(leaf_in, step_in, hist_in, leaf_out, step_out, hist_out, hist, sem):
    for stat in range(3):
        for half in range(2):
            line = stat * 2 + half
            hist[stat:stat + 1, half * TILE:(half + 1) * TILE] = hist_in[line:line + 1, :]
    copies = [
        pltpu.make_async_copy(source, target, sem.at[which])
        for which, (source, target) in enumerate(((leaf_in, leaf_out), (step_in, step_out), (hist, hist_out)))]
    for copy in copies:
        copy.start()
    for copy in copies:
        copy.wait()


def local(scores, labels, leaves, bins, lengths, owner):
    shape = jax.ShapeDtypeStruct
    dma = pltpu.SemaphoreType.DMA
    column = pltpu.VMEM((WIN, TILE), F32)
    ring = [(place, (place + 1) % RING) for place in range(RING)]
    from_left = lax.ppermute(scores, "feat", ring)
    from_right = lax.ppermute(scores, "feat", [(there, here) for here, there in ring])
    rows, table, bins_t, id_col, worth_col = pl.pallas_call(
        prepare_kernel,
        out_shape=(
            shape((8, WIN), F32),
            shape((8, TILE), jnp.int32),
            shape((FEATURES, OWN), F32),
            shape((WIN, TILE), F32),
            shape((WIN, TILE), F32),
        ),
        in_specs=[HBM] * 4,
        out_specs=(VMEM,) * 5,
        scratch_shapes=[
            pltpu.VMEM((1, BLOCK), jnp.int32), pltpu.VMEM((1, QUERIES), jnp.int32),
            pltpu.VMEM((1, FEATURES), jnp.int32), pltpu.VMEM((OWN, FEATURES), jnp.int32), dma((4,))],
        cost_estimate=pl.CostEstimate(flops=2**30, bytes_accessed=2**23, transcendentals=0),
        compiler_params=pltpu.CompilerParams(vmem_limit_bytes=32 * 2**20),
        name="prepare",
    )(in_hbm(labels.reshape(1, BLOCK)), in_hbm(lengths), in_hbm(owner.reshape(1, FEATURES)), in_hbm(bins))
    lambdas, lambdas_again = pl.pallas_call(
        pair_kernel,
        out_shape=(shape((2, OWN), F32), shape((2, OWN), F32)),
        in_specs=[SMEM] + [VMEM] * 6,
        out_specs=(VMEM, VMEM),
        scratch_shapes=[pltpu.VMEM((8, WIN), F32)] + [column] * 3 + [pltpu.VMEM((8, WIN), F32)] * 2 + [pltpu.VMEM((8, OWN), F32)] * 2,
        compiler_params=pltpu.CompilerParams(vmem_limit_bytes=32 * 2**20),
        name="pairs",
    )(table, from_left.reshape(1, OWN), scores.reshape(1, OWN), from_right.reshape(1, OWN), rows, id_col, worth_col)
    part = pltpu.VMEM((CHIPS, 3 * HI, GROUP * LO), F32)
    leaf_values, score_step, histograms = pl.pallas_call(
        histogram_kernel,
        out_shape=(
            shape((8, TILE), F32),
            shape((1, OWN), F32),
            shape((8, TILE), F32),
        ),
        in_specs=[VMEM] * 3,
        out_specs=(VMEM, VMEM, VMEM),
        scratch_shapes=[
            pltpu.VMEM((2, 5 * GROUP * HI, OWN), BF16),
            pltpu.VMEM((2, GROUP * LO, OWN), BF16),
            pltpu.VMEM((5, 16, OWN), BF16),
            part, part, part, part,
            pltpu.VMEM((2, 8, TILE), F32),
            pltpu.VMEM((8, TILE), F32),
            pltpu.VMEM((CHIPS, 8, TILE), F32),
            pltpu.VMEM((RING, 8, TILE), F32),
            pltpu.VMEM((2, 8, TILE), F32),
            pltpu.VMEM((RING, 8, TILE), F32),
            pltpu.VMEM((RING, 8, TILE), F32),
            dma((CHIPS,)), dma((CHIPS,)), dma((CHIPS,)), dma((CHIPS,)), dma((CHIPS,)), dma((CHIPS,)),
            dma((RING,)), dma((RING,)), dma((RING,)), dma((RING,)), dma((2,)), dma((2,)),
        ],
        compiler_params=pltpu.CompilerParams(
            collective_id=2, has_side_effects=True, vmem_limit_bytes=32 * 2**20),
        name="histograms",
    )(lambdas_again, leaves.reshape(1, OWN), bins_t)
    leaf_values, score_step, histograms = pl.pallas_call(
        finish_kernel,
        out_shape=(
            shape((8, TILE), F32),
            shape((1, OWN), F32),
            shape((3, BINS), F32),
        ),
        in_specs=[VMEM] * 3,
        out_specs=(HBM, HBM, HBM),
        scratch_shapes=[pltpu.VMEM((3, BINS), F32), dma((3,))],
        compiler_params=pltpu.CompilerParams(vmem_limit_bytes=2**21),
        name="finish",
    )(leaf_values, score_step, histograms)
    return lambdas, leaf_values.reshape(LEAVES), score_step.reshape(OWN), histograms


def solution(mesh):
    in_specs = (
        P(("query", "feat")),
        P("query"),
        P(("query", "feat")),
        P(("query", "feat"), None),
        P("query", None),
        P(),
    )
    out_specs = (P(None, ("query", "feat")), P(), P(("query", "feat")), P(None, ("query", "feat")))
    return jax.shard_map(local, mesh=mesh, in_specs=in_specs, out_specs=out_specs, check_vma=False)
```

```python
import jax
import jax.numpy as jnp
from jax import lax
from jax.experimental import pallas as pl
from jax.experimental.pallas import tpu as pltpu
from jax.sharding import PartitionSpec as P

BINS = 256
LEAVES = 1024
FEATURES = 256
OWN = 1024
WIN = 3 * OWN
BLOCK = 8192
QUERIES = 32
TILE = 128
TILES = WIN // TILE
OWN_TILES = OWN // TILE
STEP = 128
PAIR = 2 * TILE
CHIPS = 16
SIDE = 4
RING = 8
GROUP = 8
EARLY = 4
HI = 8
LO = 32

lasso_penalty = 1.0
ridge_penalty = 1.0
shrinkage = 0.1

F32 = jnp.float32
BF16 = jnp.bfloat16
MESH_ID = pl.DeviceIdType.MESH
VMEM = pl.BlockSpec(memory_space=pltpu.VMEM)
HBM = pl.BlockSpec(memory_space=pltpu.HBM)
SMEM = pl.BlockSpec(memory_space=pltpu.SMEM)


def nt_dot(left, right):
    return lax.dot_general(left, right, (((1,), (1,)), ((), ())), preferred_element_type=F32)


def spread(line):
    return jnp.broadcast_to(line, (TILE, TILE)).T


def in_hbm(array):
    return pltpu.with_memory_space_constraint(array, pltpu.HBM)


def iota(shape, axis):
    return lax.broadcasted_iota(jnp.int32, shape, axis)


def prepare_kernel(
    scores_in, labels_in, lengths_in, owner_in, bins_in, window, rows, table, bins_t, id_col, worth_col,
    labels, lengths, owner, bins, own_scores, from_left, from_right, load_sem, send_sem, recv_sem
):
    feat = lax.axis_index("feat")
    query = lax.axis_index("query")
    left = lax.rem(feat + RING - 1, RING)
    right = lax.rem(feat + 1, RING)

    barrier = pltpu.get_barrier_semaphore()
    for peer in (left, right):
        pl.semaphore_signal(barrier, inc=1, device_id=(query, peer), device_id_type=MESH_ID)
    loads = [
        pltpu.make_async_copy(source, target, load_sem.at[which])
        for which, (source, target) in enumerate((
            (lengths_in, lengths), (labels_in, labels), (owner_in, owner), (bins_in, bins), (scores_in, own_scores)))]
    for load in loads:
        load.start()
    to_right = pltpu.make_async_remote_copy(
        src_ref=scores_in, dst_ref=from_left, send_sem=send_sem.at[0], recv_sem=recv_sem.at[0],
        device_id=(query, right), device_id_type=MESH_ID)
    to_left = pltpu.make_async_remote_copy(
        src_ref=scores_in, dst_ref=from_right, send_sem=send_sem.at[1], recv_sem=recv_sem.at[1],
        device_id=(query, left), device_id_type=MESH_ID)
    pl.semaphore_wait(barrier, 2)
    to_right.start()
    to_left.start()
    for load in loads[:2]:
        load.wait()

    base = (feat * OWN - OWN).astype(F32)
    length_row = jnp.broadcast_to(lengths[...].astype(F32), (QUERIES, QUERIES))
    other, one = iota((QUERIES, QUERIES), 1), iota((QUERIES, QUERIES), 0)
    starts = jnp.sum(jnp.where(other < one, length_row, 0.0), axis=1, keepdims=True)
    ends = jnp.sum(jnp.where(other <= one, length_row, 0.0), axis=1, keepdims=True)
    place = iota((1, WIN), 1).astype(F32) + base
    inside = (place >= starts) & (place < ends)
    passed = jnp.sum(jnp.where(place >= ends, 1.0, 0.0), axis=0, keepdims=True)
    ids = jnp.where(place < 0.0, -1.0, passed)

    def label_part(block):
        return labels[:, pl.ds(pl.multiple_of(block * OWN, OWN), OWN)]

    grades = jnp.concatenate([label_part(left), label_part(feat), label_part(right)], axis=1)
    worth = lax.shift_left(jnp.ones_like(grades), grades).astype(F32)

    at_least = (jnp.broadcast_to(grades, (8, WIN)) > iota((8, WIN), 0)).astype(F32).astype(BF16)
    counts = nt_dot(inside.astype(F32).astype(BF16), at_least)
    spot = iota((1, OWN), 1).astype(F32)
    gain = 1.0 / jnp.log2(2.0 + spot)
    parts = jnp.zeros((QUERIES, OWN), F32)
    for level in range(4):
        parts = parts + jnp.where(spot < counts[:, level:level + 1], gain * float(2 ** level), 0.0)
    ideal = jnp.sum(parts, axis=1, keepdims=True)
    usable = ideal > 0.5
    inverse = jnp.where(usable, 1.0 / jnp.where(usable, ideal, 1.0), 0.0)
    own_inverse = jnp.sum(jnp.where(inside, inverse, 0.0), axis=0, keepdims=True)

    def bound_at(spots, values):
        hit = (spots >= starts) & (spots < ends)
        return jnp.sum(jnp.where(hit, values, 0.0), axis=0, keepdims=True)

    zeros = jnp.zeros((1, TILE), F32)
    first = bound_at(zeros + (base + OWN), starts)
    last = bound_at(zeros + (base + 2 * OWN - 1.0), ends)
    tile_first = base + iota((1, TILE), 1).astype(F32) * TILE
    low = bound_at(jnp.maximum(tile_first, first), starts)
    high = bound_at(jnp.minimum(tile_first + (TILE - 1.0), last - 1.0), ends)
    line = iota((8, TILE), 0)
    bounds = jnp.where(line == 0, low, jnp.where(line == 1, high, jnp.where(line == 2, first, last)))
    table[...] = (bounds - base).astype(jnp.int32)

    rows[...] = jnp.concatenate([ids, worth, own_inverse, own_inverse] * 2, axis=0)
    for tile in range(TILES):
        at = slice(tile * TILE, (tile + 1) * TILE)
        id_col[at, :] = spread(ids[:, at])
        worth_col[at, :] = spread(worth[:, at])

    for load in loads[2:]:
        load.wait()
    pick_t = (iota((FEATURES, FEATURES), 0) == owner[...]).astype(F32)
    pick = pick_t.T.astype(BF16)
    bins_t[...] = nt_dot(pick, bins[...].astype(F32).astype(BF16))

    window[:, OWN:2 * OWN] = own_scores[...]
    to_right.wait()
    to_left.wait()
    window[:, 0:OWN] = from_left[...]
    window[:, 2 * OWN:WIN] = from_right[...]


def pair_kernel(
    table, window_in, rows, id_col, worth_col, out, out_again,
    lines, score_col, up_col, discount_col, counts, discount_row, grads, curvs
):
    window = window_in[...]
    lines[...] = jnp.concatenate([window, jnp.exp(-window), jnp.exp(window), window] * 2, axis=0)
    for tile in range(TILES):
        at = slice(tile * TILE, (tile + 1) * TILE)
        score_col[at, :] = spread(lines[0:1, at])
        up_col[at, :] = spread(lines[1:2, at])
    counts[...] = jnp.zeros_like(counts)

    active = table[2, 0] // PAIR
    stop = (table[3, 0] + PAIR - 1) // PAIR

    def rank_pair(pair, carry):
        begin = pl.multiple_of(pair * PAIR, PAIR)
        score = jnp.broadcast_to(lines[0:1, pl.ds(begin, PAIR)], (8, PAIR))
        ident = jnp.broadcast_to(rows[0:1, pl.ds(begin, PAIR)], (8, PAIR))

        def count(start, steps, beats, total):
            for sub in range(steps):
                spot = pl.multiple_of(start + sub * 8, 8)
                other = score_col[pl.ds(spot, 8), :]
                other_id = id_col[pl.ds(spot, 8), :]
                parts = []
                for half in range(2):
                    lanes = slice(half * TILE, (half + 1) * TILE)
                    hit = (other_id == ident[:, lanes]) & beats(other, score[:, lanes], half, sub)
                    parts.append(total[half] + jnp.where(hit, 1.0, 0.0))
                total = tuple(parts)
            return total

        def ahead(other, own, half, sub):
            return other >= own

        def behind(other, own, half, sub):
            return other > own

        def around(other, own, half, sub):
            if sub * 8 < half * TILE:
                return other >= own
            if sub * 8 >= (half + 1) * TILE:
                return other > own
            earlier = iota((8, TILE), 0) + (sub * 8 - half * TILE) < iota((8, TILE), 1)
            return (other > own) | ((other == own) & earlier)

        empty = jnp.zeros((8, TILE), F32)
        total = count(begin, PAIR // 8, around, (empty, empty))
        total = lax.fori_loop(
            table[0, 2 * pair] // STEP, begin // STEP,
            lambda i, t: count(i * STEP, STEP // 8, ahead, t), total)
        total = lax.fori_loop(
            (begin + PAIR) // STEP, (table[1, 2 * pair + 1] + STEP - 1) // STEP,
            lambda i, t: count(i * STEP, STEP // 8, behind, t), total)
        counts[:, pl.ds(begin, PAIR)] = jnp.concatenate(total, axis=1)
        return carry

    lax.fori_loop(active, stop, rank_pair, 0)

    rank = jnp.broadcast_to(jnp.sum(counts[...], axis=0, keepdims=True), (8, WIN))
    discount = 1.0 / jnp.log2(2.0 + rank)
    discount_row[...] = discount
    for tile in range(TILES):
        at = slice(tile * TILE, (tile + 1) * TILE)
        discount_col[at, :] = spread(discount[0:1, at])

    def own_pair(index, carry):
        pair = index + OWN // PAIR
        begin = pl.multiple_of(pair * PAIR, PAIR)

        def own(ref, line):
            return jnp.broadcast_to(ref[line:line + 1, pl.ds(begin, PAIR)], (8, PAIR))

        up = -own(lines, 2)
        ident = own(rows, 0)
        worth = own(rows, 1)
        discount = discount_row[:, pl.ds(begin, PAIR)]

        def meet(block, sums):
            for sub in range(STEP // 8):
                at = pl.ds(pl.multiple_of(block * STEP + sub * 8, 8), 8)
                other_up, other_id = up_col[at, :], id_col[at, :]
                other_discount, other_worth = discount_col[at, :], worth_col[at, :]
                parts = []
                for half in range(2):
                    lanes = slice(half * TILE, (half + 1) * TILE)
                    odds = up[:, lanes] * other_up
                    win = pltpu.reciprocal(1.0 - odds, approx=True)
                    lose = odds * win
                    gap = jnp.where(other_id == ident[:, lanes], discount[:, lanes] - other_discount, 0.0)
                    rise = worth[:, lanes] - other_worth
                    change = jnp.abs(rise * gap)
                    parts.append(sums[half][0] + change * jnp.where(rise > 0.0, win, lose))
                    parts.append(sums[half][1] + change * (win * lose))
                sums = ((parts[0], parts[1]), (parts[2], parts[3]))
            return sums

        empty = jnp.zeros((8, TILE), F32)
        sums = lax.fori_loop(
            table[0, 2 * pair] // STEP, (table[1, 2 * pair + 1] + STEP - 1) // STEP, meet,
            ((empty, empty), (empty, empty)))
        for half in range(2):
            spot = pl.ds(pl.multiple_of(index * PAIR + half * TILE, TILE), TILE)
            grads[:, spot] = sums[half][0]
            curvs[:, spot] = sums[half][1]
        return carry

    lax.fori_loop(0, OWN // PAIR, own_pair, 0)
    inverse = -rows[2:3, OWN:2 * OWN]
    both = jnp.concatenate([
        inverse * jnp.sum(grads[...], axis=0, keepdims=True),
        inverse * jnp.sum(curvs[...], axis=0, keepdims=True)], axis=0)
    out[...] = both
    out_again[...] = both


def in_pieces(value, pieces):
    found = []
    for unused in range(pieces):
        piece = value.astype(BF16)
        found.append(piece)
        value = value - piece.astype(F32)
    return found


def histogram_kernel(
    lambdas, leaves, bins_t, leaf_out, step_out, hist_out,
    left_side, right_side, weights, pair_sent, pair_got, sent, got,
    leaf_got, leaf_ring, leaf_both, chunk, chunk_got,
    pair_send, pair_recv, send_sem, recv_sem, leaf_send, leaf_recv, ring_send, ring_recv,
    chunk_send, chunk_recv, one_send, one_recv
):
    query = lax.axis_index("query")
    feat = lax.axis_index("feat")
    core = lax.rem(query, 2)
    chip = lax.div(query, 2)
    other_core = 1 - core
    sibling = chip * 2 + other_core
    chip_y, chip_x = lax.div(chip, SIDE), lax.rem(chip, SIDE)

    def steps_to(offset):
        turn = lax.rem(offset + CHIPS - 1, CHIPS)
        return lax.rem(lax.div(turn, SIDE) + 1, SIDE), lax.rem(lax.rem(turn, SIDE) + 1, SIDE)

    def chip_peer(offset):
        down, across = steps_to(offset)
        return lax.rem(chip_y + down, SIDE) * SIDE + lax.rem(chip_x + across, SIDE)

    def chip_source(offset):
        down, across = steps_to(offset)
        return lax.rem(chip_y + SIDE - down, SIDE) * SIDE + lax.rem(chip_x + SIDE - across, SIDE)

    def ring_peer(offset):
        return lax.rem(feat + offset, RING)

    def remote(source, target, send, recv, device):
        return pltpu.make_async_remote_copy(
            src_ref=source, dst_ref=target, send_sem=send, recv_sem=recv, device_id=device, device_id_type=MESH_ID)

    barrier = pltpu.get_barrier_semaphore()
    pl.semaphore_signal(barrier, inc=1, device_id=(sibling, feat), device_id_type=MESH_ID)

    @pl.loop(1, CHIPS)
    def _(offset):
        pl.semaphore_signal(barrier, inc=1, device_id=(chip_peer(offset) * 2 + core, feat), device_id_type=MESH_ID)

    @pl.loop(1, RING)
    def _(offset):
        pl.semaphore_signal(barrier, inc=1, device_id=(query, ring_peer(offset)), device_id_type=MESH_ID)

    grad, curv = lambdas[0:1, :], lambdas[1:2, :]
    leaf = leaves[...]
    leaf_row = lax.shift_right_logical(leaf, 7)
    leaf_lane = jnp.bitwise_and(leaf, 127)
    in_row = iota((8, OWN), 0) == leaf_row
    lane_hot = (iota((TILE, OWN), 0) == leaf_lane).astype(F32).astype(BF16)
    placed = []
    for value in (grad, curv):
        for piece in in_pieces(value, 3):
            placed.append(jnp.where(in_row, piece.astype(F32), 0.0).astype(BF16))
    leaf_sums = nt_dot(jnp.concatenate(placed, axis=0), lane_hot)
    leaf_got[chip, 0:8, :] = leaf_sums[0:8] + leaf_sums[8:16] + leaf_sums[16:24]
    leaf_got[chip, 8:16, :] = leaf_sums[24:32] + leaf_sums[32:40] + leaf_sums[40:48]
    chunk[...] = jnp.zeros_like(chunk)

    stats = in_pieces(grad, 2) + in_pieces(curv, 2) + [jnp.ones((1, OWN), BF16)]
    for which, value in enumerate(stats):
        weights[which] = jnp.broadcast_to(value, (16, OWN))

    low_levels = iota((LO, OWN), 0).astype(F32).astype(BF16)
    high_levels = jnp.bitwise_and(iota((16, OWN), 0), 7).astype(F32).astype(BF16)
    upper = iota((16, OWN), 0) < 8
    zero = jnp.zeros((), BF16)
    unit = jnp.ones((), BF16)

    def one_hots(group, slot):
        block = bins_t[pl.ds(pl.multiple_of(group * GROUP, GROUP), GROUP), :]
        high = jnp.floor(block * (1.0 / LO))
        low = block - high * LO
        for k in range(GROUP):
            spread_low = jnp.broadcast_to(low[k:k + 1].astype(BF16), (LO, OWN))
            right_side[slot, k * LO:(k + 1) * LO, :] = jnp.where(spread_low == low_levels, unit, zero)
        for pair in range(GROUP // 2):
            k = 2 * pair
            both = jnp.where(
                upper, jnp.broadcast_to(high[k:k + 1], (16, OWN)),
                jnp.broadcast_to(high[k + 1:k + 2], (16, OWN))).astype(BF16)
            hot = both == high_levels
            for which in range(5):
                left_side[slot, which * 64 + pair * 16:which * 64 + (pair + 1) * 16, :] = jnp.where(
                    hot, weights[which], zero)

    def sums(slot, target, index):
        full = nt_dot(left_side[slot], right_side[slot])
        lane = iota((HI, TILE), 1)
        for stat, whichs in enumerate(((0, 1), (2, 3), (4,))):
            for half in range(2):
                lanes = slice(half * TILE, (half + 1) * TILE)
                total = None
                for which in whichs:
                    picked = None
                    for j in range(4):
                        k = half * 4 + j
                        piece = full[which * 64 + k * HI:which * 64 + (k + 1) * HI, lanes]
                        picked = piece if j == 0 else jnp.where(lane >= j * LO, piece, picked)
                    total = picked if total is None else total + picked
                target[index, stat * HI:(stat + 1) * HI, lanes] = total

    def chip_at(turn):
        return chip_peer(lax.rem(turn + 1, CHIPS))

    def groups_of(turns):
        peers = [chip_at(turn) for turn in turns]
        for which, peer in enumerate(peers):
            one_hots(peer * 2 + other_core, 2 * which)
            one_hots(peer * 2 + core, 2 * which + 1)
        for which, peer in enumerate(peers):
            sums(2 * which, pair_sent, peer)
            sums(2 * which + 1, sent, peer)

    def pair_copy(turn):
        peer = chip_at(turn)
        return remote(pair_sent.at[peer], pair_got.at[peer], pair_send.at[peer], pair_recv.at[peer], (sibling, feat))

    def plane_copy(offset):
        peer = chip_peer(offset)
        return remote(sent.at[peer], got.at[chip], send_sem.at[peer], recv_sem.at[chip], (peer * 2 + core, feat))

    def plane_arrival(offset):
        peer = chip_source(offset)
        return remote(sent.at[peer], got.at[peer], send_sem.at[peer], recv_sem.at[peer], (peer * 2 + core, feat))

    def join(turn):
        pair_copy(turn).wait_recv()
        peer = chip_at(turn)
        sent[peer] = sent[peer] + pair_got[peer]

    def join_and_send(turn):
        join(turn)
        plane_copy(turn + 1).start()

    @pl.loop(0, EARLY // 2)
    def _(step):
        groups_of((2 * step, 2 * step + 1))

    pl.semaphore_wait(barrier, 1 + CHIPS - 1 + RING - 1)

    def leaf_copy(offset):
        peer = chip_peer(offset)
        return remote(leaf_got.at[chip], leaf_got.at[chip], leaf_send.at[peer], leaf_recv.at[chip], (peer * 2 + core, feat))

    def leaf_arrival(offset):
        peer = chip_source(offset)
        return remote(leaf_got.at[chip], leaf_got.at[peer], leaf_send.at[peer], leaf_recv.at[peer], (peer * 2 + core, feat))

    @pl.loop(1, CHIPS)
    def _(offset):
        leaf_copy(offset).start()

    @pl.loop(0, EARLY)
    def _(turn):
        pair_copy(turn).start()

    groups_of((EARLY, EARLY + 1))
    pair_copy(EARLY).start()
    pair_copy(EARLY + 1).start()

    @pl.loop(0, EARLY)
    def _(turn):
        join_and_send(turn)

    @pl.loop(EARLY // 2 + 1, CHIPS // 2 - 1)
    def _(step):
        groups_of((2 * step, 2 * step + 1))
        pair_copy(2 * step).start()
        pair_copy(2 * step + 1).start()
        join_and_send(2 * step - 2)
        join_and_send(2 * step - 1)

    groups_of((CHIPS - 2,))
    pair_copy(CHIPS - 2).start()
    join_and_send(CHIPS - 4)
    join_and_send(CHIPS - 3)
    groups_of((CHIPS - 1,))
    pair_copy(CHIPS - 1).start()
    join_and_send(CHIPS - 2)
    join(CHIPS - 1)

    @pl.loop(1, CHIPS)
    def _(offset):
        leaf_arrival(offset).wait_recv()

    leaf_ring[feat] = lax.fori_loop(
        0, CHIPS, lambda peer, total: total + leaf_got[peer], jnp.zeros((16, TILE), F32))

    def ring_copy(offset):
        peer = ring_peer(offset)
        return remote(leaf_ring.at[feat], leaf_ring.at[feat], ring_send.at[peer], ring_recv.at[feat], (query, peer))

    def ring_arrival(offset):
        peer = ring_peer(offset)
        return remote(leaf_ring.at[feat], leaf_ring.at[peer], ring_send.at[peer], ring_recv.at[peer], (query, peer))

    @pl.loop(1, RING)
    def _(offset):
        ring_copy(offset).start()

    def add_hist(offset, total):
        plane_arrival(offset).wait_recv()
        return total + got[chip_source(offset)]

    summed = lax.fori_loop(1, CHIPS, add_hist, sent[chip])

    lane_block = lax.shift_right_logical(iota((GROUP, TILE), 1), 5)
    holder = iota((GROUP, TILE), 0)
    for stat in range(3):
        for half in range(2):
            moved = jnp.zeros((GROUP, TILE), F32)
            for r in range(4):
                row = stat * HI + half * 4 + r
                line = jnp.where(
                    holder < 4, jnp.broadcast_to(summed[row:row + 1, 0:TILE], (GROUP, TILE)),
                    jnp.broadcast_to(summed[row:row + 1, TILE:2 * TILE], (GROUP, TILE)))
                for kk in range(4):
                    shift = (r - kk) % 4 * LO
                    turned = pltpu.roll(line, shift, 1) if shift else line
                    moved = jnp.where((jnp.bitwise_and(holder, 3) == kk) & (lane_block == r), turned, moved)
            line = stat * 2 + half
            for k in range(GROUP):
                chunk[k, line:line + 1, :] = moved[k:k + 1, :]

    def chunk_copy(offset):
        peer = ring_peer(offset)
        return remote(chunk.at[peer], chunk_got.at[feat], chunk_send.at[peer], chunk_recv.at[feat], (query, peer))

    def chunk_arrival(offset):
        peer = ring_peer(offset)
        return remote(chunk.at[peer], chunk_got.at[peer], chunk_send.at[peer], chunk_recv.at[peer], (query, peer))

    @pl.loop(1, RING)
    def _(offset):
        chunk_copy(offset).start()

    @pl.loop(1, RING)
    def _(offset):
        ring_arrival(offset).wait_recv()

    core_total = leaf_ring[0]
    for peer in range(1, RING):
        core_total = core_total + leaf_ring[peer]
    leaf_both[core] = core_total
    leaf_back = remote(leaf_both.at[core], leaf_both.at[core], one_send.at[0], one_recv.at[0], (sibling, feat))
    leaf_back.start()

    leaf_back_here = remote(
        leaf_both.at[core], leaf_both.at[other_core], one_send.at[0], one_recv.at[0], (sibling, feat))
    leaf_back_here.wait_recv()
    totals = leaf_both[0] + leaf_both[1]
    total_grad, total_curv = totals[0:8], totals[8:16]
    shrunk = jnp.maximum(jnp.abs(total_grad) - lasso_penalty, 0.0) / (total_curv + ridge_penalty)
    values = jnp.where(total_grad > 0.0, -shrunk, shrunk)
    leaf_out[...] = values
    found = jnp.zeros((8, OWN), F32)
    for piece in in_pieces(values, 3):
        found = found + jnp.dot(piece, lane_hot, preferred_element_type=F32)
    step_out[...] = shrinkage * jnp.sum(jnp.where(in_row, found, 0.0), axis=0, keepdims=True)

    def add_chunk(offset, total):
        chunk_arrival(offset).wait_recv()
        return total + chunk_got[ring_peer(offset)]

    hist_out[...] = lax.fori_loop(1, RING, add_chunk, chunk[feat])

    leaf_back.wait_send()
    pair_copy(CHIPS - 1).wait_send()

    @pl.loop(1, CHIPS)
    def _(offset):
        pair_copy(offset - 1).wait_send()
        plane_copy(offset).wait_send()
        leaf_copy(offset).wait_send()

    @pl.loop(1, RING)
    def _(offset):
        ring_copy(offset).wait_send()
        chunk_copy(offset).wait_send()


def finish_kernel(leaf_in, step_in, hist_in, leaf_out, step_out, hist_out, hist, sem):
    for stat in range(3):
        for half in range(2):
            line = stat * 2 + half
            hist[stat:stat + 1, half * TILE:(half + 1) * TILE] = hist_in[line:line + 1, :]
    copies = [
        pltpu.make_async_copy(source, target, sem.at[which])
        for which, (source, target) in enumerate(((leaf_in, leaf_out), (step_in, step_out), (hist, hist_out)))]
    for copy in copies:
        copy.start()
    for copy in copies:
        copy.wait()


def local(scores, labels, leaves, bins, lengths, owner):
    shape = jax.ShapeDtypeStruct
    dma = pltpu.SemaphoreType.DMA
    column = pltpu.VMEM((WIN, TILE), F32)
    window, rows, table, bins_t, id_col, worth_col = pl.pallas_call(
        prepare_kernel,
        out_shape=(
            shape((1, WIN), F32),
            shape((8, WIN), F32),
            shape((8, TILE), jnp.int32),
            shape((FEATURES, OWN), F32),
            shape((WIN, TILE), F32),
            shape((WIN, TILE), F32),
        ),
        in_specs=[HBM] * 5,
        out_specs=(VMEM,) * 6,
        scratch_shapes=[
            pltpu.VMEM((1, BLOCK), jnp.int32), pltpu.VMEM((1, QUERIES), jnp.int32),
            pltpu.VMEM((1, FEATURES), jnp.int32), pltpu.VMEM((OWN, FEATURES), jnp.int32),
            pltpu.VMEM((1, OWN), F32), pltpu.VMEM((1, OWN), F32), pltpu.VMEM((1, OWN), F32),
            dma((5,)), dma((2,)), dma((2,))],
        compiler_params=pltpu.CompilerParams(
            collective_id=1, has_side_effects=True, vmem_limit_bytes=32 * 2**20),
        name="prepare",
    )(in_hbm(scores.reshape(1, OWN)), in_hbm(labels.reshape(1, BLOCK)), in_hbm(lengths), in_hbm(owner.reshape(1, FEATURES)), in_hbm(bins))
    lambdas, lambdas_again = pl.pallas_call(
        pair_kernel,
        out_shape=(shape((2, OWN), F32), shape((2, OWN), F32)),
        in_specs=[SMEM] + [VMEM] * 4,
        out_specs=(VMEM, VMEM),
        scratch_shapes=[pltpu.VMEM((8, WIN), F32)] + [column] * 3 + [pltpu.VMEM((8, WIN), F32)] * 2 + [pltpu.VMEM((8, OWN), F32)] * 2,
        compiler_params=pltpu.CompilerParams(vmem_limit_bytes=32 * 2**20),
        name="pairs",
    )(table, window, rows, id_col, worth_col)
    part = pltpu.VMEM((CHIPS, 3 * HI, GROUP * LO), F32)
    leaf_values, score_step, histograms = pl.pallas_call(
        histogram_kernel,
        out_shape=(
            shape((8, TILE), F32),
            shape((1, OWN), F32),
            shape((8, TILE), F32),
        ),
        in_specs=[VMEM] * 3,
        out_specs=(VMEM, VMEM, VMEM),
        scratch_shapes=[
            pltpu.VMEM((4, 5 * GROUP * HI, OWN), BF16),
            pltpu.VMEM((4, GROUP * LO, OWN), BF16),
            pltpu.VMEM((5, 16, OWN), BF16),
            part, part, part, part,
            pltpu.VMEM((CHIPS, 16, TILE), F32),
            pltpu.VMEM((RING, 16, TILE), F32),
            pltpu.VMEM((2, 16, TILE), F32),
            pltpu.VMEM((RING, 8, TILE), F32),
            pltpu.VMEM((RING, 8, TILE), F32),
            dma((CHIPS,)), dma((CHIPS,)), dma((CHIPS,)), dma((CHIPS,)), dma((CHIPS,)), dma((CHIPS,)),
            dma((RING,)), dma((RING,)), dma((RING,)), dma((RING,)), dma((1,)), dma((1,)),
        ],
        compiler_params=pltpu.CompilerParams(
            collective_id=2, has_side_effects=True, vmem_limit_bytes=32 * 2**20),
        name="histograms",
    )(lambdas_again, leaves.reshape(1, OWN), bins_t)
    leaf_values, score_step, histograms = pl.pallas_call(
        finish_kernel,
        out_shape=(
            shape((8, TILE), F32),
            shape((1, OWN), F32),
            shape((3, BINS), F32),
        ),
        in_specs=[VMEM] * 3,
        out_specs=(HBM, HBM, HBM),
        scratch_shapes=[pltpu.VMEM((3, BINS), F32), dma((3,))],
        compiler_params=pltpu.CompilerParams(vmem_limit_bytes=2**21),
        name="finish",
    )(leaf_values, score_step, histograms)
    return lambdas, leaf_values.reshape(LEAVES), score_step.reshape(OWN), histograms


def solution(mesh):
    in_specs = (
        P(("query", "feat")),
        P("query"),
        P(("query", "feat")),
        P(("query", "feat"), None),
        P("query", None),
        P(),
    )
    out_specs = (P(None, ("query", "feat")), P(), P(("query", "feat")), P(None, ("query", "feat")))
    return jax.shard_map(local, mesh=mesh, in_specs=in_specs, out_specs=out_specs, check_vma=False)
```

```python
import functools

import jax
import jax.numpy as jnp
from jax import lax
from jax.experimental import pallas as pl
from jax.experimental.pallas import tpu as pltpu
from jax.sharding import PartitionSpec as P

BINS = 256
LEAVES = 1024
FEATURES = 256
OWN = 1024
WIN = 3 * OWN
BLOCK = 8192
QUERIES = 32
TILE = 128
TILES = WIN // TILE
OWN_TILES = OWN // TILE
STEP = 128
PAIR = 2 * TILE
CHIPS = 16
SIDE = 4
RING = 8
GROUP = 8
EARLY = 4
HI = 8
LO = 32

lasso_penalty = 1.0
ridge_penalty = 1.0
shrinkage = 0.1

F32 = jnp.float32
BF16 = jnp.bfloat16
MESH_ID = pl.DeviceIdType.MESH
VMEM = pl.BlockSpec(memory_space=pltpu.VMEM)
HBM = pl.BlockSpec(memory_space=pltpu.HBM)
SMEM = pl.BlockSpec(memory_space=pltpu.SMEM)


def nt_dot(left, right):
    return lax.dot_general(left, right, (((1,), (1,)), ((), ())), preferred_element_type=F32)


def spread(line):
    return jnp.broadcast_to(line, (TILE, TILE)).T


def in_hbm(array):
    return pltpu.with_memory_space_constraint(array, pltpu.HBM)


def iota(shape, axis):
    return lax.broadcasted_iota(jnp.int32, shape, axis)


def prepare_kernel(
    scores_in, labels_in, lengths_in, owner_in, bins_in, window, rows, table, bins_t, id_col, worth_col,
    labels, lengths, owner, bins, own_scores, from_left, from_right, load_sem, send_sem, recv_sem
):
    feat = lax.axis_index("feat")
    query = lax.axis_index("query")
    left = lax.rem(feat + RING - 1, RING)
    right = lax.rem(feat + 1, RING)

    barrier = pltpu.get_barrier_semaphore()
    for peer in (left, right):
        pl.semaphore_signal(barrier, inc=1, device_id=(query, peer), device_id_type=MESH_ID)
    loads = [
        pltpu.make_async_copy(source, target, load_sem.at[which])
        for which, (source, target) in enumerate((
            (lengths_in, lengths), (labels_in, labels), (owner_in, owner), (bins_in, bins), (scores_in, own_scores)))]
    for load in loads:
        load.start()
    to_right = pltpu.make_async_remote_copy(
        src_ref=scores_in, dst_ref=from_left, send_sem=send_sem.at[0], recv_sem=recv_sem.at[0],
        device_id=(query, right), device_id_type=MESH_ID)
    to_left = pltpu.make_async_remote_copy(
        src_ref=scores_in, dst_ref=from_right, send_sem=send_sem.at[1], recv_sem=recv_sem.at[1],
        device_id=(query, left), device_id_type=MESH_ID)
    pl.semaphore_wait(barrier, 2)
    to_right.start()
    to_left.start()
    for load in loads[:2]:
        load.wait()

    base = (feat * OWN - OWN).astype(F32)
    length_row = jnp.broadcast_to(lengths[...].astype(F32), (QUERIES, QUERIES))
    other, one = iota((QUERIES, QUERIES), 1), iota((QUERIES, QUERIES), 0)
    starts = jnp.sum(jnp.where(other < one, length_row, 0.0), axis=1, keepdims=True)
    ends = jnp.sum(jnp.where(other <= one, length_row, 0.0), axis=1, keepdims=True)
    place = iota((1, WIN), 1).astype(F32) + base
    inside = (place >= starts) & (place < ends)
    passed = jnp.sum(jnp.where(place >= ends, 1.0, 0.0), axis=0, keepdims=True)
    ids = jnp.where(place < 0.0, -1.0, passed)

    def label_part(block):
        return labels[:, pl.ds(pl.multiple_of(block * OWN, OWN), OWN)]

    grades = jnp.concatenate([label_part(left), label_part(feat), label_part(right)], axis=1)
    worth = lax.shift_left(jnp.ones_like(grades), grades).astype(F32)

    at_least = (jnp.broadcast_to(grades, (8, WIN)) > iota((8, WIN), 0)).astype(F32).astype(BF16)
    counts = nt_dot(inside.astype(F32).astype(BF16), at_least)
    spot = iota((1, OWN), 1).astype(F32)
    gain = 1.0 / jnp.log2(2.0 + spot)
    parts = jnp.zeros((QUERIES, OWN), F32)
    for level in range(4):
        parts = parts + jnp.where(spot < counts[:, level:level + 1], gain * float(2 ** level), 0.0)
    ideal = jnp.sum(parts, axis=1, keepdims=True)
    usable = ideal > 0.5
    inverse = jnp.where(usable, 1.0 / jnp.where(usable, ideal, 1.0), 0.0)
    own_inverse = jnp.sum(jnp.where(inside, inverse, 0.0), axis=0, keepdims=True)

    def bound_at(spots, values):
        hit = (spots >= starts) & (spots < ends)
        return jnp.sum(jnp.where(hit, values, 0.0), axis=0, keepdims=True)

    zeros = jnp.zeros((1, TILE), F32)
    first = bound_at(zeros + (base + OWN), starts)
    last = bound_at(zeros + (base + 2 * OWN - 1.0), ends)
    tile_first = base + iota((1, TILE), 1).astype(F32) * TILE
    low = bound_at(jnp.maximum(tile_first, first), starts)
    high = bound_at(jnp.minimum(tile_first + (TILE - 1.0), last - 1.0), ends)
    line = iota((8, TILE), 0)
    bounds = jnp.where(line == 0, low, jnp.where(line == 1, high, jnp.where(line == 2, first, last)))
    table[...] = (bounds - base).astype(jnp.int32)

    rows[...] = jnp.concatenate([ids, worth, own_inverse, own_inverse] * 2, axis=0)
    for tile in range(TILES):
        at = slice(tile * TILE, (tile + 1) * TILE)
        id_col[at, :] = spread(ids[:, at])
        worth_col[at, :] = spread(worth[:, at])

    for load in loads[2:]:
        load.wait()
    pick_t = (iota((FEATURES, FEATURES), 0) == owner[...]).astype(F32)
    pick = pick_t.T.astype(BF16)
    bins_t[...] = nt_dot(pick, bins[...].astype(F32).astype(BF16))

    window[:, OWN:2 * OWN] = own_scores[...]
    to_right.wait()
    to_left.wait()
    window[:, 0:OWN] = from_left[...]
    window[:, 2 * OWN:WIN] = from_right[...]


def pair_kernel(
    table, window_in, rows, id_col, worth_col, out, out_again,
    lines, score_col, up_col, discount_col, counts, discount_row, grads, curvs
):
    window = window_in[...]
    lines[...] = jnp.concatenate([window, jnp.exp(-window), jnp.exp(window), window] * 2, axis=0)
    for tile in range(TILES):
        at = slice(tile * TILE, (tile + 1) * TILE)
        score_col[at, :] = spread(lines[0:1, at])
        up_col[at, :] = spread(lines[1:2, at])
    counts[...] = jnp.zeros_like(counts)

    def blocks_of(pair):
        low, high = table[0, 2 * pair], table[1, 2 * pair + 1]
        alone = (low == table[0, 2 * pair + 1]) & (high == table[1, 2 * pair])
        return low // STEP, (high + STEP - 1) // STEP, (low + STEP - 1) // STEP, high // STEP, alone

    active = table[2, 0] // PAIR
    stop = (table[3, 0] + PAIR - 1) // PAIR

    def rank_pair(pair, carry):
        begin = pl.multiple_of(pair * PAIR, PAIR)
        score = jnp.broadcast_to(lines[0:1, pl.ds(begin, PAIR)], (8, PAIR))
        ident = jnp.broadcast_to(rows[0:1, pl.ds(begin, PAIR)], (8, PAIR))

        def count(start, steps, beats, total, masked=True):
            for sub in range(steps):
                spot = pl.multiple_of(start + sub * 8, 8)
                other = score_col[pl.ds(spot, 8), :]
                other_id = id_col[pl.ds(spot, 8), :] if masked else None
                parts = []
                for half in range(2):
                    lanes = slice(half * TILE, (half + 1) * TILE)
                    hit = beats(other, score[:, lanes], half, sub)
                    if masked:
                        hit = hit & (other_id == ident[:, lanes])
                    parts.append(total[half] + jnp.where(hit, 1.0, 0.0))
                total = tuple(parts)
            return total

        def ahead(other, own, half, sub):
            return other >= own

        def behind(other, own, half, sub):
            return other > own

        def around(other, own, half, sub):
            if sub * 8 < half * TILE:
                return other >= own
            if sub * 8 >= (half + 1) * TILE:
                return other > own
            earlier = iota((8, TILE), 0) + (sub * 8 - half * TILE) < iota((8, TILE), 1)
            return (other > own) | ((other == own) & earlier)

        empty = jnp.zeros((8, TILE), F32)
        total = count(begin, PAIR // 8, around, (empty, empty))
        def run(first, stop, beats, masked, total):
            return lax.fori_loop(
                first, stop, lambda i, t: count(i * STEP, STEP // 8, beats, t, masked), total)

        low, high, inner_low, inner_high, alone = blocks_of(pair)
        here, after = begin // STEP, (begin + PAIR) // STEP
        inner_low = jnp.where(alone, jnp.minimum(inner_low, here), here)
        inner_high = jnp.where(alone, jnp.maximum(inner_high, after), after)
        total = run(low, inner_low, ahead, True, total)
        total = run(inner_low, here, ahead, False, total)
        total = run(after, inner_high, behind, False, total)
        total = run(inner_high, high, behind, True, total)
        counts[:, pl.ds(begin, PAIR)] = jnp.concatenate(total, axis=1)
        return carry

    lax.fori_loop(active, stop, rank_pair, 0)

    rank = jnp.broadcast_to(jnp.sum(counts[...], axis=0, keepdims=True), (8, WIN))
    discount = 1.0 / jnp.log2(2.0 + rank)
    discount_row[...] = discount
    for tile in range(TILES):
        at = slice(tile * TILE, (tile + 1) * TILE)
        discount_col[at, :] = spread(discount[0:1, at])

    def own_pair(index, carry):
        pair = index + OWN // PAIR
        begin = pl.multiple_of(pair * PAIR, PAIR)

        def own(ref, line):
            return jnp.broadcast_to(ref[line:line + 1, pl.ds(begin, PAIR)], (8, PAIR))

        up = -own(lines, 2)
        ident = own(rows, 0)
        worth = own(rows, 1)
        discount = discount_row[:, pl.ds(begin, PAIR)]

        def meet(masked, block, sums):
            for sub in range(STEP // 8):
                at = pl.ds(pl.multiple_of(block * STEP + sub * 8, 8), 8)
                other_up, other_id = up_col[at, :], id_col[at, :]
                other_discount, other_worth = discount_col[at, :], worth_col[at, :]
                parts = []
                for half in range(2):
                    lanes = slice(half * TILE, (half + 1) * TILE)
                    odds = up[:, lanes] * other_up
                    win = pltpu.reciprocal(1.0 - odds, approx=True)
                    lose = odds * win
                    gap = discount[:, lanes] - other_discount
                    if masked:
                        gap = jnp.where(other_id == ident[:, lanes], gap, 0.0)
                    rise = worth[:, lanes] - other_worth
                    change = jnp.abs(rise * gap)
                    parts.append(sums[half][0] + change * jnp.where(rise > 0.0, win, lose))
                    parts.append(sums[half][1] + change * (win * lose))
                sums = ((parts[0], parts[1]), (parts[2], parts[3]))
            return sums

        empty = jnp.zeros((8, TILE), F32)
        low, high, inner_low, inner_high, alone = blocks_of(pair)
        inner_low = jnp.where(alone, inner_low, high)
        inner_high = jnp.where(alone, inner_high, high)
        sums = ((empty, empty), (empty, empty))
        for first, stop, masked in ((low, inner_low, True), (inner_low, inner_high, False), (inner_high, high, True)):
            sums = lax.fori_loop(first, stop, functools.partial(meet, masked), sums)
        for half in range(2):
            spot = pl.ds(pl.multiple_of(index * PAIR + half * TILE, TILE), TILE)
            grads[:, spot] = sums[half][0]
            curvs[:, spot] = sums[half][1]
        return carry

    lax.fori_loop(0, OWN // PAIR, own_pair, 0)
    inverse = -rows[2:3, OWN:2 * OWN]
    both = jnp.concatenate([
        inverse * jnp.sum(grads[...], axis=0, keepdims=True),
        inverse * jnp.sum(curvs[...], axis=0, keepdims=True)], axis=0)
    out[...] = both
    out_again[...] = both


def in_pieces(value, pieces):
    found = []
    for unused in range(pieces):
        piece = value.astype(BF16)
        found.append(piece)
        value = value - piece.astype(F32)
    return found


def histogram_kernel(
    lambdas, leaves, bins_t, leaf_out, step_out, hist_out,
    left_side, right_side, weights, pair_sent, pair_got, sent, got,
    leaf_got, leaf_ring, leaf_both, chunk, chunk_got,
    pair_send, pair_recv, send_sem, recv_sem, leaf_send, leaf_recv, ring_send, ring_recv,
    chunk_send, chunk_recv, one_send, one_recv
):
    query = lax.axis_index("query")
    feat = lax.axis_index("feat")
    core = lax.rem(query, 2)
    chip = lax.div(query, 2)
    other_core = 1 - core
    sibling = chip * 2 + other_core
    chip_y, chip_x = lax.div(chip, SIDE), lax.rem(chip, SIDE)

    def steps_to(offset):
        turn = lax.rem(offset + CHIPS - 1, CHIPS)
        return lax.rem(lax.div(turn, SIDE) + 1, SIDE), lax.rem(lax.rem(turn, SIDE) + 1, SIDE)

    def chip_peer(offset):
        down, across = steps_to(offset)
        return lax.rem(chip_y + down, SIDE) * SIDE + lax.rem(chip_x + across, SIDE)

    def chip_source(offset):
        down, across = steps_to(offset)
        return lax.rem(chip_y + SIDE - down, SIDE) * SIDE + lax.rem(chip_x + SIDE - across, SIDE)

    def ring_peer(offset):
        return lax.rem(feat + offset, RING)

    def remote(source, target, send, recv, device):
        return pltpu.make_async_remote_copy(
            src_ref=source, dst_ref=target, send_sem=send, recv_sem=recv, device_id=device, device_id_type=MESH_ID)

    barrier = pltpu.get_barrier_semaphore()
    pl.semaphore_signal(barrier, inc=1, device_id=(sibling, feat), device_id_type=MESH_ID)

    @pl.loop(1, CHIPS)
    def _(offset):
        pl.semaphore_signal(barrier, inc=1, device_id=(chip_peer(offset) * 2 + core, feat), device_id_type=MESH_ID)

    @pl.loop(1, RING)
    def _(offset):
        pl.semaphore_signal(barrier, inc=1, device_id=(query, ring_peer(offset)), device_id_type=MESH_ID)

    grad, curv = lambdas[0:1, :], lambdas[1:2, :]
    leaf = leaves[...]
    leaf_row = lax.shift_right_logical(leaf, 7)
    leaf_lane = jnp.bitwise_and(leaf, 127)
    in_row = iota((8, OWN), 0) == leaf_row
    lane_hot = (iota((TILE, OWN), 0) == leaf_lane).astype(F32).astype(BF16)
    placed = []
    for value in (grad, curv):
        for piece in in_pieces(value, 3):
            placed.append(jnp.where(in_row, piece.astype(F32), 0.0).astype(BF16))
    leaf_sums = nt_dot(jnp.concatenate(placed, axis=0), lane_hot)
    leaf_got[chip, 0:8, :] = leaf_sums[0:8] + leaf_sums[8:16] + leaf_sums[16:24]
    leaf_got[chip, 8:16, :] = leaf_sums[24:32] + leaf_sums[32:40] + leaf_sums[40:48]
    chunk[...] = jnp.zeros_like(chunk)

    stats = in_pieces(grad, 2) + in_pieces(curv, 2) + [jnp.ones((1, OWN), BF16)]
    for which, value in enumerate(stats):
        weights[which] = jnp.broadcast_to(value, (16, OWN))

    low_levels = iota((LO, OWN), 0).astype(F32).astype(BF16)
    high_levels = jnp.bitwise_and(iota((16, OWN), 0), 7).astype(F32).astype(BF16)
    upper = iota((16, OWN), 0) < 8
    zero = jnp.zeros((), BF16)
    unit = jnp.ones((), BF16)

    def one_hots(group, slot):
        block = bins_t[pl.ds(pl.multiple_of(group * GROUP, GROUP), GROUP), :]
        high = jnp.floor(block * (1.0 / LO))
        low = block - high * LO
        for k in range(GROUP):
            spread_low = jnp.broadcast_to(low[k:k + 1].astype(BF16), (LO, OWN))
            right_side[slot, k * LO:(k + 1) * LO, :] = jnp.where(spread_low == low_levels, unit, zero)
        for pair in range(GROUP // 2):
            k = 2 * pair
            both = jnp.where(
                upper, jnp.broadcast_to(high[k:k + 1], (16, OWN)),
                jnp.broadcast_to(high[k + 1:k + 2], (16, OWN))).astype(BF16)
            hot = both == high_levels
            for which in range(5):
                left_side[slot, which * 64 + pair * 16:which * 64 + (pair + 1) * 16, :] = jnp.where(
                    hot, weights[which], zero)

    def sums(slot, target, index):
        full = nt_dot(left_side[slot], right_side[slot])
        lane = iota((HI, TILE), 1)
        for stat, whichs in enumerate(((0, 1), (2, 3), (4,))):
            for half in range(2):
                lanes = slice(half * TILE, (half + 1) * TILE)
                total = None
                for which in whichs:
                    picked = None
                    for j in range(4):
                        k = half * 4 + j
                        piece = full[which * 64 + k * HI:which * 64 + (k + 1) * HI, lanes]
                        picked = piece if j == 0 else jnp.where(lane >= j * LO, piece, picked)
                    total = picked if total is None else total + picked
                target[index, stat * HI:(stat + 1) * HI, lanes] = total

    def chip_at(turn):
        return chip_peer(lax.rem(turn + 1, CHIPS))

    def groups_of(turns):
        peers = [chip_at(turn) for turn in turns]
        for which, peer in enumerate(peers):
            one_hots(peer * 2 + other_core, 2 * which)
            one_hots(peer * 2 + core, 2 * which + 1)
        for which, peer in enumerate(peers):
            sums(2 * which, pair_sent, peer)
            sums(2 * which + 1, sent, peer)

    def pair_copy(turn):
        peer = chip_at(turn)
        return remote(pair_sent.at[peer], pair_got.at[peer], pair_send.at[peer], pair_recv.at[peer], (sibling, feat))

    def plane_copy(offset):
        peer = chip_peer(offset)
        return remote(sent.at[peer], got.at[chip], send_sem.at[peer], recv_sem.at[chip], (peer * 2 + core, feat))

    def plane_arrival(offset):
        peer = chip_source(offset)
        return remote(sent.at[peer], got.at[peer], send_sem.at[peer], recv_sem.at[peer], (peer * 2 + core, feat))

    def join(turn):
        pair_copy(turn).wait_recv()
        peer = chip_at(turn)
        sent[peer] = sent[peer] + pair_got[peer]

    def join_and_send(turn):
        join(turn)
        plane_copy(turn + 1).start()

    @pl.loop(0, EARLY // 2)
    def _(step):
        groups_of((2 * step, 2 * step + 1))

    pl.semaphore_wait(barrier, 1 + CHIPS - 1 + RING - 1)

    def leaf_copy(offset):
        peer = chip_peer(offset)
        return remote(leaf_got.at[chip], leaf_got.at[chip], leaf_send.at[peer], leaf_recv.at[chip], (peer * 2 + core, feat))

    def leaf_arrival(offset):
        peer = chip_source(offset)
        return remote(leaf_got.at[chip], leaf_got.at[peer], leaf_send.at[peer], leaf_recv.at[peer], (peer * 2 + core, feat))

    @pl.loop(1, CHIPS)
    def _(offset):
        leaf_copy(offset).start()

    @pl.loop(0, EARLY)
    def _(turn):
        pair_copy(turn).start()

    groups_of((EARLY, EARLY + 1))
    pair_copy(EARLY).start()
    pair_copy(EARLY + 1).start()

    @pl.loop(0, EARLY)
    def _(turn):
        join_and_send(turn)

    @pl.loop(EARLY // 2 + 1, CHIPS // 2 - 1)
    def _(step):
        groups_of((2 * step, 2 * step + 1))
        pair_copy(2 * step).start()
        pair_copy(2 * step + 1).start()
        join_and_send(2 * step - 2)
        join_and_send(2 * step - 1)

    groups_of((CHIPS - 2,))
    pair_copy(CHIPS - 2).start()
    join_and_send(CHIPS - 4)
    join_and_send(CHIPS - 3)
    groups_of((CHIPS - 1,))
    pair_copy(CHIPS - 1).start()
    @pl.loop(1, CHIPS)
    def _(offset):
        leaf_arrival(offset).wait_recv()

    leaf_ring[feat] = lax.fori_loop(
        0, CHIPS, lambda peer, total: total + leaf_got[peer], jnp.zeros((16, TILE), F32))

    def ring_copy(offset):
        peer = ring_peer(offset)
        return remote(leaf_ring.at[feat], leaf_ring.at[feat], ring_send.at[peer], ring_recv.at[feat], (query, peer))

    def ring_arrival(offset):
        peer = ring_peer(offset)
        return remote(leaf_ring.at[feat], leaf_ring.at[peer], ring_send.at[peer], ring_recv.at[peer], (query, peer))

    @pl.loop(1, RING)
    def _(offset):
        ring_copy(offset).start()

    join_and_send(CHIPS - 2)
    join(CHIPS - 1)

    def add_hist(offset, total):
        plane_arrival(offset).wait_recv()
        return total + got[chip_source(offset)]

    summed = lax.fori_loop(1, CHIPS, add_hist, sent[chip])

    lane_block = lax.shift_right_logical(iota((GROUP, TILE), 1), 5)
    holder = iota((GROUP, TILE), 0)
    for stat in range(3):
        for half in range(2):
            moved = jnp.zeros((GROUP, TILE), F32)
            for r in range(4):
                row = stat * HI + half * 4 + r
                line = jnp.where(
                    holder < 4, jnp.broadcast_to(summed[row:row + 1, 0:TILE], (GROUP, TILE)),
                    jnp.broadcast_to(summed[row:row + 1, TILE:2 * TILE], (GROUP, TILE)))
                for kk in range(4):
                    shift = (r - kk) % 4 * LO
                    turned = pltpu.roll(line, shift, 1) if shift else line
                    moved = jnp.where((jnp.bitwise_and(holder, 3) == kk) & (lane_block == r), turned, moved)
            line = stat * 2 + half
            for k in range(GROUP):
                chunk[k, line:line + 1, :] = moved[k:k + 1, :]

    def chunk_copy(offset):
        peer = ring_peer(offset)
        return remote(chunk.at[peer], chunk_got.at[feat], chunk_send.at[peer], chunk_recv.at[feat], (query, peer))

    def chunk_arrival(offset):
        peer = ring_peer(offset)
        return remote(chunk.at[peer], chunk_got.at[peer], chunk_send.at[peer], chunk_recv.at[peer], (query, peer))

    @pl.loop(1, RING)
    def _(offset):
        chunk_copy(offset).start()

    @pl.loop(1, RING)
    def _(offset):
        ring_arrival(offset).wait_recv()

    core_total = leaf_ring[0]
    for peer in range(1, RING):
        core_total = core_total + leaf_ring[peer]
    leaf_both[core] = core_total
    leaf_back = remote(leaf_both.at[core], leaf_both.at[core], one_send.at[0], one_recv.at[0], (sibling, feat))
    leaf_back.start()

    leaf_back_here = remote(
        leaf_both.at[core], leaf_both.at[other_core], one_send.at[0], one_recv.at[0], (sibling, feat))
    leaf_back_here.wait_recv()
    totals = leaf_both[0] + leaf_both[1]
    total_grad, total_curv = totals[0:8], totals[8:16]
    shrunk = jnp.maximum(jnp.abs(total_grad) - lasso_penalty, 0.0) / (total_curv + ridge_penalty)
    values = jnp.where(total_grad > 0.0, -shrunk, shrunk)
    leaf_out[...] = values
    found = jnp.zeros((8, OWN), F32)
    for piece in in_pieces(values, 3):
        found = found + jnp.dot(piece, lane_hot, preferred_element_type=F32)
    step_out[...] = shrinkage * jnp.sum(jnp.where(in_row, found, 0.0), axis=0, keepdims=True)

    def add_chunk(offset, total):
        chunk_arrival(offset).wait_recv()
        return total + chunk_got[ring_peer(offset)]

    hist_out[...] = lax.fori_loop(1, RING, add_chunk, chunk[feat])

    leaf_back.wait_send()
    pair_copy(CHIPS - 1).wait_send()

    @pl.loop(1, CHIPS)
    def _(offset):
        pair_copy(offset - 1).wait_send()
        plane_copy(offset).wait_send()
        leaf_copy(offset).wait_send()

    @pl.loop(1, RING)
    def _(offset):
        ring_copy(offset).wait_send()
        chunk_copy(offset).wait_send()


def finish_kernel(leaf_in, step_in, hist_in, leaf_out, step_out, hist_out, hist, sem):
    for stat in range(3):
        for half in range(2):
            line = stat * 2 + half
            hist[stat:stat + 1, half * TILE:(half + 1) * TILE] = hist_in[line:line + 1, :]
    copies = [
        pltpu.make_async_copy(source, target, sem.at[which])
        for which, (source, target) in enumerate(((leaf_in, leaf_out), (step_in, step_out), (hist, hist_out)))]
    for copy in copies:
        copy.start()
    for copy in copies:
        copy.wait()


def local(scores, labels, leaves, bins, lengths, owner):
    shape = jax.ShapeDtypeStruct
    dma = pltpu.SemaphoreType.DMA
    column = pltpu.VMEM((WIN, TILE), F32)
    window, rows, table, bins_t, id_col, worth_col = pl.pallas_call(
        prepare_kernel,
        out_shape=(
            shape((1, WIN), F32),
            shape((8, WIN), F32),
            shape((8, TILE), jnp.int32),
            shape((FEATURES, OWN), F32),
            shape((WIN, TILE), F32),
            shape((WIN, TILE), F32),
        ),
        in_specs=[HBM] * 5,
        out_specs=(VMEM,) * 6,
        scratch_shapes=[
            pltpu.VMEM((1, BLOCK), jnp.int32), pltpu.VMEM((1, QUERIES), jnp.int32),
            pltpu.VMEM((1, FEATURES), jnp.int32), pltpu.VMEM((OWN, FEATURES), jnp.int32),
            pltpu.VMEM((1, OWN), F32), pltpu.VMEM((1, OWN), F32), pltpu.VMEM((1, OWN), F32),
            dma((5,)), dma((2,)), dma((2,))],
        compiler_params=pltpu.CompilerParams(
            collective_id=1, has_side_effects=True, vmem_limit_bytes=32 * 2**20),
        name="prepare",
    )(in_hbm(scores.reshape(1, OWN)), in_hbm(labels.reshape(1, BLOCK)), in_hbm(lengths), in_hbm(owner.reshape(1, FEATURES)), in_hbm(bins))
    lambdas, lambdas_again = pl.pallas_call(
        pair_kernel,
        out_shape=(shape((2, OWN), F32), shape((2, OWN), F32)),
        in_specs=[SMEM] + [VMEM] * 4,
        out_specs=(VMEM, VMEM),
        scratch_shapes=[pltpu.VMEM((8, WIN), F32)] + [column] * 3 + [pltpu.VMEM((8, WIN), F32)] * 2 + [pltpu.VMEM((8, OWN), F32)] * 2,
        compiler_params=pltpu.CompilerParams(vmem_limit_bytes=32 * 2**20),
        name="pairs",
    )(table, window, rows, id_col, worth_col)
    part = pltpu.VMEM((CHIPS, 3 * HI, GROUP * LO), F32)
    leaf_values, score_step, histograms = pl.pallas_call(
        histogram_kernel,
        out_shape=(
            shape((8, TILE), F32),
            shape((1, OWN), F32),
            shape((8, TILE), F32),
        ),
        in_specs=[VMEM] * 3,
        out_specs=(VMEM, VMEM, VMEM),
        scratch_shapes=[
            pltpu.VMEM((4, 5 * GROUP * HI, OWN), BF16),
            pltpu.VMEM((4, GROUP * LO, OWN), BF16),
            pltpu.VMEM((5, 16, OWN), BF16),
            part, part, part, part,
            pltpu.VMEM((CHIPS, 16, TILE), F32),
            pltpu.VMEM((RING, 16, TILE), F32),
            pltpu.VMEM((2, 16, TILE), F32),
            pltpu.VMEM((RING, 8, TILE), F32),
            pltpu.VMEM((RING, 8, TILE), F32),
            dma((CHIPS,)), dma((CHIPS,)), dma((CHIPS,)), dma((CHIPS,)), dma((CHIPS,)), dma((CHIPS,)),
            dma((RING,)), dma((RING,)), dma((RING,)), dma((RING,)), dma((1,)), dma((1,)),
        ],
        compiler_params=pltpu.CompilerParams(
            collective_id=2, has_side_effects=True, vmem_limit_bytes=32 * 2**20),
        name="histograms",
    )(lambdas_again, leaves.reshape(1, OWN), bins_t)
    leaf_values, score_step, histograms = pl.pallas_call(
        finish_kernel,
        out_shape=(
            shape((8, TILE), F32),
            shape((1, OWN), F32),
            shape((3, BINS), F32),
        ),
        in_specs=[VMEM] * 3,
        out_specs=(HBM, HBM, HBM),
        scratch_shapes=[pltpu.VMEM((3, BINS), F32), dma((3,))],
        compiler_params=pltpu.CompilerParams(vmem_limit_bytes=2**21),
        name="finish",
    )(leaf_values, score_step, histograms)
    return lambdas, leaf_values.reshape(LEAVES), score_step.reshape(OWN), histograms


def solution(mesh):
    in_specs = (
        P(("query", "feat")),
        P("query"),
        P(("query", "feat")),
        P(("query", "feat"), None),
        P("query", None),
        P(),
    )
    out_specs = (P(None, ("query", "feat")), P(), P(("query", "feat")), P(None, ("query", "feat")))
    return jax.shard_map(local, mesh=mesh, in_specs=in_specs, out_specs=out_specs, check_vma=False)
```

```python
import functools

import jax
import jax.numpy as jnp
from jax import lax
from jax.experimental import pallas as pl
from jax.experimental.pallas import tpu as pltpu
from jax.sharding import PartitionSpec as P

BINS = 256
LEAVES = 1024
FEATURES = 256
OWN = 1024
WIN = 3 * OWN
BLOCK = 8192
QUERIES = 32
TILE = 128
TILES = WIN // TILE
OWN_TILES = OWN // TILE
STEP = 128
PAIR = 2 * TILE
CHIPS = 16
SIDE = 4
RING = 8
GROUP = 8
FAR_FIRST = (4, 3, 5, 2, 6, 1, 7)
EARLY = 6
HI = 8
LO = 32

lasso_penalty = 1.0
ridge_penalty = 1.0
shrinkage = 0.1

F32 = jnp.float32
BF16 = jnp.bfloat16
MESH_ID = pl.DeviceIdType.MESH
VMEM = pl.BlockSpec(memory_space=pltpu.VMEM)
HBM = pl.BlockSpec(memory_space=pltpu.HBM)
SMEM = pl.BlockSpec(memory_space=pltpu.SMEM)


def nt_dot(left, right):
    return lax.dot_general(left, right, (((1,), (1,)), ((), ())), preferred_element_type=F32)


def spread(line):
    return jnp.broadcast_to(line, (TILE, TILE)).T


def in_hbm(array):
    return pltpu.with_memory_space_constraint(array, pltpu.HBM)


def iota(shape, axis):
    return lax.broadcasted_iota(jnp.int32, shape, axis)


def prepare_kernel(
    scores_in, labels_in, lengths_in, owner_in, bins_in, window, rows, table, bins_t, id_col, worth_col,
    labels, lengths, owner, bins, own_scores, from_left, from_right, load_sem, send_sem, recv_sem
):
    feat = lax.axis_index("feat")
    query = lax.axis_index("query")
    left = lax.rem(feat + RING - 1, RING)
    right = lax.rem(feat + 1, RING)

    barrier = pltpu.get_barrier_semaphore()
    for peer in (left, right):
        pl.semaphore_signal(barrier, inc=1, device_id=(query, peer), device_id_type=MESH_ID)
    loads = [
        pltpu.make_async_copy(source, target, load_sem.at[which])
        for which, (source, target) in enumerate((
            (lengths_in, lengths), (labels_in, labels), (owner_in, owner), (bins_in, bins), (scores_in, own_scores)))]
    for load in loads:
        load.start()
    to_right = pltpu.make_async_remote_copy(
        src_ref=scores_in, dst_ref=from_left, send_sem=send_sem.at[0], recv_sem=recv_sem.at[0],
        device_id=(query, right), device_id_type=MESH_ID)
    to_left = pltpu.make_async_remote_copy(
        src_ref=scores_in, dst_ref=from_right, send_sem=send_sem.at[1], recv_sem=recv_sem.at[1],
        device_id=(query, left), device_id_type=MESH_ID)
    pl.semaphore_wait(barrier, 2)
    to_right.start()
    to_left.start()
    for load in loads[:2]:
        load.wait()

    base = (feat * OWN - OWN).astype(F32)
    length_row = jnp.broadcast_to(lengths[...].astype(F32), (QUERIES, QUERIES))
    other, one = iota((QUERIES, QUERIES), 1), iota((QUERIES, QUERIES), 0)
    starts = jnp.sum(jnp.where(other < one, length_row, 0.0), axis=1, keepdims=True)
    ends = jnp.sum(jnp.where(other <= one, length_row, 0.0), axis=1, keepdims=True)
    place = iota((1, WIN), 1).astype(F32) + base
    inside = (place >= starts) & (place < ends)
    passed = jnp.sum(jnp.where(place >= ends, 1.0, 0.0), axis=0, keepdims=True)
    ids = jnp.where(place < 0.0, -1.0, passed)

    def label_part(block):
        return labels[:, pl.ds(pl.multiple_of(block * OWN, OWN), OWN)]

    grades = jnp.concatenate([label_part(left), label_part(feat), label_part(right)], axis=1)
    worth = lax.shift_left(jnp.ones_like(grades), grades).astype(F32)

    at_least = (jnp.broadcast_to(grades, (8, WIN)) > iota((8, WIN), 0)).astype(F32).astype(BF16)
    counts = nt_dot(inside.astype(F32).astype(BF16), at_least)
    spot = iota((1, OWN), 1).astype(F32)
    gain = 1.0 / jnp.log2(2.0 + spot)
    parts = jnp.zeros((QUERIES, OWN), F32)
    for level in range(4):
        parts = parts + jnp.where(spot < counts[:, level:level + 1], gain * float(2 ** level), 0.0)
    ideal = jnp.sum(parts, axis=1, keepdims=True)
    usable = ideal > 0.5
    inverse = jnp.where(usable, 1.0 / jnp.where(usable, ideal, 1.0), 0.0)
    own_inverse = jnp.sum(jnp.where(inside, inverse, 0.0), axis=0, keepdims=True)

    def bound_at(spots, values):
        hit = (spots >= starts) & (spots < ends)
        return jnp.sum(jnp.where(hit, values, 0.0), axis=0, keepdims=True)

    zeros = jnp.zeros((1, TILE), F32)
    first = bound_at(zeros + (base + OWN), starts)
    last = bound_at(zeros + (base + 2 * OWN - 1.0), ends)
    tile_first = base + iota((1, TILE), 1).astype(F32) * TILE
    low = bound_at(jnp.maximum(tile_first, first), starts)
    high = bound_at(jnp.minimum(tile_first + (TILE - 1.0), last - 1.0), ends)
    line = iota((8, TILE), 0)
    bounds = jnp.where(line == 0, low, jnp.where(line == 1, high, jnp.where(line == 2, first, last)))
    table[...] = (bounds - base).astype(jnp.int32)

    rows[...] = jnp.concatenate([ids, worth, own_inverse, own_inverse] * 2, axis=0)
    for tile in range(TILES):
        at = slice(tile * TILE, (tile + 1) * TILE)
        id_col[at, :] = spread(ids[:, at])
        worth_col[at, :] = spread(worth[:, at])

    for load in loads[2:]:
        load.wait()
    pick_t = (iota((FEATURES, FEATURES), 0) == owner[...]).astype(F32)
    pick = pick_t.T.astype(BF16)
    bins_t[...] = nt_dot(pick, bins[...].astype(F32).astype(BF16))

    window[:, OWN:2 * OWN] = own_scores[...]
    to_right.wait()
    to_left.wait()
    window[:, 0:OWN] = from_left[...]
    window[:, 2 * OWN:WIN] = from_right[...]


def pair_kernel(
    table, window_in, rows, id_col, worth_col, out, out_again,
    lines, score_col, up_col, discount_col, counts, discount_row, grads, curvs
):
    window = window_in[...]
    lines[...] = jnp.concatenate([window, jnp.exp(-window), jnp.exp(window), window] * 2, axis=0)
    for tile in range(TILES):
        at = slice(tile * TILE, (tile + 1) * TILE)
        score_col[at, :] = spread(lines[0:1, at])
        up_col[at, :] = spread(lines[1:2, at])
    counts[...] = jnp.zeros_like(counts)

    def blocks_of(pair):
        low, high = table[0, 2 * pair], table[1, 2 * pair + 1]
        alone = (low == table[0, 2 * pair + 1]) & (high == table[1, 2 * pair])
        return low // STEP, (high + STEP - 1) // STEP, (low + STEP - 1) // STEP, high // STEP, alone

    active = table[2, 0] // PAIR
    stop = (table[3, 0] + PAIR - 1) // PAIR

    def rank_pair(pair, carry):
        begin = pl.multiple_of(pair * PAIR, PAIR)
        score = jnp.broadcast_to(lines[0:1, pl.ds(begin, PAIR)], (8, PAIR))
        ident = jnp.broadcast_to(rows[0:1, pl.ds(begin, PAIR)], (8, PAIR))

        def count(start, steps, beats, total, masked=True):
            for sub in range(steps):
                spot = pl.multiple_of(start + sub * 8, 8)
                other = score_col[pl.ds(spot, 8), :]
                other_id = id_col[pl.ds(spot, 8), :] if masked else None
                parts = []
                for half in range(2):
                    lanes = slice(half * TILE, (half + 1) * TILE)
                    hit = beats(other, score[:, lanes], half, sub)
                    if masked:
                        hit = hit & (other_id == ident[:, lanes])
                    parts.append(total[half] + jnp.where(hit, 1.0, 0.0))
                total = tuple(parts)
            return total

        def ahead(other, own, half, sub):
            return other >= own

        def behind(other, own, half, sub):
            return other > own

        def around(other, own, half, sub):
            if sub * 8 < half * TILE:
                return other >= own
            if sub * 8 >= (half + 1) * TILE:
                return other > own
            earlier = iota((8, TILE), 0) + (sub * 8 - half * TILE) < iota((8, TILE), 1)
            return (other > own) | ((other == own) & earlier)

        empty = jnp.zeros((8, TILE), F32)
        total = count(begin, PAIR // 8, around, (empty, empty))
        def run(first, stop, beats, masked, total):
            return lax.fori_loop(
                first, stop, lambda i, t: count(i * STEP, STEP // 8, beats, t, masked), total)

        low, high, inner_low, inner_high, alone = blocks_of(pair)
        here, after = begin // STEP, (begin + PAIR) // STEP
        inner_low = jnp.where(alone, jnp.minimum(inner_low, here), here)
        inner_high = jnp.where(alone, jnp.maximum(inner_high, after), after)
        total = run(low, inner_low, ahead, True, total)
        total = run(inner_low, here, ahead, False, total)
        total = run(after, inner_high, behind, False, total)
        total = run(inner_high, high, behind, True, total)
        counts[:, pl.ds(begin, PAIR)] = jnp.concatenate(total, axis=1)
        return carry

    lax.fori_loop(active, stop, rank_pair, 0)

    rank = jnp.broadcast_to(jnp.sum(counts[...], axis=0, keepdims=True), (8, WIN))
    discount = 1.0 / jnp.log2(2.0 + rank)
    discount_row[...] = discount
    for tile in range(TILES):
        at = slice(tile * TILE, (tile + 1) * TILE)
        discount_col[at, :] = spread(discount[0:1, at])

    def own_pair(index, carry):
        pair = index + OWN // PAIR
        begin = pl.multiple_of(pair * PAIR, PAIR)

        def own(ref, line):
            return jnp.broadcast_to(ref[line:line + 1, pl.ds(begin, PAIR)], (8, PAIR))

        up = -own(lines, 2)
        ident = own(rows, 0)
        worth = own(rows, 1)
        discount = discount_row[:, pl.ds(begin, PAIR)]

        def meet(masked, block, sums):
            for sub in range(STEP // 8):
                at = pl.ds(pl.multiple_of(block * STEP + sub * 8, 8), 8)
                other_up, other_id = up_col[at, :], id_col[at, :]
                other_discount, other_worth = discount_col[at, :], worth_col[at, :]
                parts = []
                for half in range(2):
                    lanes = slice(half * TILE, (half + 1) * TILE)
                    odds = up[:, lanes] * other_up
                    win = pltpu.reciprocal(1.0 - odds, approx=True)
                    lose = odds * win
                    gap = discount[:, lanes] - other_discount
                    if masked:
                        gap = jnp.where(other_id == ident[:, lanes], gap, 0.0)
                    rise = worth[:, lanes] - other_worth
                    change = jnp.abs(rise * gap)
                    parts.append(sums[half][0] + change * jnp.where(rise > 0.0, win, lose))
                    parts.append(sums[half][1] + change * (win * lose))
                sums = ((parts[0], parts[1]), (parts[2], parts[3]))
            return sums

        empty = jnp.zeros((8, TILE), F32)
        low, high, inner_low, inner_high, alone = blocks_of(pair)
        inner_low = jnp.where(alone, inner_low, high)
        inner_high = jnp.where(alone, inner_high, high)
        sums = ((empty, empty), (empty, empty))
        for first, stop, masked in ((low, inner_low, True), (inner_low, inner_high, False), (inner_high, high, True)):
            sums = lax.fori_loop(first, stop, functools.partial(meet, masked), sums)
        for half in range(2):
            spot = pl.ds(pl.multiple_of(index * PAIR + half * TILE, TILE), TILE)
            grads[:, spot] = sums[half][0]
            curvs[:, spot] = sums[half][1]
        return carry

    lax.fori_loop(0, OWN // PAIR, own_pair, 0)
    inverse = -rows[2:3, OWN:2 * OWN]
    both = jnp.concatenate([
        inverse * jnp.sum(grads[...], axis=0, keepdims=True),
        inverse * jnp.sum(curvs[...], axis=0, keepdims=True)], axis=0)
    out[...] = both
    out_again[...] = both


def in_pieces(value, pieces):
    found = []
    for unused in range(pieces):
        piece = value.astype(BF16)
        found.append(piece)
        value = value - piece.astype(F32)
    return found


def histogram_kernel(
    lambdas, leaves, bins_t, leaf_out, step_out, hist_out,
    left_side, right_side, weights, pair_sent, pair_got, sent, got,
    leaf_got, leaf_ring, leaf_both, chunk, chunk_got,
    pair_send, pair_recv, send_sem, recv_sem, leaf_send, leaf_recv, ring_send, ring_recv,
    chunk_send, chunk_recv, one_send, one_recv
):
    query = lax.axis_index("query")
    feat = lax.axis_index("feat")
    core = lax.rem(query, 2)
    chip = lax.div(query, 2)
    other_core = 1 - core
    sibling = chip * 2 + other_core
    chip_y, chip_x = lax.div(chip, SIDE), lax.rem(chip, SIDE)

    def steps_to(offset):
        turn = lax.rem(offset + CHIPS - 1, CHIPS)
        return lax.rem(lax.div(turn, SIDE) + 1, SIDE), lax.rem(lax.rem(turn, SIDE) + 1, SIDE)

    def chip_peer(offset):
        down, across = steps_to(offset)
        return lax.rem(chip_y + down, SIDE) * SIDE + lax.rem(chip_x + across, SIDE)

    def chip_source(offset):
        down, across = steps_to(offset)
        return lax.rem(chip_y + SIDE - down, SIDE) * SIDE + lax.rem(chip_x + SIDE - across, SIDE)

    def ring_peer(offset):
        return lax.rem(feat + offset, RING)

    def remote(source, target, send, recv, device):
        return pltpu.make_async_remote_copy(
            src_ref=source, dst_ref=target, send_sem=send, recv_sem=recv, device_id=device, device_id_type=MESH_ID)

    barrier = pltpu.get_barrier_semaphore()
    for offset in FAR_FIRST[:3]:
        pl.semaphore_signal(barrier, inc=1, device_id=(query, ring_peer(offset)), device_id_type=MESH_ID)

    @pl.loop(1, CHIPS)
    def _(offset):
        pl.semaphore_signal(barrier, inc=1, device_id=(chip_peer(offset) * 2 + core, feat), device_id_type=MESH_ID)

    for offset in FAR_FIRST[3:]:
        pl.semaphore_signal(barrier, inc=1, device_id=(query, ring_peer(offset)), device_id_type=MESH_ID)
    pl.semaphore_signal(barrier, inc=1, device_id=(sibling, feat), device_id_type=MESH_ID)

    grad, curv = lambdas[0:1, :], lambdas[1:2, :]
    leaf = leaves[...]
    leaf_row = lax.shift_right_logical(leaf, 7)
    leaf_lane = jnp.bitwise_and(leaf, 127)
    in_row = iota((8, OWN), 0) == leaf_row
    lane_hot = (iota((TILE, OWN), 0) == leaf_lane).astype(F32).astype(BF16)
    placed = []
    for value in (grad, curv):
        for piece in in_pieces(value, 3):
            placed.append(jnp.where(in_row, piece.astype(F32), 0.0).astype(BF16))
    leaf_sums = nt_dot(jnp.concatenate(placed, axis=0), lane_hot)
    leaf_got[chip, 0:8, :] = leaf_sums[0:8] + leaf_sums[8:16] + leaf_sums[16:24]
    leaf_got[chip, 8:16, :] = leaf_sums[24:32] + leaf_sums[32:40] + leaf_sums[40:48]
    chunk[...] = jnp.zeros_like(chunk)

    stats = in_pieces(grad, 2) + in_pieces(curv, 2) + [jnp.ones((1, OWN), BF16)]
    for which, value in enumerate(stats):
        weights[which] = jnp.broadcast_to(value, (16, OWN))

    low_levels = iota((LO, OWN), 0).astype(F32).astype(BF16)
    high_levels = jnp.bitwise_and(iota((16, OWN), 0), 7).astype(F32).astype(BF16)
    upper = iota((16, OWN), 0) < 8
    zero = jnp.zeros((), BF16)
    unit = jnp.ones((), BF16)

    def one_hots(group, slot):
        block = bins_t[pl.ds(pl.multiple_of(group * GROUP, GROUP), GROUP), :]
        high = jnp.floor(block * (1.0 / LO))
        low = block - high * LO
        for k in range(GROUP):
            spread_low = jnp.broadcast_to(low[k:k + 1].astype(BF16), (LO, OWN))
            right_side[slot, k * LO:(k + 1) * LO, :] = jnp.where(spread_low == low_levels, unit, zero)
        for pair in range(GROUP // 2):
            k = 2 * pair
            both = jnp.where(
                upper, jnp.broadcast_to(high[k:k + 1], (16, OWN)),
                jnp.broadcast_to(high[k + 1:k + 2], (16, OWN))).astype(BF16)
            hot = both == high_levels
            for which in range(5):
                left_side[slot, which * 64 + pair * 16:which * 64 + (pair + 1) * 16, :] = jnp.where(
                    hot, weights[which], zero)

    def sums(slot, target, index):
        full = nt_dot(left_side[slot], right_side[slot])
        lane = iota((HI, TILE), 1)
        for stat, whichs in enumerate(((0, 1), (2, 3), (4,))):
            for half in range(2):
                lanes = slice(half * TILE, (half + 1) * TILE)
                total = None
                for which in whichs:
                    picked = None
                    for j in range(4):
                        k = half * 4 + j
                        piece = full[which * 64 + k * HI:which * 64 + (k + 1) * HI, lanes]
                        picked = piece if j == 0 else jnp.where(lane >= j * LO, piece, picked)
                    total = picked if total is None else total + picked
                target[index, stat * HI:(stat + 1) * HI, lanes] = total

    def chip_at(turn):
        return chip_peer(lax.rem(turn + 1, CHIPS))

    def groups_of(turns):
        peers = [chip_at(turn) for turn in turns]
        for which, peer in enumerate(peers):
            one_hots(peer * 2 + other_core, 2 * which)
            one_hots(peer * 2 + core, 2 * which + 1)
        for which, peer in enumerate(peers):
            sums(2 * which, pair_sent, peer)
            sums(2 * which + 1, sent, peer)

    def pair_copy(turn):
        peer = chip_at(turn)
        return remote(pair_sent.at[peer], pair_got.at[peer], pair_send.at[peer], pair_recv.at[peer], (sibling, feat))

    def plane_copy(offset):
        peer = chip_peer(offset)
        return remote(sent.at[peer], got.at[chip], send_sem.at[peer], recv_sem.at[chip], (peer * 2 + core, feat))

    def plane_arrival(offset):
        peer = chip_source(offset)
        return remote(sent.at[peer], got.at[peer], send_sem.at[peer], recv_sem.at[peer], (peer * 2 + core, feat))

    def join(turn):
        pair_copy(turn).wait_recv()
        peer = chip_at(turn)
        sent[peer] = sent[peer] + pair_got[peer]

    def join_and_send(turn):
        join(turn)
        plane_copy(turn + 1).start()

    @pl.loop(0, EARLY // 2)
    def _(step):
        groups_of((2 * step, 2 * step + 1))

    pl.semaphore_wait(barrier, 1 + CHIPS - 1 + RING - 1)

    def leaf_copy(offset):
        peer = chip_peer(offset)
        return remote(leaf_got.at[chip], leaf_got.at[chip], leaf_send.at[peer], leaf_recv.at[chip], (peer * 2 + core, feat))

    def leaf_arrival(offset):
        peer = chip_source(offset)
        return remote(leaf_got.at[chip], leaf_got.at[peer], leaf_send.at[peer], leaf_recv.at[peer], (peer * 2 + core, feat))

    @pl.loop(1, CHIPS)
    def _(offset):
        leaf_copy(offset).start()

    @pl.loop(0, EARLY)
    def _(turn):
        pair_copy(turn).start()

    groups_of((EARLY, EARLY + 1))
    pair_copy(EARLY).start()
    pair_copy(EARLY + 1).start()

    @pl.loop(0, EARLY)
    def _(turn):
        join_and_send(turn)

    @pl.loop(EARLY // 2 + 1, CHIPS // 2 - 1)
    def _(step):
        groups_of((2 * step, 2 * step + 1))
        pair_copy(2 * step).start()
        pair_copy(2 * step + 1).start()
        join_and_send(2 * step - 2)
        join_and_send(2 * step - 1)

    groups_of((CHIPS - 2,))
    pair_copy(CHIPS - 2).start()
    join_and_send(CHIPS - 4)
    join_and_send(CHIPS - 3)
    groups_of((CHIPS - 1,))
    pair_copy(CHIPS - 1).start()
    @pl.loop(1, CHIPS)
    def _(offset):
        leaf_arrival(offset).wait_recv()

    leaf_ring[feat] = lax.fori_loop(
        0, CHIPS, lambda peer, total: total + leaf_got[peer], jnp.zeros((16, TILE), F32))

    def ring_copy(offset):
        peer = ring_peer(offset)
        return remote(leaf_ring.at[feat], leaf_ring.at[feat], ring_send.at[peer], ring_recv.at[feat], (query, peer))

    def ring_arrival(offset):
        peer = ring_peer(offset)
        return remote(leaf_ring.at[feat], leaf_ring.at[peer], ring_send.at[peer], ring_recv.at[peer], (query, peer))

    @pl.loop(1, RING)
    def _(offset):
        ring_copy(offset).start()

    join_and_send(CHIPS - 2)
    join(CHIPS - 1)

    def add_hist(offset, total):
        plane_arrival(offset).wait_recv()
        return total + got[chip_source(offset)]

    summed = lax.fori_loop(1, CHIPS, add_hist, sent[chip])

    lane_block = lax.shift_right_logical(iota((GROUP, TILE), 1), 5)
    holder = iota((GROUP, TILE), 0)
    for stat in range(3):
        for half in range(2):
            moved = jnp.zeros((GROUP, TILE), F32)
            for r in range(4):
                row = stat * HI + half * 4 + r
                line = jnp.where(
                    holder < 4, jnp.broadcast_to(summed[row:row + 1, 0:TILE], (GROUP, TILE)),
                    jnp.broadcast_to(summed[row:row + 1, TILE:2 * TILE], (GROUP, TILE)))
                for kk in range(4):
                    shift = (r - kk) % 4 * LO
                    turned = pltpu.roll(line, shift, 1) if shift else line
                    moved = jnp.where((jnp.bitwise_and(holder, 3) == kk) & (lane_block == r), turned, moved)
            line = stat * 2 + half
            for k in range(GROUP):
                chunk[k, line:line + 1, :] = moved[k:k + 1, :]

    def chunk_copy(offset):
        peer = ring_peer(offset)
        return remote(chunk.at[peer], chunk_got.at[feat], chunk_send.at[peer], chunk_recv.at[feat], (query, peer))

    def chunk_arrival(offset):
        peer = ring_peer(offset)
        return remote(chunk.at[peer], chunk_got.at[peer], chunk_send.at[peer], chunk_recv.at[peer], (query, peer))

    for offset in FAR_FIRST:
        chunk_copy(offset).start()

    @pl.loop(1, RING)
    def _(offset):
        ring_arrival(offset).wait_recv()

    core_total = leaf_ring[0]
    for peer in range(1, RING):
        core_total = core_total + leaf_ring[peer]
    leaf_both[core] = core_total
    leaf_back = remote(leaf_both.at[core], leaf_both.at[core], one_send.at[0], one_recv.at[0], (sibling, feat))
    leaf_back.start()

    leaf_back_here = remote(
        leaf_both.at[core], leaf_both.at[other_core], one_send.at[0], one_recv.at[0], (sibling, feat))
    leaf_back_here.wait_recv()
    totals = leaf_both[0] + leaf_both[1]
    total_grad, total_curv = totals[0:8], totals[8:16]
    shrunk = jnp.maximum(jnp.abs(total_grad) - lasso_penalty, 0.0) / (total_curv + ridge_penalty)
    values = jnp.where(total_grad > 0.0, -shrunk, shrunk)
    leaf_out[...] = values
    found = jnp.zeros((8, OWN), F32)
    for piece in in_pieces(values, 3):
        found = found + jnp.dot(piece, lane_hot, preferred_element_type=F32)
    step_out[...] = shrinkage * jnp.sum(jnp.where(in_row, found, 0.0), axis=0, keepdims=True)

    leaf_back.wait_send()
    pair_copy(CHIPS - 1).wait_send()

    @pl.loop(1, CHIPS)
    def _(offset):
        pair_copy(offset - 1).wait_send()
        plane_copy(offset).wait_send()
        leaf_copy(offset).wait_send()

    @pl.loop(1, RING)
    def _(offset):
        ring_copy(offset).wait_send()

    total = chunk[feat]
    for offset in reversed(FAR_FIRST):
        chunk_arrival(offset).wait_recv()
        total = total + chunk_got[ring_peer(offset)]
    hist_out[...] = total
    for offset in FAR_FIRST:
        chunk_copy(offset).wait_send()


def finish_kernel(leaf_in, step_in, hist_in, leaf_out, step_out, hist_out, hist, sem):
    for stat in range(3):
        for half in range(2):
            line = stat * 2 + half
            hist[stat:stat + 1, half * TILE:(half + 1) * TILE] = hist_in[line:line + 1, :]
    copies = [
        pltpu.make_async_copy(source, target, sem.at[which])
        for which, (source, target) in enumerate(((leaf_in, leaf_out), (step_in, step_out), (hist, hist_out)))]
    for copy in copies:
        copy.start()
    for copy in copies:
        copy.wait()


def local(scores, labels, leaves, bins, lengths, owner):
    shape = jax.ShapeDtypeStruct
    dma = pltpu.SemaphoreType.DMA
    column = pltpu.VMEM((WIN, TILE), F32)
    window, rows, table, bins_t, id_col, worth_col = pl.pallas_call(
        prepare_kernel,
        out_shape=(
            shape((1, WIN), F32),
            shape((8, WIN), F32),
            shape((8, TILE), jnp.int32),
            shape((FEATURES, OWN), F32),
            shape((WIN, TILE), F32),
            shape((WIN, TILE), F32),
        ),
        in_specs=[HBM] * 5,
        out_specs=(VMEM,) * 6,
        scratch_shapes=[
            pltpu.VMEM((1, BLOCK), jnp.int32), pltpu.VMEM((1, QUERIES), jnp.int32),
            pltpu.VMEM((1, FEATURES), jnp.int32), pltpu.VMEM((OWN, FEATURES), jnp.int32),
            pltpu.VMEM((1, OWN), F32), pltpu.VMEM((1, OWN), F32), pltpu.VMEM((1, OWN), F32),
            dma((5,)), dma((2,)), dma((2,))],
        compiler_params=pltpu.CompilerParams(
            collective_id=1, has_side_effects=True, vmem_limit_bytes=32 * 2**20),
        name="prepare",
    )(in_hbm(scores.reshape(1, OWN)), in_hbm(labels.reshape(1, BLOCK)), in_hbm(lengths), in_hbm(owner.reshape(1, FEATURES)), in_hbm(bins))
    lambdas, lambdas_again = pl.pallas_call(
        pair_kernel,
        out_shape=(shape((2, OWN), F32), shape((2, OWN), F32)),
        in_specs=[SMEM] + [VMEM] * 4,
        out_specs=(VMEM, VMEM),
        scratch_shapes=[pltpu.VMEM((8, WIN), F32)] + [column] * 3 + [pltpu.VMEM((8, WIN), F32)] * 2 + [pltpu.VMEM((8, OWN), F32)] * 2,
        compiler_params=pltpu.CompilerParams(vmem_limit_bytes=32 * 2**20),
        name="pairs",
    )(table, window, rows, id_col, worth_col)
    part = pltpu.VMEM((CHIPS, 3 * HI, GROUP * LO), F32)
    leaf_values, score_step, histograms = pl.pallas_call(
        histogram_kernel,
        out_shape=(
            shape((8, TILE), F32),
            shape((1, OWN), F32),
            shape((8, TILE), F32),
        ),
        in_specs=[VMEM] * 3,
        out_specs=(VMEM, VMEM, VMEM),
        scratch_shapes=[
            pltpu.VMEM((4, 5 * GROUP * HI, OWN), BF16),
            pltpu.VMEM((4, GROUP * LO, OWN), BF16),
            pltpu.VMEM((5, 16, OWN), BF16),
            part, part, part, part,
            pltpu.VMEM((CHIPS, 16, TILE), F32),
            pltpu.VMEM((RING, 16, TILE), F32),
            pltpu.VMEM((2, 16, TILE), F32),
            pltpu.VMEM((RING, 8, TILE), F32),
            pltpu.VMEM((RING, 8, TILE), F32),
            dma((CHIPS,)), dma((CHIPS,)), dma((CHIPS,)), dma((CHIPS,)), dma((CHIPS,)), dma((CHIPS,)),
            dma((RING,)), dma((RING,)), dma((RING,)), dma((RING,)), dma((1,)), dma((1,)),
        ],
        compiler_params=pltpu.CompilerParams(
            collective_id=2, has_side_effects=True, vmem_limit_bytes=32 * 2**20),
        name="histograms",
    )(lambdas_again, leaves.reshape(1, OWN), bins_t)
    leaf_values, score_step, histograms = pl.pallas_call(
        finish_kernel,
        out_shape=(
            shape((8, TILE), F32),
            shape((1, OWN), F32),
            shape((3, BINS), F32),
        ),
        in_specs=[VMEM] * 3,
        out_specs=(HBM, HBM, HBM),
        scratch_shapes=[pltpu.VMEM((3, BINS), F32), dma((3,))],
        compiler_params=pltpu.CompilerParams(vmem_limit_bytes=2**21),
        name="finish",
    )(leaf_values, score_step, histograms)
    return lambdas, leaf_values.reshape(LEAVES), score_step.reshape(OWN), histograms


def solution(mesh):
    in_specs = (
        P(("query", "feat")),
        P("query"),
        P(("query", "feat")),
        P(("query", "feat"), None),
        P("query", None),
        P(),
    )
    out_specs = (P(None, ("query", "feat")), P(), P(("query", "feat")), P(None, ("query", "feat")))
    return jax.shard_map(local, mesh=mesh, in_specs=in_specs, out_specs=out_specs, check_vma=False)
```

```python
import functools

import jax
import jax.numpy as jnp
from jax import lax
from jax.experimental import pallas as pl
from jax.experimental.pallas import tpu as pltpu
from jax.sharding import PartitionSpec as P

BINS = 256
LEAVES = 1024
FEATURES = 256
OWN = 1024
WIN = 3 * OWN
BLOCK = 8192
QUERIES = 32
TILE = 128
TILES = WIN // TILE
OWN_TILES = OWN // TILE
STEP = 128
PAIR = 2 * TILE
CHIPS = 16
SIDE = 4
RING = 8
GROUP = 8
FAR_FIRST = (4, 3, 5, 2, 6, 1, 7)
EARLY = 6
HI = 8
LO = 32

lasso_penalty = 1.0
ridge_penalty = 1.0
shrinkage = 0.1

F32 = jnp.float32
BF16 = jnp.bfloat16
MESH_ID = pl.DeviceIdType.MESH
VMEM = pl.BlockSpec(memory_space=pltpu.VMEM)
HBM = pl.BlockSpec(memory_space=pltpu.HBM)
SMEM = pl.BlockSpec(memory_space=pltpu.SMEM)


def nt_dot(left, right):
    return lax.dot_general(left, right, (((1,), (1,)), ((), ())), preferred_element_type=F32)


def spread(line):
    return jnp.broadcast_to(line, (TILE, TILE)).T


def in_hbm(array):
    return pltpu.with_memory_space_constraint(array, pltpu.HBM)


def iota(shape, axis):
    return lax.broadcasted_iota(jnp.int32, shape, axis)


def prepare_kernel(
    scores_in, labels_in, lengths_in, owner_in, bins_in, window, rows, table, bins_t, id_col, worth_col,
    labels, lengths, owner, bins, own_scores, from_left, from_right, load_sem, send_sem, recv_sem
):
    feat = lax.axis_index("feat")
    query = lax.axis_index("query")
    left = lax.rem(feat + RING - 1, RING)
    right = lax.rem(feat + 1, RING)

    barrier = pltpu.get_barrier_semaphore()
    for peer in (left, right):
        pl.semaphore_signal(barrier, inc=1, device_id=(query, peer), device_id_type=MESH_ID)
    loads = [
        pltpu.make_async_copy(source, target, load_sem.at[which])
        for which, (source, target) in enumerate((
            (lengths_in, lengths), (labels_in, labels), (owner_in, owner), (bins_in, bins), (scores_in, own_scores)))]
    for load in loads:
        load.start()
    to_right = pltpu.make_async_remote_copy(
        src_ref=scores_in, dst_ref=from_left, send_sem=send_sem.at[0], recv_sem=recv_sem.at[0],
        device_id=(query, right), device_id_type=MESH_ID)
    to_left = pltpu.make_async_remote_copy(
        src_ref=scores_in, dst_ref=from_right, send_sem=send_sem.at[1], recv_sem=recv_sem.at[1],
        device_id=(query, left), device_id_type=MESH_ID)
    pl.semaphore_wait(barrier, 2)
    to_right.start()
    to_left.start()
    for load in loads[:2]:
        load.wait()

    base = (feat * OWN - OWN).astype(F32)
    length_row = jnp.broadcast_to(lengths[...].astype(F32), (QUERIES, QUERIES))
    other, one = iota((QUERIES, QUERIES), 1), iota((QUERIES, QUERIES), 0)
    starts = jnp.sum(jnp.where(other < one, length_row, 0.0), axis=1, keepdims=True)
    ends = jnp.sum(jnp.where(other <= one, length_row, 0.0), axis=1, keepdims=True)
    place = iota((1, WIN), 1).astype(F32) + base
    inside = (place >= starts) & (place < ends)
    passed = jnp.sum(jnp.where(place >= ends, 1.0, 0.0), axis=0, keepdims=True)
    ids = jnp.where(place < 0.0, -1.0, passed)

    def label_part(block):
        return labels[:, pl.ds(pl.multiple_of(block * OWN, OWN), OWN)]

    grades = jnp.concatenate([label_part(left), label_part(feat), label_part(right)], axis=1)
    worth = lax.shift_left(jnp.ones_like(grades), grades).astype(F32)

    at_least = (jnp.broadcast_to(grades, (8, WIN)) > iota((8, WIN), 0)).astype(F32).astype(BF16)
    counts = nt_dot(inside.astype(F32).astype(BF16), at_least)
    spot = iota((1, OWN), 1).astype(F32)
    gain = 1.0 / jnp.log2(2.0 + spot)
    parts = jnp.zeros((QUERIES, OWN), F32)
    for level in range(4):
        parts = parts + jnp.where(spot < counts[:, level:level + 1], gain * float(2 ** level), 0.0)
    ideal = jnp.sum(parts, axis=1, keepdims=True)
    usable = ideal > 0.5
    inverse = jnp.where(usable, 1.0 / jnp.where(usable, ideal, 1.0), 0.0)
    own_inverse = jnp.sum(jnp.where(inside, inverse, 0.0), axis=0, keepdims=True)

    def bound_at(spots, values):
        hit = (spots >= starts) & (spots < ends)
        return jnp.sum(jnp.where(hit, values, 0.0), axis=0, keepdims=True)

    zeros = jnp.zeros((1, TILE), F32)
    first = bound_at(zeros + (base + OWN), starts)
    last = bound_at(zeros + (base + 2 * OWN - 1.0), ends)
    tile_first = base + iota((1, TILE), 1).astype(F32) * TILE
    low = bound_at(jnp.maximum(tile_first, first), starts)
    high = bound_at(jnp.minimum(tile_first + (TILE - 1.0), last - 1.0), ends)
    line = iota((8, TILE), 0)
    bounds = jnp.where(line == 0, low, jnp.where(line == 1, high, jnp.where(line == 2, first, last)))
    table[...] = (bounds - base).astype(jnp.int32)

    rows[...] = jnp.concatenate([ids, worth, own_inverse, own_inverse] * 2, axis=0)
    for tile in range(TILES):
        at = slice(tile * TILE, (tile + 1) * TILE)
        id_col[at, :] = spread(ids[:, at])
        worth_col[at, :] = spread(worth[:, at])

    for load in loads[2:]:
        load.wait()
    pick_t = (iota((FEATURES, FEATURES), 0) == owner[...]).astype(F32)
    pick = pick_t.T.astype(BF16)
    bins_t[...] = nt_dot(pick, bins[...].astype(F32).astype(BF16))

    window[:, OWN:2 * OWN] = own_scores[...]
    to_right.wait()
    to_left.wait()
    window[:, 0:OWN] = from_left[...]
    window[:, 2 * OWN:WIN] = from_right[...]


def pair_kernel(
    table, window_in, rows, id_col, worth_col, out, out_again,
    lines, score_col, up_col, discount_col, counts, discount_row, grads, curvs
):
    window = window_in[...]
    lines[...] = jnp.concatenate([window, jnp.exp(-window), jnp.exp(window), window] * 2, axis=0)
    for tile in range(TILES):
        at = slice(tile * TILE, (tile + 1) * TILE)
        score_col[at, :] = spread(lines[0:1, at])
        up_col[at, :] = spread(lines[1:2, at])
    counts[...] = jnp.zeros_like(counts)

    def blocks_of(pair):
        low, high = table[0, 2 * pair], table[1, 2 * pair + 1]
        alone = (low == table[0, 2 * pair + 1]) & (high == table[1, 2 * pair])
        return low // STEP, (high + STEP - 1) // STEP, (low + STEP - 1) // STEP, high // STEP, alone

    active = table[2, 0] // PAIR
    stop = (table[3, 0] + PAIR - 1) // PAIR

    def rank_pair(pair, carry):
        begin = pl.multiple_of(pair * PAIR, PAIR)
        score = jnp.broadcast_to(lines[0:1, pl.ds(begin, PAIR)], (8, PAIR))
        ident = jnp.broadcast_to(rows[0:1, pl.ds(begin, PAIR)], (8, PAIR))

        def count(start, steps, beats, total, masked=True):
            for sub in range(steps):
                spot = pl.multiple_of(start + sub * 8, 8)
                other = score_col[pl.ds(spot, 8), :]
                other_id = id_col[pl.ds(spot, 8), :] if masked else None
                parts = []
                for half in range(2):
                    lanes = slice(half * TILE, (half + 1) * TILE)
                    hit = beats(other, score[:, lanes], half, sub)
                    if masked:
                        hit = hit & (other_id == ident[:, lanes])
                    parts.append(total[half] + jnp.where(hit, 1.0, 0.0))
                total = tuple(parts)
            return total

        def ahead(other, own, half, sub):
            return other >= own

        def behind(other, own, half, sub):
            return other > own

        def around(other, own, half, sub):
            if sub * 8 < half * TILE:
                return other >= own
            if sub * 8 >= (half + 1) * TILE:
                return other > own
            earlier = iota((8, TILE), 0) + (sub * 8 - half * TILE) < iota((8, TILE), 1)
            return (other > own) | ((other == own) & earlier)

        empty = jnp.zeros((8, TILE), F32)
        total = count(begin, PAIR // 8, around, (empty, empty))
        def run(first, stop, beats, masked, total):
            return lax.fori_loop(
                first, stop, lambda i, t: count(i * STEP, STEP // 8, beats, t, masked), total)

        low, high, inner_low, inner_high, alone = blocks_of(pair)
        here, after = begin // STEP, (begin + PAIR) // STEP
        inner_low = jnp.where(alone, jnp.minimum(inner_low, here), here)
        inner_high = jnp.where(alone, jnp.maximum(inner_high, after), after)
        total = run(low, inner_low, ahead, True, total)
        total = run(inner_low, here, ahead, False, total)
        total = run(after, inner_high, behind, False, total)
        total = run(inner_high, high, behind, True, total)
        counts[:, pl.ds(begin, PAIR)] = jnp.concatenate(total, axis=1)
        return carry

    lax.fori_loop(active, stop, rank_pair, 0)

    rank = jnp.broadcast_to(jnp.sum(counts[...], axis=0, keepdims=True), (8, WIN))
    discount = 1.0 / jnp.log2(2.0 + rank)
    discount_row[...] = discount
    for tile in range(TILES):
        at = slice(tile * TILE, (tile + 1) * TILE)
        discount_col[at, :] = spread(discount[0:1, at])

    def own_pair(index, carry):
        pair = index + OWN // PAIR
        begin = pl.multiple_of(pair * PAIR, PAIR)

        def own(ref, line):
            return jnp.broadcast_to(ref[line:line + 1, pl.ds(begin, PAIR)], (8, PAIR))

        up = -own(lines, 2)
        ident = own(rows, 0)
        worth = own(rows, 1)
        discount = discount_row[:, pl.ds(begin, PAIR)]

        def meet(masked, block, sums):
            for sub in range(STEP // 8):
                at = pl.ds(pl.multiple_of(block * STEP + sub * 8, 8), 8)
                other_up, other_id = up_col[at, :], id_col[at, :]
                other_discount, other_worth = discount_col[at, :], worth_col[at, :]
                parts = []
                for half in range(2):
                    lanes = slice(half * TILE, (half + 1) * TILE)
                    odds = up[:, lanes] * other_up
                    win = pltpu.reciprocal(1.0 - odds, approx=True)
                    lose = odds * win
                    gap = discount[:, lanes] - other_discount
                    if masked:
                        gap = jnp.where(other_id == ident[:, lanes], gap, 0.0)
                    rise = worth[:, lanes] - other_worth
                    change = jnp.abs(rise * gap)
                    parts.append(sums[half][0] + change * jnp.where(rise > 0.0, win, lose))
                    parts.append(sums[half][1] + change * (win * lose))
                sums = ((parts[0], parts[1]), (parts[2], parts[3]))
            return sums

        empty = jnp.zeros((8, TILE), F32)
        low, high, inner_low, inner_high, alone = blocks_of(pair)
        inner_low = jnp.where(alone, inner_low, high)
        inner_high = jnp.where(alone, inner_high, high)
        sums = ((empty, empty), (empty, empty))
        for first, stop, masked in ((low, inner_low, True), (inner_low, inner_high, False), (inner_high, high, True)):
            sums = lax.fori_loop(first, stop, functools.partial(meet, masked), sums)
        for half in range(2):
            spot = pl.ds(pl.multiple_of(index * PAIR + half * TILE, TILE), TILE)
            grads[:, spot] = sums[half][0]
            curvs[:, spot] = sums[half][1]
        return carry

    lax.fori_loop(0, OWN // PAIR, own_pair, 0)
    inverse = -rows[2:3, OWN:2 * OWN]
    both = jnp.concatenate([
        inverse * jnp.sum(grads[...], axis=0, keepdims=True),
        inverse * jnp.sum(curvs[...], axis=0, keepdims=True)], axis=0)
    out[...] = both
    out_again[...] = both


def in_pieces(value, pieces):
    found = []
    for unused in range(pieces):
        piece = value.astype(BF16)
        found.append(piece)
        value = value - piece.astype(F32)
    return found


def histogram_kernel(
    lambdas, leaves, bins_t, leaf_out, step_out, hist_out,
    left_side, right_side, weights, pair_sent, pair_got, sent, got,
    leaf_got, leaf_ring, leaf_both, chunk, chunk_got,
    pair_send, pair_recv, send_sem, recv_sem, leaf_send, leaf_recv, ring_send, ring_recv,
    chunk_send, chunk_recv, one_send, one_recv
):
    query = lax.axis_index("query")
    feat = lax.axis_index("feat")
    core = lax.rem(query, 2)
    chip = lax.div(query, 2)
    other_core = 1 - core
    sibling = chip * 2 + other_core
    chip_y, chip_x = lax.div(chip, SIDE), lax.rem(chip, SIDE)

    def steps_to(offset):
        turn = lax.rem(offset + CHIPS - 1, CHIPS)
        return lax.rem(lax.div(turn, SIDE) + 1, SIDE), lax.rem(lax.rem(turn, SIDE) + 1, SIDE)

    def chip_peer(offset):
        down, across = steps_to(offset)
        return lax.rem(chip_y + down, SIDE) * SIDE + lax.rem(chip_x + across, SIDE)

    def chip_source(offset):
        down, across = steps_to(offset)
        return lax.rem(chip_y + SIDE - down, SIDE) * SIDE + lax.rem(chip_x + SIDE - across, SIDE)

    def ring_peer(offset):
        return lax.rem(feat + offset, RING)

    def remote(source, target, send, recv, device):
        return pltpu.make_async_remote_copy(
            src_ref=source, dst_ref=target, send_sem=send, recv_sem=recv, device_id=device, device_id_type=MESH_ID)

    barrier = pltpu.get_barrier_semaphore()
    for offset in FAR_FIRST[:3]:
        pl.semaphore_signal(barrier, inc=1, device_id=(query, ring_peer(offset)), device_id_type=MESH_ID)

    @pl.loop(1, CHIPS)
    def _(offset):
        pl.semaphore_signal(barrier, inc=1, device_id=(chip_peer(offset) * 2 + core, feat), device_id_type=MESH_ID)

    for offset in FAR_FIRST[3:]:
        pl.semaphore_signal(barrier, inc=1, device_id=(query, ring_peer(offset)), device_id_type=MESH_ID)
    pl.semaphore_signal(barrier, inc=1, device_id=(sibling, feat), device_id_type=MESH_ID)

    grad, curv = lambdas[0:1, :], lambdas[1:2, :]
    leaf = leaves[...]
    leaf_row = lax.shift_right_logical(leaf, 7)
    leaf_lane = jnp.bitwise_and(leaf, 127)
    in_row = iota((8, OWN), 0) == leaf_row
    lane_hot = (iota((TILE, OWN), 0) == leaf_lane).astype(F32).astype(BF16)
    placed = []
    for value in (grad, curv):
        for piece in in_pieces(value, 3):
            placed.append(jnp.where(in_row, piece.astype(F32), 0.0).astype(BF16))
    leaf_sums = nt_dot(jnp.concatenate(placed, axis=0), lane_hot)
    leaf_got[chip, 0:8, :] = leaf_sums[0:8] + leaf_sums[8:16] + leaf_sums[16:24]
    leaf_got[chip, 8:16, :] = leaf_sums[24:32] + leaf_sums[32:40] + leaf_sums[40:48]
    chunk[...] = jnp.zeros_like(chunk)

    stats = in_pieces(grad, 2) + in_pieces(curv, 2) + [jnp.ones((1, OWN), BF16)]
    for which, value in enumerate(stats):
        weights[which] = jnp.broadcast_to(value, (16, OWN))

    low_levels = iota((LO, OWN), 0).astype(F32).astype(BF16)
    high_levels = jnp.bitwise_and(iota((16, OWN), 0), 7).astype(F32).astype(BF16)
    upper = iota((16, OWN), 0) < 8
    zero = jnp.zeros((), BF16)
    unit = jnp.ones((), BF16)

    def one_hots(group, slot):
        block = bins_t[pl.ds(pl.multiple_of(group * GROUP, GROUP), GROUP), :]
        high = jnp.floor(block * (1.0 / LO))
        low = block - high * LO
        for k in range(GROUP):
            spread_low = jnp.broadcast_to(low[k:k + 1].astype(BF16), (LO, OWN))
            right_side[slot, k * LO:(k + 1) * LO, :] = jnp.where(spread_low == low_levels, unit, zero)
        for pair in range(GROUP // 2):
            k = 2 * pair
            both = jnp.where(
                upper, jnp.broadcast_to(high[k:k + 1], (16, OWN)),
                jnp.broadcast_to(high[k + 1:k + 2], (16, OWN))).astype(BF16)
            hot = both == high_levels
            for which in range(5):
                left_side[slot, which * 64 + pair * 16:which * 64 + (pair + 1) * 16, :] = jnp.where(
                    hot, weights[which], zero)

    def sums(slot, target, index):
        full = nt_dot(left_side[slot], right_side[slot])
        lane = iota((HI, TILE), 1)
        for stat, whichs in enumerate(((0, 1), (2, 3), (4,))):
            for half in range(2):
                lanes = slice(half * TILE, (half + 1) * TILE)
                total = None
                for which in whichs:
                    picked = None
                    for j in range(4):
                        k = half * 4 + j
                        piece = full[which * 64 + k * HI:which * 64 + (k + 1) * HI, lanes]
                        picked = piece if j == 0 else jnp.where(lane >= j * LO, piece, picked)
                    total = picked if total is None else total + picked
                target[index, stat * HI:(stat + 1) * HI, lanes] = total

    def chip_at(turn):
        return chip_peer(lax.rem(turn + 1, CHIPS))

    def groups_of(turns):
        peers = [chip_at(turn) for turn in turns]
        for which, peer in enumerate(peers):
            one_hots(peer * 2 + other_core, 2 * which)
            one_hots(peer * 2 + core, 2 * which + 1)
        for which, peer in enumerate(peers):
            sums(2 * which, pair_sent, peer)
            sums(2 * which + 1, sent, peer)

    def pair_copy(turn):
        peer = chip_at(turn)
        return remote(pair_sent.at[peer], pair_got.at[peer], pair_send.at[peer], pair_recv.at[peer], (sibling, feat))

    def plane_copy(offset):
        peer = chip_peer(offset)
        return remote(sent.at[peer], got.at[chip], send_sem.at[peer], recv_sem.at[chip], (peer * 2 + core, feat))

    def plane_arrival(offset):
        peer = chip_source(offset)
        return remote(sent.at[peer], got.at[peer], send_sem.at[peer], recv_sem.at[peer], (peer * 2 + core, feat))

    def join(turn):
        pair_copy(turn).wait_recv()
        peer = chip_at(turn)
        sent[peer] = sent[peer] + pair_got[peer]

    def join_and_send(turn):
        join(turn)
        plane_copy(turn + 1).start()

    groups_of((0, 1))

    @pl.loop(1, EARLY // 2)
    def _(step):
        groups_of((2 * step, 2 * step + 1))

    pl.semaphore_wait(barrier, 1 + CHIPS - 1 + RING - 1)

    def leaf_copy(offset):
        peer = chip_peer(offset)
        return remote(leaf_got.at[chip], leaf_got.at[chip], leaf_send.at[peer], leaf_recv.at[chip], (peer * 2 + core, feat))

    def leaf_arrival(offset):
        peer = chip_source(offset)
        return remote(leaf_got.at[chip], leaf_got.at[peer], leaf_send.at[peer], leaf_recv.at[peer], (peer * 2 + core, feat))

    @pl.loop(1, CHIPS)
    def _(offset):
        leaf_copy(offset).start()

    @pl.loop(0, EARLY)
    def _(turn):
        pair_copy(turn).start()

    groups_of((EARLY, EARLY + 1))
    pair_copy(EARLY).start()
    pair_copy(EARLY + 1).start()

    @pl.loop(0, EARLY)
    def _(turn):
        join_and_send(turn)

    @pl.loop(EARLY // 2 + 1, CHIPS // 2 - 1)
    def _(step):
        groups_of((2 * step, 2 * step + 1))
        pair_copy(2 * step).start()
        pair_copy(2 * step + 1).start()
        join_and_send(2 * step - 2)
        join_and_send(2 * step - 1)

    groups_of((CHIPS - 2,))
    pair_copy(CHIPS - 2).start()
    join_and_send(CHIPS - 4)
    join_and_send(CHIPS - 3)
    groups_of((CHIPS - 1,))
    pair_copy(CHIPS - 1).start()
    @pl.loop(1, CHIPS)
    def _(offset):
        leaf_arrival(offset).wait_recv()

    leaf_ring[feat] = lax.fori_loop(
        0, CHIPS, lambda peer, total: total + leaf_got[peer], jnp.zeros((16, TILE), F32))

    def ring_copy(offset):
        peer = ring_peer(offset)
        return remote(leaf_ring.at[feat], leaf_ring.at[feat], ring_send.at[peer], ring_recv.at[feat], (query, peer))

    def ring_arrival(offset):
        peer = ring_peer(offset)
        return remote(leaf_ring.at[feat], leaf_ring.at[peer], ring_send.at[peer], ring_recv.at[peer], (query, peer))

    @pl.loop(1, RING)
    def _(offset):
        ring_copy(offset).start()

    join_and_send(CHIPS - 2)
    join(CHIPS - 1)

    def add_hist(offset, total):
        plane_arrival(offset).wait_recv()
        return total + got[chip_source(offset)]

    summed = lax.fori_loop(1, CHIPS, add_hist, sent[chip])

    lane_block = lax.shift_right_logical(iota((GROUP, TILE), 1), 5)
    holder = iota((GROUP, TILE), 0)
    for stat in range(3):
        for half in range(2):
            moved = jnp.zeros((GROUP, TILE), F32)
            for r in range(4):
                row = stat * HI + half * 4 + r
                line = jnp.where(
                    holder < 4, jnp.broadcast_to(summed[row:row + 1, 0:TILE], (GROUP, TILE)),
                    jnp.broadcast_to(summed[row:row + 1, TILE:2 * TILE], (GROUP, TILE)))
                for kk in range(4):
                    shift = (r - kk) % 4 * LO
                    turned = pltpu.roll(line, shift, 1) if shift else line
                    moved = jnp.where((jnp.bitwise_and(holder, 3) == kk) & (lane_block == r), turned, moved)
            line = stat * 2 + half
            for k in range(GROUP):
                chunk[k, line:line + 1, :] = moved[k:k + 1, :]

    def chunk_copy(offset):
        peer = ring_peer(offset)
        return remote(chunk.at[peer], chunk_got.at[feat], chunk_send.at[peer], chunk_recv.at[feat], (query, peer))

    def chunk_arrival(offset):
        peer = ring_peer(offset)
        return remote(chunk.at[peer], chunk_got.at[peer], chunk_send.at[peer], chunk_recv.at[peer], (query, peer))

    for offset in FAR_FIRST:
        chunk_copy(offset).start()

    @pl.loop(1, RING)
    def _(offset):
        ring_arrival(offset).wait_recv()

    core_total = leaf_ring[0]
    for peer in range(1, RING):
        core_total = core_total + leaf_ring[peer]
    leaf_both[core] = core_total
    leaf_back = remote(leaf_both.at[core], leaf_both.at[core], one_send.at[0], one_recv.at[0], (sibling, feat))
    leaf_back.start()

    leaf_back_here = remote(
        leaf_both.at[core], leaf_both.at[other_core], one_send.at[0], one_recv.at[0], (sibling, feat))
    leaf_back_here.wait_recv()
    totals = leaf_both[0] + leaf_both[1]
    total_grad, total_curv = totals[0:8], totals[8:16]
    shrunk = jnp.maximum(jnp.abs(total_grad) - lasso_penalty, 0.0) / (total_curv + ridge_penalty)
    values = jnp.where(total_grad > 0.0, -shrunk, shrunk)
    leaf_out[...] = values
    found = jnp.zeros((8, OWN), F32)
    for piece in in_pieces(values, 3):
        found = found + jnp.dot(piece, lane_hot, preferred_element_type=F32)
    step_out[...] = shrinkage * jnp.sum(jnp.where(in_row, found, 0.0), axis=0, keepdims=True)

    leaf_back.wait_send()
    pair_copy(CHIPS - 1).wait_send()

    @pl.loop(1, CHIPS)
    def _(offset):
        pair_copy(offset - 1).wait_send()
        plane_copy(offset).wait_send()
        leaf_copy(offset).wait_send()

    @pl.loop(1, RING)
    def _(offset):
        ring_copy(offset).wait_send()

    total = chunk[feat]
    for offset in reversed(FAR_FIRST):
        chunk_arrival(offset).wait_recv()
        total = total + chunk_got[ring_peer(offset)]
    hist_out[...] = total
    for offset in FAR_FIRST:
        chunk_copy(offset).wait_send()


def finish_kernel(leaf_in, step_in, hist_in, leaf_out, step_out, hist_out, hist, sem):
    for stat in range(3):
        for half in range(2):
            line = stat * 2 + half
            hist[stat:stat + 1, half * TILE:(half + 1) * TILE] = hist_in[line:line + 1, :]
    copies = [
        pltpu.make_async_copy(source, target, sem.at[which])
        for which, (source, target) in enumerate(((leaf_in, leaf_out), (step_in, step_out), (hist, hist_out)))]
    for copy in copies:
        copy.start()
    for copy in copies:
        copy.wait()


def local(scores, labels, leaves, bins, lengths, owner):
    shape = jax.ShapeDtypeStruct
    dma = pltpu.SemaphoreType.DMA
    column = pltpu.VMEM((WIN, TILE), F32)
    window, rows, table, bins_t, id_col, worth_col = pl.pallas_call(
        prepare_kernel,
        out_shape=(
            shape((1, WIN), F32),
            shape((8, WIN), F32),
            shape((8, TILE), jnp.int32),
            shape((FEATURES, OWN), F32),
            shape((WIN, TILE), F32),
            shape((WIN, TILE), F32),
        ),
        in_specs=[HBM] * 5,
        out_specs=(VMEM,) * 6,
        scratch_shapes=[
            pltpu.VMEM((1, BLOCK), jnp.int32), pltpu.VMEM((1, QUERIES), jnp.int32),
            pltpu.VMEM((1, FEATURES), jnp.int32), pltpu.VMEM((OWN, FEATURES), jnp.int32),
            pltpu.VMEM((1, OWN), F32), pltpu.VMEM((1, OWN), F32), pltpu.VMEM((1, OWN), F32),
            dma((5,)), dma((2,)), dma((2,))],
        compiler_params=pltpu.CompilerParams(
            collective_id=1, has_side_effects=True, vmem_limit_bytes=32 * 2**20),
        name="prepare",
    )(in_hbm(scores.reshape(1, OWN)), in_hbm(labels.reshape(1, BLOCK)), in_hbm(lengths), in_hbm(owner.reshape(1, FEATURES)), in_hbm(bins))
    lambdas, lambdas_again = pl.pallas_call(
        pair_kernel,
        out_shape=(shape((2, OWN), F32), shape((2, OWN), F32)),
        in_specs=[SMEM] + [VMEM] * 4,
        out_specs=(VMEM, VMEM),
        scratch_shapes=[pltpu.VMEM((8, WIN), F32)] + [column] * 3 + [pltpu.VMEM((8, WIN), F32)] * 2 + [pltpu.VMEM((8, OWN), F32)] * 2,
        compiler_params=pltpu.CompilerParams(vmem_limit_bytes=32 * 2**20),
        name="pairs",
    )(table, window, rows, id_col, worth_col)
    part = pltpu.VMEM((CHIPS, 3 * HI, GROUP * LO), F32)
    leaf_values, score_step, histograms = pl.pallas_call(
        histogram_kernel,
        out_shape=(
            shape((8, TILE), F32),
            shape((1, OWN), F32),
            shape((8, TILE), F32),
        ),
        in_specs=[VMEM] * 3,
        out_specs=(VMEM, VMEM, VMEM),
        scratch_shapes=[
            pltpu.VMEM((4, 5 * GROUP * HI, OWN), BF16),
            pltpu.VMEM((4, GROUP * LO, OWN), BF16),
            pltpu.VMEM((5, 16, OWN), BF16),
            part, part, part, part,
            pltpu.VMEM((CHIPS, 16, TILE), F32),
            pltpu.VMEM((RING, 16, TILE), F32),
            pltpu.VMEM((2, 16, TILE), F32),
            pltpu.VMEM((RING, 8, TILE), F32),
            pltpu.VMEM((RING, 8, TILE), F32),
            dma((CHIPS,)), dma((CHIPS,)), dma((CHIPS,)), dma((CHIPS,)), dma((CHIPS,)), dma((CHIPS,)),
            dma((RING,)), dma((RING,)), dma((RING,)), dma((RING,)), dma((1,)), dma((1,)),
        ],
        compiler_params=pltpu.CompilerParams(
            collective_id=2, has_side_effects=True, vmem_limit_bytes=32 * 2**20),
        name="histograms",
    )(lambdas_again, leaves.reshape(1, OWN), bins_t)
    leaf_values, score_step, histograms = pl.pallas_call(
        finish_kernel,
        out_shape=(
            shape((8, TILE), F32),
            shape((1, OWN), F32),
            shape((3, BINS), F32),
        ),
        in_specs=[VMEM] * 3,
        out_specs=(HBM, HBM, HBM),
        scratch_shapes=[pltpu.VMEM((3, BINS), F32), dma((3,))],
        compiler_params=pltpu.CompilerParams(vmem_limit_bytes=2**21),
        name="finish",
    )(leaf_values, score_step, histograms)
    return lambdas, leaf_values.reshape(LEAVES), score_step.reshape(OWN), histograms


def solution(mesh):
    in_specs = (
        P(("query", "feat")),
        P("query"),
        P(("query", "feat")),
        P(("query", "feat"), None),
        P("query", None),
        P(),
    )
    out_specs = (P(None, ("query", "feat")), P(), P(("query", "feat")), P(None, ("query", "feat")))
    return jax.shard_map(local, mesh=mesh, in_specs=in_specs, out_specs=out_specs, check_vma=False)
```
